256 devices in a mesh: dp: 64 (over x, y_hi, z), ctx: 4 (over y_lo, core).
Axes of the slice: x: 4, y: 4 (y_hi: 2, y_lo: 2; y = y_hi * 2 + y_lo), z: 8, core: 2. Of those that a mesh axis runs over, the one named last changes fastest.
Arguments:
- frames: bfloat16 [64, 1024, 1536], P('dp', 'ctx'), may hold values from -6 to 6
- destinations: int32 [64, 1024], P('dp', 'ctx'), may hold values from 0 to 16383, as said below
- segments: int32 [64, 1024], P('dp'), may hold values from 0 to 2, as said below
- tile_mask: int32 [64, 8, 8], P('dp', 'ctx'), may hold values from 0 to 1, as said below
- attn_gain: float32 [1536], replicated, may hold values from 0.1 to 1.9
- w_qkv: bfloat16 [1536, 2304], replicated
- w_out: bfloat16 [768, 1536], replicated, may hold values from -5 to 5
- conv_gain: float32 [1536], replicated, may hold values from 0.1 to 1.9
- w_pointin: bfloat16 [1536, 1536], P(('dp', 'ctx')), may hold values from -0.625 to 0.625
- w_pointout: bfloat16 [768, 1536], P(None, ('dp', 'ctx')), may hold values from -0.43164062 to 0.43164062
- w_depth: float32 [32, 768], replicated, may hold values from -1 to 1
- bn_scale: float32 [768], replicated, may hold values from 0.1 to 1.9
- bn_shift: float32 [768], replicated, may hold values from -3 to 3
Outputs:
- layer_out: bfloat16 [64, 1024, 1536], P('dp', 'ctx')
The draws below stay inside these ranges and needn't reach their ends.
Inputs may be any that keep to these rules, and one draw needn't show every extreme that they name: `destinations`: per ctx index c, the values at positions c * 256 to (c + 1) * 256 - 1 over all rows of the first dimension are all different, so every target row is filled once. The rows of one device send at most 8 frames to one sequence, and exactly 8 to some sequences. `segments`: along a sequence the ids never fall, start at 0 and end at 2. tile_mask[b, t, t] = 1; tile_mask[b, t, u] = 0 where tiles t and u of sequence b share no segment id.
All inputs are finite; a program needn't handle non-finite values.
Results may differ from the reference program's by a relative error of at most 0.01.
Values may be sent and summed in bfloat16 or wider, within the bound.
A program may use at most 128 MiB of HBM per device.

```python
import math
import jax
import jax.numpy as jnp
from jax import lax

D = 1536
HEADS = 8
HEAD = 96
CC = 768
KERNEL = 32
TILE = 128
ROWS_DEV = 256
SEQ = 1024
TILES = 8
HALF = 16
N_DP = 64
N_CTX = 4


def packed_segments(key):
    base = jax.random.fold_in(key, 23)
    first_key, second_key = jax.random.split(base)
    first_cut = jax.random.randint(first_key, (N_DP, 1), 1, SEQ // 2)
    second_cut = jax.random.randint(second_key, (N_DP, 1), SEQ // 2 + 1, SEQ)
    positions = jnp.arange(SEQ, dtype=jnp.int32)[None, :]
    return (positions >= first_cut).astype(jnp.int32) + (positions >= second_cut).astype(jnp.int32)


def draw_segments(key, part):
    return packed_segments(key)


def draw_tile_mask(key, part):
    seg_ids = packed_segments(key)
    tiled = seg_ids.reshape(N_DP, TILES, TILE)
    first_id = tiled[:, :, 0]
    last_id = tiled[:, :, TILE - 1]
    meets = (last_id[:, :, None] >= first_id[:, None, :]) & (last_id[:, None, :] >= first_id[:, :, None])
    keep = jax.random.randint(jax.random.fold_in(key, 29), (N_DP, TILES, TILES), 0, 4) > 0
    diagonal = jnp.eye(TILES, dtype=jnp.bool_)[None]
    return (meets & (keep | diagonal)).astype(jnp.int32)


def draw_destinations(key, part):
    unit = ROWS_DEV // N_DP
    pattern = jnp.array([2, 1, 1, 0], jnp.int32)
    loaders = jnp.arange(N_DP, dtype=jnp.int32)
    row_iota = jnp.arange(ROWS_DEV, dtype=jnp.int32)

    def one_column(col_key):
        perm_key, shift_key, row_key, slot_key = jax.random.split(col_key, 4)
        owner_perm = jax.random.permutation(perm_key, N_DP).astype(jnp.int32)
        shift_rank = jax.random.permutation(shift_key, N_DP).astype(jnp.int32)
        weights = pattern[shift_rank % 4] * unit
        bounds = jnp.cumsum(weights)
        shift_of_row = jnp.sum((bounds[None, :] <= row_iota[:, None]).astype(jnp.int32), axis=1)
        owners = owner_perm[(loaders[:, None] + shift_of_row[None, :]) % N_DP]
        row_keys = jax.random.split(row_key, N_DP)
        owners = jax.vmap(lambda one_key, row_owners: jax.random.permutation(one_key, row_owners))(row_keys, owners)
        flat_owner = owners.reshape(-1)
        onehot = (flat_owner[:, None] == loaders[None, :]).astype(jnp.int32)
        rank_in = jnp.sum((jnp.cumsum(onehot, axis=0) - onehot) * onehot, axis=1)
        slot_perms = jax.vmap(lambda one_key: jax.random.permutation(one_key, ROWS_DEV).astype(jnp.int32))(jax.random.split(slot_key, N_DP))
        slot_index = slot_perms[flat_owner, rank_in]
        return (flat_owner * ROWS_DEV + slot_index).reshape(N_DP, ROWS_DEV)
    columns = jax.vmap(one_column)(jax.random.split(jax.random.fold_in(key, 11), N_CTX))
    return jnp.transpose(columns, (1, 0, 2)).reshape(N_DP, N_CTX * ROWS_DEV).astype(jnp.int32)


def draw_w_qkv(key, part):
    query_key, key_key, value_key = jax.random.split(jax.random.fold_in(key, 37), 3)
    width = HEADS * HEAD
    base_scale = 1.2 / math.sqrt(D)
    w_query = jax.random.normal(query_key, (D, width), jnp.float32) * base_scale
    w_key = jax.random.normal(key_key, (D, width), jnp.float32) * base_scale
    w_value = jax.random.normal(value_key, (D, width), jnp.float32) * (1.0 / math.sqrt(D))
    return jnp.concatenate([w_query, w_key, w_value], axis=1).astype(jnp.bfloat16)


def strengthened(values, stream_key, source, target, parts, factor):
    def block_of(position):
        return (jnp.arange(values.shape[position]) // (values.shape[position] // parts)).reshape((-1,) + (1,) * (values.ndim - 1 - position))

    near = jax.random.permutation(stream_key, parts)[block_of(target)]
    second = (block_of(target) + parts // 2) % parts
    return jnp.where((block_of(source) == near) | (block_of(source) == second), factor * values, values)


def steps_of(stream_key, extent, cuts, low, high):
    level = 1.0
    for position, blocks in cuts:
        steps = jax.random.uniform(jax.random.fold_in(jax.random.fold_in(stream_key, 6), position), (blocks,), jnp.float32, low / len(cuts), high / len(cuts))
        level = level * jnp.repeat(jnp.exp(steps), extent[position] // blocks).reshape((-1,) + (1,) * (len(extent) - 1 - position))
    return level


def noise(rng, dims, scale, reach, cuts=(), kind=jnp.bfloat16):
    entries = jax.random.normal(rng, dims, jnp.float32) * scale
    if len(cuts) > 0:
        entries = steps_of(rng, dims, cuts, -0.22, 0.18) * entries
    return jnp.clip(entries, min=-reach, max=reach).astype(kind)


def heavy_noise(stream_key, extent, deviation, most, pieces, heavy, kind=jnp.bfloat16):
    drawn = deviation * jax.random.normal(stream_key, extent, jnp.float32)
    if pieces:
        drawn = drawn * steps_of(stream_key, extent, pieces, -0.22, 0.18)
    return jnp.clip(strengthened(drawn, jax.random.fold_in(stream_key, 3), *heavy), -most, most).astype(kind)


def setup_inputs(seed: int = 0) -> dict:
    arg_keys = jax.random.split(jax.random.key(seed), 14)
    frames = noise(arg_keys[0], (N_DP, SEQ, D), 1.0, 6.0, ((0, 64), (1, 4)))
    destinations = draw_destinations(jax.random.fold_in(arg_keys[13], 71), 0)
    segments = draw_segments(jax.random.fold_in(arg_keys[13], 71), 0)
    tile_mask = draw_tile_mask(jax.random.fold_in(arg_keys[13], 71), 0)
    attn_gain = jnp.clip(1.0 + 0.18 * jax.random.normal(arg_keys[4], (D,), jnp.float32), 0.1, 1.9)
    w_qkv = draw_w_qkv(jax.random.fold_in(arg_keys[13], 71), 0)
    w_out = noise(arg_keys[6], (HEADS * HEAD, D), 0.35, 5.0)
    conv_gain = jnp.clip(1.0 + 0.18 * jax.random.normal(arg_keys[7], (D,), jnp.float32), 0.1, 1.9)
    w_pointin = heavy_noise(arg_keys[8], (D, 2 * CC), D ** -0.5, 0.625, ((0, 256),), (0, 1, 256, 6.0))
    w_pointout = noise(arg_keys[9], (CC, D), (2.0 / CC ** 0.5), 0.43164062, ((1, 256),))
    w_depth = noise(arg_keys[10], (KERNEL, CC), KERNEL ** -0.5, 1.0, (), jnp.float32)
    bn_scale = jnp.clip(1.0 + 0.18 * jax.random.normal(arg_keys[11], (CC,), jnp.float32), 0.1, 1.9)
    bn_shift = noise(arg_keys[12], (CC,), 0.5, 3.0, (), jnp.float32)
    return {"frames": frames, "destinations": destinations, "segments": segments, "tile_mask": tile_mask, "attn_gain": attn_gain, "w_qkv": w_qkv, "w_out": w_out, "conv_gain": conv_gain, "w_pointin": w_pointin, "w_pointout": w_pointout, "w_depth": w_depth, "bn_scale": bn_scale, "bn_shift": bn_shift}


def layer_norm(values, gain):
    as_float = values.astype(jnp.float32)
    row_mean = lax.optimization_barrier(jnp.mean(as_float, axis=-1, keepdims=True))
    centred = as_float - row_mean
    row_var = lax.optimization_barrier(jnp.mean(centred * centred, axis=-1, keepdims=True))
    return centred * lax.rsqrt(row_var + 1e-06) * gain

def reference(frames, destinations, segments, tile_mask, attn_gain, w_qkv, w_out, conv_gain, w_pointin, w_pointout, w_depth, bn_scale, bn_shift):
    owner_index = destinations // ROWS_DEV
    slot_index = destinations % ROWS_DEV
    column = (jnp.arange(SEQ, dtype=jnp.int32) // ROWS_DEV)[None, :]
    target_row = column * ROWS_DEV + slot_index
    placed = jnp.zeros((N_DP, SEQ, D), jnp.bfloat16).at[owner_index, target_row].set(frames)
    head_cols = HEADS * HEAD
    qblock = min(512, SEQ)
    scale_factor = 1.0 / HEAD ** 0.5

    def seq_layer(packed):
        seq_frames, seg_ids, mask_table = packed
        normed = layer_norm(seq_frames, attn_gain).astype(jnp.bfloat16)
        qkv_rows = jnp.dot(normed, w_qkv, preferred_element_type=jnp.float32).astype(jnp.bfloat16)
        queries = qkv_rows[:, :head_cols].reshape(SEQ, HEADS, HEAD)
        keys_all = qkv_rows[:, head_cols:2 * head_cols].reshape(SEQ, HEADS, HEAD).astype(jnp.float32)
        values_all = qkv_rows[:, 2 * head_cols:].reshape(SEQ, HEADS, HEAD).astype(jnp.float32)

        def attend(block_index):
            begin = block_index * qblock
            query_block = lax.dynamic_slice_in_dim(queries, begin, qblock, 0).astype(jnp.float32)
            seg_block = lax.dynamic_slice_in_dim(seg_ids, begin, qblock, 0)
            mask_rows = lax.dynamic_slice_in_dim(mask_table, begin // TILE, qblock // TILE, 0)
            wide_mask = jnp.repeat(jnp.repeat(mask_rows, TILE, axis=0), TILE, axis=1)
            allowed = (seg_block[:, None] == seg_ids[None, :]) & (wide_mask == 1)
            scores = jnp.einsum('qhd,khd->hqk', query_block, keys_all) * scale_factor
            scores = jnp.where(allowed[None], scores, -1e+30)
            row_max = lax.optimization_barrier(jnp.max(scores, axis=-1, keepdims=True))
            weights = jnp.where(allowed[None], jnp.exp(scores - row_max), 0.0)
            total = lax.optimization_barrier(jnp.sum(weights, axis=-1))
            weights_b = weights.astype(jnp.bfloat16).astype(jnp.float32)
            summed = jnp.einsum('hqk,khd->qhd', weights_b, values_all)
            result = summed / jnp.transpose(total)[:, :, None]
            return result.astype(jnp.bfloat16).reshape(qblock, head_cols)
        attended = lax.map(attend, jnp.arange(SEQ // qblock, dtype=jnp.int32)).reshape(SEQ, head_cols)
        branch = jnp.dot(attended, w_out, preferred_element_type=jnp.float32)
        after_attn = (seq_frames.astype(jnp.float32) + branch).astype(jnp.bfloat16)
        conv_normed = layer_norm(after_attn, conv_gain).astype(jnp.bfloat16)
        projected = jnp.dot(conv_normed, w_pointin, preferred_element_type=jnp.float32)
        gated = (projected[:, :CC] * jax.nn.sigmoid(projected[:, CC:])).astype(jnp.bfloat16)
        gated_pad = jnp.pad(gated.astype(jnp.float32), ((HALF, HALF), (0, 0)))
        seg_pad = jnp.pad(seg_ids, (HALF, HALF), constant_values=-1)
        depthwise = jnp.zeros((SEQ, CC), jnp.float32)
        for tap_index in range(KERNEL):
            same_seg = (seg_pad[tap_index:tap_index + SEQ] == seg_ids).astype(jnp.float32)
            depthwise = depthwise + w_depth[tap_index][None, :] * gated_pad[tap_index:tap_index + SEQ] * same_seg[:, None]
        shifted = depthwise * bn_scale + bn_shift
        activated = (shifted * jax.nn.sigmoid(shifted)).astype(jnp.bfloat16)
        closing = jnp.dot(activated, w_pointout, preferred_element_type=jnp.float32)
        return (after_attn.astype(jnp.float32) + closing).astype(jnp.bfloat16)
    return lax.map(seq_layer, (placed, segments, tile_mask))
```

```python
import math

import numpy as np

import jax
import jax.numpy as jnp
from jax import lax
from jax.experimental import pallas as pl
from jax.experimental.pallas import tpu as pltpu
from jax.sharding import PartitionSpec as P

HEADS = 8
NX = 4
NY = 2
MESH = pl.DeviceIdType.MESH
BF = jnp.bfloat16
F32 = jnp.float32
MASKED = -2e38


def dot(a, b):
    return jnp.dot(a, b, preferred_element_type=F32)


def dot_nt(a, b):
    return lax.dot_general(a, b, (((1,), (1,)), ((), ())), preferred_element_type=F32)


def layer_norm(as_float, gain):
    row_mean = jnp.mean(as_float, axis=-1, keepdims=True)
    centred = as_float - row_mean
    row_var = jnp.mean(centred * centred, axis=-1, keepdims=True)
    return centred * lax.rsqrt(row_var + 1e-06) * gain


def layer_kernel(
    n_dp,
    shard_rows,
    dest_ref,
    frames_ref,
    seg_ref,
    tile_ref,
    again_ref,
    wqkv_hbm,
    wout_hbm,
    cgain_ref,
    shard_ref,
    pick_ref,
    wdepth_ref,
    bns_ref,
    bnb_ref,
    out_ref,
    wqkv_ref,
    wout_ref,
    send_ref,
    got_ref,
    zbuf_ref,
    cbuf_ref,
    wfull_ref,
    kv_ref,
    q_ref,
    att_ref,
    placed_ref,
    after_ref,
    bias_ref,
    segc_ref,
    segn_ref,
    mask_ref,
    gat_ref,
    htop_ref,
    hbot_ref,
    gf_ref,
    act_ref,
    load_sem,
    a_send,
    a_recv,
    bz_send,
    bz_recv,
    bc_send,
    bc_recv,
    by_send,
    by_recv,
    bx_send,
    bx_recv,
    sib_send,
    sib_recv,
    kv_send,
    kv_recv,
    halo_send,
    halo_recv,
):
    rows, width = frames_ref.shape
    seq = seg_ref.shape[1]
    nz = n_dp // (NX * NY)
    cap = send_ref.shape[1]
    head_cols = wout_ref.shape[0]
    head = head_cols // HEADS
    group = head_cols // 2
    half_cols = cbuf_ref.shape[3]
    block = NY * 0 + wfull_ref.shape[1] // (NX * NY)
    channels = wdepth_ref.shape[1]
    taps = wdepth_ref.shape[0]
    half = taps // 2
    tile = 128

    dp = lax.axis_index("dp")
    ctx = lax.axis_index("ctx")
    x = dp // (NY * nz)
    yh = (dp // nz) % NY
    z = dp % nz
    core = ctx % 2

    def dp_of(px, py, pz):
        return (px * NY + py) * nz + pz

    def peer(k):
        kx, ky, kz = k // (NY * nz), (k // nz) % NY, k % nz
        return dp_of((x + kx) % NX, (yh + ky) % NY, (z + kz) % nz)

    def put(src, dst, ssem, rsem, d, c):
        copy = pltpu.make_async_remote_copy(
            src_ref=src, dst_ref=dst, send_sem=ssem, recv_sem=rsem, device_id=(d, c), device_id_type=MESH
        )
        copy.start()

    def settle(ref, sem):
        pltpu.make_async_copy(ref, ref, sem).wait()

    barrier = pltpu.get_barrier_semaphore()

    def greet(k, carry):
        pl.semaphore_signal(barrier, inc=1, device_id=(peer(k), ctx), device_id_type=MESH)
        return carry

    lax.fori_loop(1, n_dp, greet, 0)
    for d in range(1, 4):
        pl.semaphore_signal(barrier, inc=1, device_id=(dp, ctx ^ d), device_id_type=MESH)

    load_qkv = pltpu.make_async_copy(wqkv_hbm, wqkv_ref, load_sem.at[0])
    load_qkv.start()
    load_out = pltpu.make_async_copy(wout_hbm, wout_ref, load_sem.at[1])
    load_out.start()

    dest = dest_ref[...]
    owner = dest // rows
    slot = dest % rows
    oz = owner % nz
    oy = (owner // nz) % NY
    ox = owner // (nz * NY)
    rel = (((ox - x + NX) % NX) * NY + (oy - yh + NY) % NY) * nz + (oz - z + nz) % nz
    rel_wide = jnp.broadcast_to(rel.astype(F32), (rows, rows))
    rel_tall = jnp.transpose(rel_wide)
    earlier = lax.broadcasted_iota(jnp.int32, (rows, rows), 0) < lax.broadcasted_iota(jnp.int32, (rows, rows), 1)
    rank = jnp.sum(jnp.where((rel_tall == rel_wide) & earlier, 1.0, 0.0), axis=0, keepdims=True)
    pos = rel * cap + rank.astype(jnp.int32)
    slot_tall = jnp.transpose(jnp.broadcast_to(slot.astype(F32) + 1.0, (tile, rows))).astype(BF)
    frames = frames_ref[...]
    zbuf_ref[pl.ds(z, 1)] = shard_ref[...]

    parts = 4
    per = n_dp // parts
    for c in range(parts):
        chunk = lax.broadcasted_iota(jnp.int32, (per * cap, rows), 0) + c * per * cap
        onehot = jnp.where(chunk == pos, 1.0, 0.0).astype(BF)
        send_ref[c * per : (c + 1) * per, :, :width] = dot(onehot, frames).reshape(per, cap, width).astype(BF)
        send_ref[c * per : (c + 1) * per, :, width:] = dot(onehot, slot_tall).reshape(per, cap, tile).astype(BF)
        if c == 0:
            pl.semaphore_wait(barrier, n_dp - 1 + 3)
            for k in range(1, nz):
                put(
                    zbuf_ref.at[z], zbuf_ref.at[z], bz_send.at[k], bz_recv.at[k], dp_of(x, yh, (z + k) % nz), ctx
                )
            got_ref[0:1] = send_ref[0:1]

        def ship(k, carry):
            put(send_ref.at[k], got_ref.at[k], a_send, a_recv, peer(k), ctx)
            return carry

        lax.fori_loop(max(1, c * per), (c + 1) * per, ship, 0)

    segf = seg_ref[...].astype(F32)
    segc_ref[0:half] = jnp.full((half, tile), -1.0, F32)
    segc_ref[half + seq :] = jnp.full((half, tile), -1.0, F32)
    segc_ref[half : half + seq] = jnp.transpose(jnp.broadcast_to(segf, (tile, seq)))
    first = pl.multiple_of(ctx * rows, rows)
    segn_ref[...] = segc_ref[pl.ds(first, rows + 2 * half)]
    own_seg = segn_ref[half : half + rows]
    for tk in range(seq // tile):
        same = own_seg == segf[:, tk * tile : (tk + 1) * tile]
        for tq in range(rows // tile):
            off = (1 - tile_ref[tq, tk]).astype(F32) * MASKED
            bias_ref[tq * tile : (tq + 1) * tile, tk * tile : (tk + 1) * tile] = jnp.where(
                same[tq * tile : (tq + 1) * tile], off, MASKED
            )
    for k in range(taps):
        mask_ref[k] = jnp.where(segn_ref[k : k + rows] == own_seg, 1.0, 0.0)

    for k in range(1, nz):
        settle(zbuf_ref.at[0], bz_recv.at[k])
    for d in range(1, 4):
        cols = pl.ds(pl.multiple_of(((ctx ^ d) % 2) * half_cols, 128), half_cols)
        put(zbuf_ref.at[:, :, cols], cbuf_ref.at[ctx], bc_send.at[d], bc_recv.at[d], dp, ctx ^ d)
    mine = pl.ds(pl.multiple_of(core * half_cols, 128), half_cols)
    cbuf_ref[pl.ds(ctx, 1)] = zbuf_ref[:, :, mine][None]
    for d in range(1, 4):
        settle(cbuf_ref.at[0], bc_recv.at[d])
    padded = cbuf_ref[...].astype(F32).reshape(pick_ref.shape[1], half_cols).astype(BF)

    def piece(px, py):
        start = pl.multiple_of((((px + NX) % NX) * NY + py) * block, 16)
        return wfull_ref.at[core, pl.ds(start, block)]

    own_start = pl.multiple_of((x * NY + yh) * block, 16)
    wfull_ref[core, pl.ds(own_start, block)] = dot(pick_ref[...], padded).astype(BF)
    right = dp_of((x + 1) % NX, yh, z)
    left = dp_of((x + NX - 1) % NX, yh, z)
    other = 1 - yh

    def to_sibling(i, ref):
        put(ref, ref, sib_send.at[i], sib_recv.at[i], dp, ctx ^ 1)

    put(piece(x, yh), piece(x, yh), by_send, by_recv, dp_of(x, other, z), ctx)
    put(piece(x, yh), piece(x, yh), bx_send.at[0], bx_recv.at[0], right, ctx)
    put(piece(x, yh), piece(x, yh), bx_send.at[1], bx_recv.at[1], left, ctx)
    to_sibling(0, piece(x, yh))

    settle(got_ref.at[pl.ds(1, n_dp - 1)], a_recv)
    got = got_ref[...].astype(F32).reshape(n_dp * cap, width + tile)
    slots = jnp.transpose(got[:, width:])[0:1]
    lane = lax.broadcasted_iota(jnp.int32, (rows, n_dp * cap), 0).astype(F32) + 1.0
    place = jnp.where(lane == slots, 1.0, 0.0).astype(BF)
    placed = dot(place, got[:, :width].astype(BF))
    placed_ref[...] = placed
    normed = layer_norm(placed, again_ref[...]).astype(BF)

    load_qkv.wait()
    base = pl.multiple_of(ctx * rows, rows)
    keys = dot(normed, wqkv_ref[:, head_cols : 2 * head_cols]).astype(BF)
    values = dot(normed, wqkv_ref[:, 2 * head_cols :]).astype(BF)
    for g in range(2):
        kv_ref[pl.ds(base, rows), 2 * g * group : (2 * g + 1) * group] = keys[:, g * group : (g + 1) * group]
        kv_ref[pl.ds(base, rows), (2 * g + 1) * group : (2 * g + 2) * group] = values[:, g * group : (g + 1) * group]

    def kv_part(c, g):
        return kv_ref.at[pl.ds(pl.multiple_of(c * rows, rows), rows), pl.ds(2 * g * group, 2 * group)]

    for g in range(2):
        part = kv_part(ctx, g)
        put(part, part, kv_send.at[g, 0], kv_recv.at[g, 0], dp, ctx ^ 2)
        put(part, part, kv_send.at[g, 1], kv_recv.at[g, 1], dp, ctx ^ 1)
    scale = math.log2(math.e) / math.sqrt(head)
    q_ref[...] = (dot(normed, wqkv_ref[:, :head_cols]) * scale).astype(BF)

    settle(piece(x, other), by_recv)
    put(piece(x, other), piece(x, other), bx_send.at[2], bx_recv.at[2], right, ctx)
    put(piece(x, other), piece(x, other), bx_send.at[3], bx_recv.at[3], left, ctx)
    to_sibling(1, piece(x, other))

    def attend(g):
        settle(kv_part(ctx ^ 2, g), kv_recv.at[g, 0])
        part = kv_part(ctx ^ 2, g)
        put(part, part, kv_send.at[g, 2], kv_recv.at[g, 2], dp, ctx ^ 1)
        settle(part, kv_recv.at[g, 1])
        settle(part, kv_recv.at[g, 2])
        tiles = [None] * (group // tile)
        for h in range(HEADS // 2):
            lo, hi = h * head, (h + 1) * head
            t0, t1 = lo // tile, (hi + tile - 1) // tile
            c0, c1 = t0 * tile, t1 * tile
            lanes = lax.broadcasted_iota(jnp.int32, (rows, c1 - c0), 1) + c0
            inside = (lanes >= lo) & (lanes < hi)
            query = q_ref[:, g * group + c0 : g * group + c1].astype(F32)
            query = jnp.where(inside, query, 0.0).astype(BF)
            scores = dot_nt(query, kv_ref[:, 2 * g * group + c0 : 2 * g * group + c1]) + bias_ref[...]
            top = jnp.max(scores, axis=1, keepdims=True)
            weights = jnp.exp2(scores - top)
            total = jnp.sum(weights, axis=1, keepdims=True)
            mixed = dot(weights.astype(BF), kv_ref[:, (2 * g + 1) * group + c0 : (2 * g + 1) * group + c1])
            mixed = jnp.where(inside, mixed / total, 0.0)
            for t in range(t0, t1):
                term = mixed[:, (t - t0) * tile : (t - t0 + 1) * tile]
                tiles[t] = term if tiles[t] is None else tiles[t] + term
        for t, whole in enumerate(tiles):
            att_ref[:, g * group + t * tile : g * group + (t + 1) * tile] = whole.astype(BF)

    attend(0)
    settle(piece(x - 1, yh), bx_recv.at[0])
    settle(piece(x + 1, yh), bx_recv.at[1])
    put(piece(x - 1, yh), piece(x - 1, yh), bx_send.at[4], bx_recv.at[4], right, ctx)
    to_sibling(2, piece(x - 1, yh))
    to_sibling(3, piece(x + 1, yh))
    attend(1)
    settle(piece(x - 1, other), bx_recv.at[2])
    settle(piece(x + 1, other), bx_recv.at[3])
    put(piece(x + 1, other), piece(x + 1, other), bx_send.at[5], bx_recv.at[5], left, ctx)
    to_sibling(4, piece(x - 1, other))
    to_sibling(5, piece(x + 1, other))

    load_out.wait()
    after = (placed_ref[...] + dot(att_ref[...], wout_ref[...])).astype(BF)
    after_ref[...] = after
    conv_normed = layer_norm(after.astype(F32), cgain_ref[...]).astype(BF)

    settle(piece(x + 2, yh), bx_recv.at[4])
    to_sibling(6, piece(x + 2, yh))
    settle(piece(x + 2, other), bx_recv.at[5])
    to_sibling(7, piece(x + 2, other))
    for i in range(NX * NY):
        settle(piece(x, yh), sib_recv.at[i])

    gate = jax.nn.sigmoid(dot(conv_normed, wfull_ref[1, :, :channels]))
    gated = (dot(conv_normed, wfull_ref[0, :, :channels]) * gate).astype(BF)
    gat_ref[...] = gated
    gf_ref[half : half + rows] = gated.astype(F32)

    head_rows = gat_ref.at[0:half]
    tail_rows = gat_ref.at[rows - half : rows]

    @pl.when(ctx > 0)
    def _():
        put(head_rows, hbot_ref, halo_send.at[0], halo_recv.at[0], dp, ctx - 1)

    @pl.when(ctx < 3)
    def _():
        put(tail_rows, htop_ref, halo_send.at[1], halo_recv.at[1], dp, ctx + 1)

    @pl.when(ctx == 0)
    def _():
        htop_ref[...] = jnp.zeros_like(htop_ref)

    @pl.when(ctx == 3)
    def _():
        hbot_ref[...] = jnp.zeros_like(hbot_ref)

    span = 64

    def convolve(r0):
        def body(t, carry):
            lanes = pl.ds(pl.multiple_of(t * tile, tile), tile)
            near = gf_ref[r0 : r0 + span + 2 * half, lanes]
            total = jnp.zeros((span, tile), F32)
            for b in range(8):
                shifted = near if b == 0 else pltpu.roll(near, span + 2 * half - b, 0)
                for a in range(taps // 8):
                    k = 8 * a + b
                    term = shifted[8 * a : 8 * a + span] * mask_ref[k, r0 : r0 + span]
                    total = total + term * wdepth_ref[k : k + 1, lanes]
            moved = total * bns_ref[:, lanes] + bnb_ref[:, lanes]
            act_ref[r0 : r0 + span, lanes] = (moved * jax.nn.sigmoid(moved)).astype(BF)
            return carry

        lax.fori_loop(0, channels // tile, body, 0)

    for r0 in range(span, rows - span, span):
        convolve(r0)

    @pl.when(ctx > 0)
    def _():
        settle(htop_ref, halo_recv.at[1])

    @pl.when(ctx < 3)
    def _():
        settle(hbot_ref, halo_recv.at[0])

    gf_ref[0:half] = htop_ref[...].astype(F32)
    gf_ref[half + rows :] = hbot_ref[...].astype(F32)
    convolve(0)
    convolve(rows - span)

    quarter = channels // 2
    closing = dot_nt(act_ref[:, :quarter], wfull_ref[0, :, channels:])
    closing = closing + dot_nt(act_ref[:, quarter:], wfull_ref[1, :, channels:])
    out_ref[...] = (after_ref[...].astype(F32) + closing).astype(BF)

    settle(send_ref.at[pl.ds(1, n_dp - 1)], a_send)
    for k in range(1, nz):
        settle(zbuf_ref.at[0], bz_send.at[k])
    for d in range(1, 4):
        settle(cbuf_ref.at[0], bc_send.at[d])
    settle(piece(x, yh), by_send)
    for i in range(6):
        settle(piece(x, yh), bx_send.at[i])
    for i in range(NX * NY):
        settle(piece(x, yh), sib_send.at[i])
    for g in range(2):
        for i in range(3):
            settle(kv_part(ctx, g), kv_send.at[g, i])

    @pl.when(ctx > 0)
    def _():
        settle(head_rows, halo_send.at[0])

    @pl.when(ctx < 3)
    def _():
        settle(tail_rows, halo_send.at[1])


def solution(mesh):
    n_dp = mesh.shape["dp"]
    n_ctx = mesh.shape["ctx"]
    nz = n_dp // (NX * NY)

    def per_device(
        frames,
        destinations,
        segments,
        tile_mask,
        attn_gain,
        w_qkv,
        w_out,
        conv_gain,
        w_pointin,
        w_pointout,
        w_depth,
        bn_scale,
        bn_shift,
    ):
        rows, width = frames.shape[1:]
        seq = segments.shape[1]
        channels = w_depth.shape[1]
        taps = w_depth.shape[0]
        head_cols = w_out.shape[0]
        cap = 2 * rows // n_dp
        shard_rows = w_pointin.shape[0]
        pad_rows = -(-shard_rows // 8) * 8
        half_cols = channels + channels // 2
        flipped = w_pointout.T
        shard = jnp.concatenate(
            [
                w_pointin[:, :channels],
                flipped[:, : channels // 2],
                w_pointin[:, channels:],
                flipped[:, channels // 2 :],
            ],
            axis=1,
        )
        shard = jnp.pad(shard, ((0, pad_rows - shard_rows), (0, 0)))[None]
        pick = np.zeros((nz * n_ctx * shard_rows, n_ctx * nz * pad_rows), np.float32)
        for a in range(nz):
            for b in range(n_ctx):
                for j in range(shard_rows):
                    pick[(a * n_ctx + b) * shard_rows + j, (b * nz + a) * pad_rows + j] = 1.0
        pick = jnp.asarray(pick, BF)
        vmem = pl.BlockSpec(memory_space=pltpu.VMEM)
        smem = pl.BlockSpec(memory_space=pltpu.SMEM)
        hbm = pl.BlockSpec(memory_space=pl.ANY)

        def body(*refs):
            layer_kernel(n_dp, shard_rows, *refs)

        dma = pltpu.SemaphoreType.DMA
        out = pl.pallas_call(
            body,
            name="conformer_layer",
            out_shape=jax.ShapeDtypeStruct((rows, width), BF),
            in_specs=[vmem, vmem, vmem, smem, vmem, hbm, hbm] + [vmem] * 6,
            out_specs=vmem,
            scratch_shapes=[
                pltpu.VMEM(w_qkv.shape, BF),
                pltpu.VMEM(w_out.shape, BF),
                pltpu.VMEM((n_dp, cap, width + 128), BF),
                pltpu.VMEM((n_dp, cap, width + 128), BF),
                pltpu.VMEM((nz, pad_rows, 2 * half_cols), BF),
                pltpu.VMEM((n_ctx, nz, pad_rows, half_cols), BF),
                pltpu.VMEM((2, width, half_cols), BF),
                pltpu.VMEM((seq, 2 * head_cols), BF),
                pltpu.VMEM((rows, head_cols), BF),
                pltpu.VMEM((rows, head_cols), BF),
                pltpu.VMEM((rows, width), F32),
                pltpu.VMEM((rows, width), BF),
                pltpu.VMEM((rows, seq), F32),
                pltpu.VMEM((seq + taps, 128), F32),
                pltpu.VMEM((rows + taps, 128), F32),
                pltpu.VMEM((taps, rows, 128), F32),
                pltpu.VMEM((rows, channels), BF),
                pltpu.VMEM((taps // 2, channels), BF),
                pltpu.VMEM((taps // 2, channels), BF),
                pltpu.VMEM((rows + taps, channels), F32),
                pltpu.VMEM((rows, channels), BF),
                dma((2,)),
                dma,
                dma,
                dma((8,)),
                dma((8,)),
                dma((4,)),
                dma((4,)),
                dma,
                dma,
                dma((6,)),
                dma((6,)),
                dma((NX * NY,)),
                dma((NX * NY,)),
                dma((2, 3)),
                dma((2, 3)),
                dma((2,)),
                dma((2,)),
            ],
            compiler_params=pltpu.CompilerParams(
                collective_id=0, has_side_effects=True, vmem_limit_bytes=60 * 2**20
            ),
            cost_estimate=pl.CostEstimate(flops=6 * 10**9, bytes_accessed=20 * 10**6, transcendentals=3 * 10**6),
        )(
            destinations,
            frames[0],
            segments,
            tile_mask[0],
            attn_gain[None],
            w_qkv,
            w_out,
            conv_gain[None],
            shard,
            pick,
            w_depth,
            bn_scale[None],
            bn_shift[None],
        )
        return out[None]

    return jax.shard_map(
        per_device,
        mesh=mesh,
        in_specs=(
            P("dp", "ctx", None),
            P("dp", "ctx"),
            P("dp", None),
            P("dp", "ctx", None),
            P(),
            P(),
            P(),
            P(),
            P(("dp", "ctx"), None),
            P(None, ("dp", "ctx")),
            P(),
            P(),
            P(),
        ),
        out_specs=P("dp", "ctx", None),
        check_vma=False,
    )
```

```python
import math

import numpy as np

import jax
import jax.numpy as jnp
from jax import lax
from jax.experimental import pallas as pl
from jax.experimental.pallas import tpu as pltpu
from jax.sharding import PartitionSpec as P

HEADS = 8
NX = 4
NY = 2
MESH = pl.DeviceIdType.MESH
BF = jnp.bfloat16
F32 = jnp.float32
MASKED = -2e38


def dot(a, b):
    return jnp.dot(a, b, preferred_element_type=F32)


def dot_nt(a, b):
    return lax.dot_general(a, b, (((1,), (1,)), ((), ())), preferred_element_type=F32)


def layer_norm(as_float, gain):
    row_mean = jnp.mean(as_float, axis=-1, keepdims=True)
    centred = as_float - row_mean
    row_var = jnp.mean(centred * centred, axis=-1, keepdims=True)
    return centred * lax.rsqrt(row_var + 1e-06) * gain


def layer_kernel(
    n_dp,
    shard_rows,
    dest_ref,
    frames_ref,
    seg_ref,
    tile_ref,
    again_ref,
    wqkv_hbm,
    wout_hbm,
    cgain_ref,
    pin_ref,
    pout_ref,
    pick_ref,
    wdepth_ref,
    bns_ref,
    bnb_ref,
    out_ref,
    wqkv_ref,
    wout_ref,
    send_ref,
    got_ref,
    meta_ref,
    gmeta_ref,
    prob_ref,
    zbuf_ref,
    cbuf_ref,
    wfull_ref,
    kv_ref,
    q_ref,
    att_ref,
    placed_ref,
    after_ref,
    bias_ref,
    segc_ref,
    segn_ref,
    mask_ref,
    gat_ref,
    htop_ref,
    hbot_ref,
    gf_ref,
    act_ref,
    load_sem,
    a_send,
    a_recv,
    m_send,
    m_recv,
    bz_send,
    bz_recv,
    bc_send,
    bc_recv,
    by_send,
    by_recv,
    bx_send,
    bx_recv,
    sib_send,
    sib_recv,
    kv_send,
    kv_recv,
    halo_send,
    halo_recv,
):
    rows, width = frames_ref.shape
    seq = seg_ref.shape[1]
    nz = n_dp // (NX * NY)
    cap = send_ref.shape[1]
    head_cols = wout_ref.shape[0]
    head = head_cols // HEADS
    group = head_cols // 2
    half_cols = cbuf_ref.shape[3]
    block = wfull_ref.shape[1] // (NX * NY)
    channels = wdepth_ref.shape[1]
    taps = wdepth_ref.shape[0]
    half = taps // 2
    tile = 128

    dp = lax.axis_index("dp")
    ctx = lax.axis_index("ctx")
    x = dp // (NY * nz)
    yh = (dp // nz) % NY
    z = dp % nz
    core = ctx % 2

    def dp_of(px, py, pz):
        return (px * NY + py) * nz + pz

    def peer(i):
        zi, rest = i // (NX * NY), NX * NY - 1 - i % (NX * NY)
        kz = nz // 2 + ((zi + 1) // 2) * (1 - 2 * (zi % 2))
        return dp_of((x + rest // NY) % NX, (yh + rest % NY) % NY, (z + kz + nz) % nz)

    def put(src, dst, ssem, rsem, d, c):
        copy = pltpu.make_async_remote_copy(
            src_ref=src, dst_ref=dst, send_sem=ssem, recv_sem=rsem, device_id=(d, c), device_id_type=MESH
        )
        copy.start()

    def settle(ref, sem):
        pltpu.make_async_copy(ref, ref, sem).wait()

    barrier = pltpu.get_barrier_semaphore()

    def greet(k, carry):
        pl.semaphore_signal(barrier, inc=1, device_id=(peer(k), ctx), device_id_type=MESH)
        return carry

    lax.fori_loop(0, n_dp - 1, greet, 0)
    for d in range(1, 4):
        pl.semaphore_signal(barrier, inc=1, device_id=(dp, ctx ^ d), device_id_type=MESH)

    load_qkv = pltpu.make_async_copy(wqkv_hbm, wqkv_ref, load_sem.at[0])
    load_qkv.start()
    load_out = pltpu.make_async_copy(wout_hbm, wout_ref, load_sem.at[1])
    load_out.start()

    dest = dest_ref[...]
    owner = dest // rows
    slot = dest % rows
    oz = owner % nz
    oy = (owner // nz) % NY
    ox = owner // (nz * NY)
    dz = (oz - z + nz) % nz - nz // 2
    zi = jnp.where(dz >= 0, 2 * dz, -2 * dz - 1)
    rel = (zi + 1) * (NX * NY) - 1 - (((ox - x + NX) % NX) * NY + (oy - yh + NY) % NY)
    rel_wide = jnp.broadcast_to(rel.astype(F32), (rows, rows))
    rel_tall = jnp.transpose(rel_wide)
    earlier = lax.broadcasted_iota(jnp.int32, (rows, rows), 0) < lax.broadcasted_iota(jnp.int32, (rows, rows), 1)
    rank = jnp.sum(jnp.where((rel_tall == rel_wide) & earlier, 1.0, 0.0), axis=0, keepdims=True)
    pos = rel * cap + rank.astype(jnp.int32)
    frames = frames_ref[...]
    per = n_dp // 4

    def pack(c):
        chunk = lax.broadcasted_iota(jnp.int32, (per * cap, rows), 0) + c * per * cap
        onehot = jnp.where(chunk == pos, 1.0, 0.0).astype(BF)
        send_ref[c * per : (c + 1) * per] = dot(onehot, frames).reshape(per, cap, width).astype(BF)

    def ship(i, carry):
        put(send_ref.at[i], got_ref.at[i], a_send, a_recv, peer(i), ctx)
        put(meta_ref.at[i], gmeta_ref.at[i], m_send, m_recv, peer(i), ctx)
        return carry

    def piece(px, py):
        start = pl.multiple_of((((px + NX) % NX) * NY + py) * block, 16)
        return wfull_ref.at[core, pl.ds(start, block)]

    right = dp_of((x + 1) % NX, yh, z)
    left = dp_of((x + NX - 1) % NX, yh, z)
    other = 1 - yh

    def to_sibling(i, ref):
        put(ref, ref, sib_send.at[i], sib_recv.at[i], dp, ctx ^ 1)

    zbuf_ref[pl.ds(z, 1)] = jnp.zeros((1,) + zbuf_ref.shape[1:], BF)
    for c in range(2):
        left_col = c * half_cols
        zbuf_ref[pl.ds(z, 1), :shard_rows, left_col : left_col + channels] = pin_ref[
            :, c * channels : (c + 1) * channels
        ][None]
        zbuf_ref[pl.ds(z, 1), :shard_rows, left_col + channels : left_col + half_cols] = pout_ref[
            :, c * (channels // 2) : (c + 1) * (channels // 2)
        ][None]
    pack(0)
    rank_tall = jnp.transpose(jnp.broadcast_to(rank, (tile, rows)))
    slot_tall = jnp.transpose(jnp.broadcast_to(slot.astype(F32) + 1.0, (tile, rows)))
    lane = lax.broadcasted_iota(jnp.int32, (rows, tile), 1).astype(F32)
    at_rank = jnp.where(rank_tall == lane, slot_tall, 0.0).astype(BF)
    to_peer = jnp.where(lax.broadcasted_iota(jnp.int32, (n_dp, rows), 0) == rel, 1.0, 0.0).astype(BF)
    meta_ref[...] = dot(to_peer, at_rank).reshape(n_dp, 1, tile)
    pl.semaphore_wait(barrier, n_dp - 1 + 3)
    for k in range(1, nz):
        put(zbuf_ref.at[z], zbuf_ref.at[z], bz_send.at[k], bz_recv.at[k], dp_of(x, yh, (z + k) % nz), ctx)
    lax.fori_loop(0, per, ship, 0)
    pack(1)

    for k in range(1, nz):
        settle(zbuf_ref.at[0], bz_recv.at[k])
    for d in range(1, 4):
        cols = pl.ds(pl.multiple_of(((ctx ^ d) % 2) * half_cols, 128), half_cols)
        put(zbuf_ref.at[:, :, cols], cbuf_ref.at[ctx], bc_send.at[d], bc_recv.at[d], dp, ctx ^ d)
    lax.fori_loop(per, 2 * per, ship, 0)
    mine = pl.ds(pl.multiple_of(core * half_cols, 128), half_cols)
    cbuf_ref[pl.ds(ctx, 1)] = zbuf_ref[:, :, mine][None]
    pack(2)
    pack(3)
    for d in range(1, 4):
        settle(cbuf_ref.at[0], bc_recv.at[d])
    padded = cbuf_ref[...].astype(F32).reshape(pick_ref.shape[1], half_cols).astype(BF)
    own_start = pl.multiple_of((x * NY + yh) * block, 16)
    wfull_ref[core, pl.ds(own_start, block)] = dot(pick_ref[...], padded).astype(BF)
    put(piece(x, yh), piece(x, yh), by_send, by_recv, dp_of(x, other, z), ctx)
    put(piece(x, yh), piece(x, yh), bx_send.at[0], bx_recv.at[0], right, ctx)
    put(piece(x, yh), piece(x, yh), bx_send.at[1], bx_recv.at[1], left, ctx)
    to_sibling(0, piece(x, yh))
    lax.fori_loop(2 * per, n_dp - 1, ship, 0)
    got_ref[n_dp - 1] = send_ref[n_dp - 1]
    gmeta_ref[n_dp - 1] = meta_ref[n_dp - 1]

    segf = seg_ref[...].astype(F32)
    segc_ref[0:half] = jnp.full((half, tile), -1.0, F32)
    segc_ref[half + seq :] = jnp.full((half, tile), -1.0, F32)
    segc_ref[half : half + seq] = jnp.transpose(jnp.broadcast_to(segf, (tile, seq)))
    first = pl.multiple_of(ctx * rows, rows)
    segn_ref[...] = segc_ref[pl.ds(first, rows + 2 * half)]
    own_seg = segn_ref[half : half + rows]
    for tk in range(seq // tile):
        same = own_seg == segf[:, tk * tile : (tk + 1) * tile]
        for tq in range(rows // tile):
            off = (1 - tile_ref[tq, tk]).astype(F32) * MASKED
            bias_ref[tq * tile : (tq + 1) * tile, tk * tile : (tk + 1) * tile] = jnp.where(
                same[tq * tile : (tq + 1) * tile], off, MASKED
            )
    for k in range(taps):
        mask_ref[k] = jnp.where(segn_ref[k : k + rows] == own_seg, 1.0, 0.0)

    def send_pair():
        settle(piece(x, other), by_recv)
        put(piece(x, other), piece(x, other), bx_send.at[2], bx_recv.at[2], right, ctx)
        put(piece(x, other), piece(x, other), bx_send.at[3], bx_recv.at[3], left, ctx)
        to_sibling(1, piece(x, other))

    send_pair()

    settle(gmeta_ref.at[pl.ds(0, n_dp - 1)], m_recv)
    spots = n_dp * cap
    spot = lax.broadcasted_iota(jnp.int32, (tile, spots), 1)
    spread = jnp.where(lax.broadcasted_iota(jnp.int32, (tile, spots), 0) == spot % cap, 1.0, 0.0).astype(BF)
    spread = dot(gmeta_ref[...].reshape(n_dp, tile).astype(BF), spread)
    spot = lax.broadcasted_iota(jnp.int32, (n_dp, spots), 1)
    from_peer = lax.broadcasted_iota(jnp.int32, (n_dp, spots), 0) == spot // cap
    slots = jnp.sum(jnp.where(from_peer, spread, 0.0), axis=0, keepdims=True)
    lane = lax.broadcasted_iota(jnp.int32, (rows, spots), 0).astype(F32) + 1.0
    place = jnp.where(lane == slots, 1.0, 0.0).astype(BF)
    settle(got_ref.at[pl.ds(0, n_dp - 1)], a_recv)
    got = got_ref[...].astype(F32).reshape(spots, width).astype(BF)
    placed = dot(place, got)
    placed_ref[...] = placed
    normed = layer_norm(placed, again_ref[...][None]).astype(BF)

    load_qkv.wait()
    base = pl.multiple_of(ctx * rows, rows)
    keys = dot(normed, wqkv_ref[:, head_cols : 2 * head_cols]).astype(BF)
    values = dot(normed, wqkv_ref[:, 2 * head_cols :]).astype(BF)
    for g in range(2):
        kv_ref[pl.ds(base, rows), 2 * g * group : (2 * g + 1) * group] = keys[:, g * group : (g + 1) * group]
        kv_ref[pl.ds(base, rows), (2 * g + 1) * group : (2 * g + 2) * group] = values[:, g * group : (g + 1) * group]

    def kv_part(c, i):
        return kv_ref.at[pl.ds(pl.multiple_of(c * rows, rows), rows), pl.ds(i * group, group)]

    for i in range(4):
        part = kv_part(ctx, i)
        put(part, part, kv_send.at[i, 0], kv_recv.at[i, 0], dp, ctx ^ 2)
        put(part, part, kv_send.at[i, 1], kv_recv.at[i, 1], dp, ctx ^ 1)
    scale = math.log2(math.e) / math.sqrt(head)
    q_ref[...] = (dot(normed, wqkv_ref[:, :head_cols]) * scale).astype(BF)

    def arrive(i):
        part = kv_part(ctx ^ 2, i)
        settle(part, kv_recv.at[i, 0])
        put(part, part, kv_send.at[i, 2], kv_recv.at[i, 2], dp, ctx ^ 1)
        settle(part, kv_recv.at[i, 1])
        settle(part, kv_recv.at[i, 2])

    def windows(h):
        lo, hi = h * head, (h + 1) * head
        c0, c1 = lo // tile * tile, (hi + tile - 1) // tile * tile
        lanes = lax.broadcasted_iota(jnp.int32, (rows, c1 - c0), 1) + c0
        return c0, c1, (lanes >= lo) & (lanes < hi)

    def score(g):
        totals = []
        for h in range(HEADS // 2):
            c0, c1, inside = windows(h)
            query = q_ref[:, g * group + c0 : g * group + c1].astype(F32)
            query = jnp.where(inside, query, 0.0).astype(BF)
            scores = dot_nt(query, kv_ref[:, 2 * g * group + c0 : 2 * g * group + c1]) + bias_ref[...]
            weights = jnp.exp2(scores - jnp.max(scores, axis=1, keepdims=True))
            totals.append(jnp.sum(weights, axis=1, keepdims=True))
            prob_ref[h] = weights.astype(BF)
        return totals

    def mix(g, totals):
        tiles = [None] * (group // tile)
        for h in range(HEADS // 2):
            c0, c1, inside = windows(h)
            mixed = dot(prob_ref[h], kv_ref[:, (2 * g + 1) * group + c0 : (2 * g + 1) * group + c1])
            mixed = jnp.where(inside, mixed / totals[h], 0.0)
            for t in range(c0 // tile, c1 // tile):
                term = mixed[:, t * tile - c0 : (t + 1) * tile - c0]
                tiles[t] = term if tiles[t] is None else tiles[t] + term
        for t, whole in enumerate(tiles):
            att_ref[:, g * group + t * tile : g * group + (t + 1) * tile] = whole.astype(BF)

    arrive(0)
    totals = score(0)
    arrive(1)
    mix(0, totals)
    settle(piece(x - 1, yh), bx_recv.at[0])
    settle(piece(x + 1, yh), bx_recv.at[1])
    put(piece(x - 1, yh), piece(x - 1, yh), bx_send.at[4], bx_recv.at[4], right, ctx)
    to_sibling(2, piece(x - 1, yh))
    to_sibling(3, piece(x + 1, yh))
    arrive(2)
    totals = score(1)
    settle(piece(x - 1, other), bx_recv.at[2])
    settle(piece(x + 1, other), bx_recv.at[3])
    put(piece(x + 1, other), piece(x + 1, other), bx_send.at[5], bx_recv.at[5], left, ctx)
    to_sibling(4, piece(x - 1, other))
    to_sibling(5, piece(x + 1, other))
    arrive(3)
    mix(1, totals)

    load_out.wait()
    after = (placed_ref[...] + dot(att_ref[...], wout_ref[...])).astype(BF)
    after_ref[...] = after
    conv_normed = layer_norm(after.astype(F32), cgain_ref[...][None]).astype(BF)

    settle(piece(x + 2, yh), bx_recv.at[4])
    to_sibling(6, piece(x + 2, yh))
    settle(piece(x + 2, other), bx_recv.at[5])
    to_sibling(7, piece(x + 2, other))
    for i in range(NX * NY):
        settle(piece(x, yh), sib_recv.at[i])

    gate = jax.nn.sigmoid(dot(conv_normed, wfull_ref[1, :, :channels]))
    gated = (dot(conv_normed, wfull_ref[0, :, :channels]) * gate).astype(BF)
    gat_ref[...] = gated
    gf_ref[half : half + rows] = gated.astype(F32)

    head_rows = gat_ref.at[0:half]
    tail_rows = gat_ref.at[rows - half : rows]

    @pl.when(ctx > 0)
    def _():
        put(head_rows, hbot_ref, halo_send.at[0], halo_recv.at[0], dp, ctx - 1)

    @pl.when(ctx < 3)
    def _():
        put(tail_rows, htop_ref, halo_send.at[1], halo_recv.at[1], dp, ctx + 1)

    @pl.when(ctx == 0)
    def _():
        htop_ref[...] = jnp.zeros_like(htop_ref)

    @pl.when(ctx == 3)
    def _():
        hbot_ref[...] = jnp.zeros_like(hbot_ref)

    span = 64

    def convolve(r0):
        def body(t, carry):
            lanes = pl.ds(pl.multiple_of(t * tile, tile), tile)
            near = gf_ref[r0 : r0 + span + 2 * half, lanes]
            total = jnp.zeros((span, tile), F32)
            for b in range(8):
                shifted = near if b == 0 else pltpu.roll(near, span + 2 * half - b, 0)
                for a in range(taps // 8):
                    k = 8 * a + b
                    term = shifted[8 * a : 8 * a + span] * mask_ref[k, r0 : r0 + span]
                    total = total + term * wdepth_ref[k : k + 1, lanes]
            moved = total * bns_ref[lanes][None] + bnb_ref[lanes][None]
            act_ref[r0 : r0 + span, lanes] = (moved * jax.nn.sigmoid(moved)).astype(BF)
            return carry

        lax.fori_loop(0, channels // tile, body, 0)

    for r0 in range(span, rows - span, span):
        convolve(r0)

    @pl.when(ctx > 0)
    def _():
        settle(htop_ref, halo_recv.at[1])

    @pl.when(ctx < 3)
    def _():
        settle(hbot_ref, halo_recv.at[0])

    gf_ref[0:half] = htop_ref[...].astype(F32)
    gf_ref[half + rows :] = hbot_ref[...].astype(F32)
    convolve(0)
    convolve(rows - span)

    quarter = channels // 2
    closing = dot_nt(act_ref[:, :quarter], wfull_ref[0, :, channels:])
    closing = closing + dot_nt(act_ref[:, quarter:], wfull_ref[1, :, channels:])
    out_ref[...] = (after_ref[...].astype(F32) + closing).astype(BF)

    settle(send_ref.at[pl.ds(0, n_dp - 1)], a_send)
    settle(meta_ref.at[pl.ds(0, n_dp - 1)], m_send)
    for k in range(1, nz):
        settle(zbuf_ref.at[0], bz_send.at[k])
    for d in range(1, 4):
        settle(cbuf_ref.at[0], bc_send.at[d])
    settle(piece(x, yh), by_send)
    for i in range(6):
        settle(piece(x, yh), bx_send.at[i])
    for i in range(NX * NY):
        settle(piece(x, yh), sib_send.at[i])
    for i in range(4):
        for j in range(3):
            settle(kv_part(ctx, i), kv_send.at[i, j])

    @pl.when(ctx > 0)
    def _():
        settle(head_rows, halo_send.at[0])

    @pl.when(ctx < 3)
    def _():
        settle(tail_rows, halo_send.at[1])


def solution(mesh):
    n_dp = mesh.shape["dp"]
    n_ctx = mesh.shape["ctx"]
    nz = n_dp // (NX * NY)

    def per_device(
        frames,
        destinations,
        segments,
        tile_mask,
        attn_gain,
        w_qkv,
        w_out,
        conv_gain,
        w_pointin,
        w_pointout,
        w_depth,
        bn_scale,
        bn_shift,
    ):
        rows, width = frames.shape[1:]
        seq = segments.shape[1]
        channels = w_depth.shape[1]
        taps = w_depth.shape[0]
        head_cols = w_out.shape[0]
        cap = 2 * rows // n_dp
        shard_rows = w_pointin.shape[0]
        pad_rows = -(-shard_rows // 8) * 8
        half_cols = channels + channels // 2
        pick = np.zeros((nz * n_ctx * shard_rows, n_ctx * nz * pad_rows), np.float32)
        for a in range(nz):
            for b in range(n_ctx):
                for j in range(shard_rows):
                    pick[(a * n_ctx + b) * shard_rows + j, (b * nz + a) * pad_rows + j] = 1.0
        pick = jnp.asarray(pick, BF)
        vmem = pl.BlockSpec(memory_space=pltpu.VMEM)
        smem = pl.BlockSpec(memory_space=pltpu.SMEM)
        hbm = pl.BlockSpec(memory_space=pl.ANY)

        def body(*refs):
            layer_kernel(n_dp, shard_rows, *refs)

        dma = pltpu.SemaphoreType.DMA
        out = pl.pallas_call(
            body,
            name="conformer_layer",
            out_shape=jax.ShapeDtypeStruct((rows, width), BF),
            in_specs=[vmem, vmem, vmem, smem, vmem, hbm, hbm] + [vmem] * 7,
            out_specs=vmem,
            scratch_shapes=[
                pltpu.VMEM(w_qkv.shape, BF),
                pltpu.VMEM(w_out.shape, BF),
                pltpu.VMEM((n_dp, cap, width), BF),
                pltpu.VMEM((n_dp, cap, width), BF),
                pltpu.VMEM((n_dp, 1, 128), F32),
                pltpu.VMEM((n_dp, 1, 128), F32),
                pltpu.VMEM((HEADS // 2, rows, seq), BF),
                pltpu.VMEM((nz, pad_rows, 2 * half_cols), BF),
                pltpu.VMEM((n_ctx, nz, pad_rows, half_cols), BF),
                pltpu.VMEM((2, width, half_cols), BF),
                pltpu.VMEM((seq, 2 * head_cols), BF),
                pltpu.VMEM((rows, head_cols), BF),
                pltpu.VMEM((rows, head_cols), BF),
                pltpu.VMEM((rows, width), F32),
                pltpu.VMEM((rows, width), BF),
                pltpu.VMEM((rows, seq), F32),
                pltpu.VMEM((seq + taps, 128), F32),
                pltpu.VMEM((rows + taps, 128), F32),
                pltpu.VMEM((taps, rows, 128), F32),
                pltpu.VMEM((rows, channels), BF),
                pltpu.VMEM((taps // 2, channels), BF),
                pltpu.VMEM((taps // 2, channels), BF),
                pltpu.VMEM((rows + taps, channels), F32),
                pltpu.VMEM((rows, channels), BF),
                dma((2,)),
                dma,
                dma,
                dma,
                dma,
                dma((8,)),
                dma((8,)),
                dma((4,)),
                dma((4,)),
                dma,
                dma,
                dma((6,)),
                dma((6,)),
                dma((NX * NY,)),
                dma((NX * NY,)),
                dma((4, 3)),
                dma((4, 3)),
                dma((2,)),
                dma((2,)),
            ],
            compiler_params=pltpu.CompilerParams(
                collective_id=0, has_side_effects=True, vmem_limit_bytes=60 * 2**20
            ),
            cost_estimate=pl.CostEstimate(flops=6 * 10**9, bytes_accessed=20 * 10**6, transcendentals=3 * 10**6),
        )(
            destinations,
            frames[0],
            segments,
            tile_mask[0],
            attn_gain,
            w_qkv,
            w_out,
            conv_gain,
            w_pointin,
            w_pointout.T,
            pick,
            w_depth,
            bn_scale,
            bn_shift,
        )

        def hand_on(src_ref, dst_ref, sem):
            copies = []
            for i in range(4):
                part = pl.ds(i * (rows // 4), rows // 4)
                copies.append(pltpu.make_async_copy(src_ref.at[part], dst_ref.at[part], sem.at[i]))
                copies[i].start()
            for copy in copies:
                copy.wait()

        out = pl.pallas_call(
            hand_on,
            name="result",
            out_shape=jax.ShapeDtypeStruct((rows, width), BF),
            in_specs=[hbm],
            out_specs=hbm,
            scratch_shapes=[dma((4,))],
            compiler_params=pltpu.CompilerParams(vmem_limit_bytes=2**20),
        )(out)
        return out[None]

    return jax.shard_map(
        per_device,
        mesh=mesh,
        in_specs=(
            P("dp", "ctx", None),
            P("dp", "ctx"),
            P("dp", None),
            P("dp", "ctx", None),
            P(),
            P(),
            P(),
            P(),
            P(("dp", "ctx"), None),
            P(None, ("dp", "ctx")),
            P(),
            P(),
            P(),
        ),
        out_specs=P("dp", "ctx", None),
        check_vma=False,
    )
```

```python
import math

import numpy as np

import jax
import jax.numpy as jnp
from jax import lax
from jax.experimental import pallas as pl
from jax.experimental.pallas import tpu as pltpu
from jax.sharding import PartitionSpec as P

HEADS = 8
NX = 4
NY = 2
MESH = pl.DeviceIdType.MESH
BF = jnp.bfloat16
F32 = jnp.float32
MASKED = -2e38


def dot(a, b):
    return jnp.dot(a, b, preferred_element_type=F32)


def dot_nt(a, b):
    return lax.dot_general(a, b, (((1,), (1,)), ((), ())), preferred_element_type=F32)


def layer_norm(as_float, gain):
    row_mean = jnp.mean(as_float, axis=-1, keepdims=True)
    centred = as_float - row_mean
    row_var = jnp.mean(centred * centred, axis=-1, keepdims=True)
    return centred * lax.rsqrt(row_var + 1e-06) * gain


def layer_kernel(
    n_dp,
    shard_rows,
    dest_ref,
    frames_ref,
    seg_ref,
    tile_ref,
    again_ref,
    wqkv_hbm,
    wout_hbm,
    cgain_ref,
    pin_ref,
    pout_ref,
    pick_ref,
    wdepth_ref,
    bns_ref,
    bnb_ref,
    out_ref,
    wqkv_ref,
    wout_ref,
    send_ref,
    got_ref,
    meta_ref,
    gmeta_ref,
    prob_ref,
    zbuf_ref,
    cbuf_ref,
    wfull_ref,
    kv_ref,
    q_ref,
    att_ref,
    placed_ref,
    after_ref,
    bias_ref,
    segc_ref,
    segn_ref,
    mask_ref,
    gat_ref,
    htop_ref,
    hbot_ref,
    gf_ref,
    act_ref,
    load_sem,
    a_send,
    a_recv,
    m_send,
    m_recv,
    bz_send,
    bz_recv,
    bc_send,
    bc_recv,
    by_send,
    by_recv,
    bx_send,
    bx_recv,
    sib_send,
    sib_recv,
    kv_send,
    kv_recv,
    halo_send,
    halo_recv,
):
    rows, width = frames_ref.shape
    seq = seg_ref.shape[1]
    nz = n_dp // (NX * NY)
    cap = send_ref.shape[1]
    head_cols = wout_ref.shape[0]
    head = head_cols // HEADS
    group = head_cols // 2
    half_cols = cbuf_ref.shape[3]
    block = wfull_ref.shape[1] // (NX * NY)
    channels = wdepth_ref.shape[1]
    taps = wdepth_ref.shape[0]
    half = taps // 2
    tile = 128

    dp = lax.axis_index("dp")
    ctx = lax.axis_index("ctx")
    x = dp // (NY * nz)
    yh = (dp // nz) % NY
    z = dp % nz
    core = ctx % 2

    def dp_of(px, py, pz):
        return (px * NY + py) * nz + pz

    def peer(i):
        zi, rest = i // (NX * NY), NX * NY - 1 - i % (NX * NY)
        kz = nz // 2 + ((zi + 1) // 2) * (1 - 2 * (zi % 2))
        return dp_of((x + rest // NY) % NX, (yh + rest % NY) % NY, (z + kz + nz) % nz)

    def put(src, dst, ssem, rsem, d, c):
        copy = pltpu.make_async_remote_copy(
            src_ref=src, dst_ref=dst, send_sem=ssem, recv_sem=rsem, device_id=(d, c), device_id_type=MESH
        )
        copy.start()

    def settle(ref, sem):
        pltpu.make_async_copy(ref, ref, sem).wait()

    barrier = pltpu.get_barrier_semaphore()

    def greet(k, carry):
        pl.semaphore_signal(barrier, inc=1, device_id=(peer(k), ctx), device_id_type=MESH)
        return carry

    lax.fori_loop(0, n_dp - 1, greet, 0)
    for d in range(1, 4):
        pl.semaphore_signal(barrier, inc=1, device_id=(dp, ctx ^ d), device_id_type=MESH)

    load_qkv = pltpu.make_async_copy(wqkv_hbm, wqkv_ref, load_sem.at[0])
    load_qkv.start()
    load_out = pltpu.make_async_copy(wout_hbm, wout_ref, load_sem.at[1])
    load_out.start()

    dest = dest_ref[...]
    owner = dest // rows
    slot = dest % rows
    oz = owner % nz
    oy = (owner // nz) % NY
    ox = owner // (nz * NY)
    dz = (oz - z + nz) % nz - nz // 2
    zi = jnp.where(dz >= 0, 2 * dz, -2 * dz - 1)
    rel = (zi + 1) * (NX * NY) - 1 - (((ox - x + NX) % NX) * NY + (oy - yh + NY) % NY)
    rel_wide = jnp.broadcast_to(rel.astype(F32), (rows, rows))
    rel_tall = jnp.transpose(rel_wide)
    earlier = lax.broadcasted_iota(jnp.int32, (rows, rows), 0) < lax.broadcasted_iota(jnp.int32, (rows, rows), 1)
    rank = jnp.sum(jnp.where((rel_tall == rel_wide) & earlier, 1.0, 0.0), axis=0, keepdims=True)
    pos = rel * cap + rank.astype(jnp.int32)
    frames = frames_ref[...]
    per = n_dp // 4

    def pack(c):
        chunk = lax.broadcasted_iota(jnp.int32, (per * cap, rows), 0) + c * per * cap
        onehot = jnp.where(chunk == pos, 1.0, 0.0).astype(BF)
        send_ref[c * per : (c + 1) * per] = dot(onehot, frames).reshape(per, cap, width).astype(BF)

    def ship(i, carry):
        put(send_ref.at[i], got_ref.at[i], a_send, a_recv, peer(i), ctx)
        put(meta_ref.at[i], gmeta_ref.at[i], m_send, m_recv, peer(i), ctx)
        return carry

    def piece(px, py, part):
        start = pl.multiple_of((((px + NX) % NX) * NY + py) * block, 16)
        cols = pl.ds(0, channels) if part == 0 else pl.ds(channels, half_cols - channels)
        return wfull_ref.at[core, pl.ds(start, block), cols]

    right = dp_of((x + 1) % NX, yh, z)
    left = dp_of((x + NX - 1) % NX, yh, z)
    other = 1 - yh

    def to_sibling(i, px, py, part):
        ref = piece(px, py, part)
        put(ref, ref, sib_send.at[part, i], sib_recv.at[part, i], dp, ctx ^ 1)

    def to_x(i, px, py, part, d):
        ref = piece(px, py, part)
        put(ref, ref, bx_send.at[part, i], bx_recv.at[part, i], d, ctx)

    def own_to_x(part):
        to_x(0, x, yh, part, right)
        to_x(1, x, yh, part, left)

    def pair_to_x(part):
        settle(piece(x, other, part), by_recv.at[part])
        to_x(2, x, other, part, right)
        to_x(3, x, other, part, left)
        to_sibling(1, x, other, part)

    def hand_right(part):
        settle(piece(x - 1, yh, part), bx_recv.at[part, 0])
        settle(piece(x + 1, yh, part), bx_recv.at[part, 1])
        to_x(4, x - 1, yh, part, right)
        to_sibling(2, x - 1, yh, part)
        to_sibling(3, x + 1, yh, part)

    def hand_left(part):
        settle(piece(x - 1, other, part), bx_recv.at[part, 2])
        settle(piece(x + 1, other, part), bx_recv.at[part, 3])
        to_x(5, x + 1, other, part, left)
        to_sibling(4, x - 1, other, part)
        to_sibling(5, x + 1, other, part)

    def two_away(part):
        settle(piece(x + 2, yh, part), bx_recv.at[part, 4])
        to_sibling(6, x + 2, yh, part)
        settle(piece(x + 2, other, part), bx_recv.at[part, 5])
        to_sibling(7, x + 2, other, part)

    def from_sibling(part):
        for i in range(NX * NY):
            settle(piece(x, yh, part), sib_recv.at[part, i])

    zbuf_ref[pl.ds(z, 1)] = jnp.zeros((1,) + zbuf_ref.shape[1:], BF)
    for c in range(2):
        left_col = c * half_cols
        zbuf_ref[pl.ds(z, 1), :shard_rows, left_col : left_col + channels] = pin_ref[
            :, c * channels : (c + 1) * channels
        ][None]
        zbuf_ref[pl.ds(z, 1), :shard_rows, left_col + channels : left_col + half_cols] = pout_ref[
            :, c * (channels // 2) : (c + 1) * (channels // 2)
        ][None]
    pack(0)
    rank_tall = jnp.transpose(jnp.broadcast_to(rank, (tile, rows)))
    slot_tall = jnp.transpose(jnp.broadcast_to(slot.astype(F32) + 1.0, (tile, rows)))
    lane = lax.broadcasted_iota(jnp.int32, (rows, tile), 1).astype(F32)
    at_rank = jnp.where(rank_tall == lane, slot_tall, 0.0).astype(BF)
    to_peer = jnp.where(lax.broadcasted_iota(jnp.int32, (n_dp, rows), 0) == rel, 1.0, 0.0).astype(BF)
    meta_ref[...] = dot(to_peer, at_rank).reshape(n_dp, 1, tile)
    pl.semaphore_wait(barrier, n_dp - 1 + 3)
    def along_z(root, k):
        shard = zbuf_ref.at[(root + nz) % nz]
        put(shard, shard, bz_send.at[k], bz_recv.at[k], dp_of(x, yh, (root + k + nz) % nz), ctx)

    if nz == 8:
        along_z(z, 2)
        along_z(z, 6)
    else:
        for k in range(1, nz):
            along_z(z, k)
    lax.fori_loop(0, n_dp // 16, ship, 0)
    if nz == 8:
        settle(zbuf_ref.at[0], bz_recv.at[2])
        for k in (1, 3, 4):
            along_z(z - 2, k)
        settle(zbuf_ref.at[0], bz_recv.at[6])
        for k in (5, 7):
            along_z(z + 2, k)
    lax.fori_loop(n_dp // 16, n_dp // 8, ship, 0)
    pack(1)
    for k in range(1, nz):
        if nz != 8 or k not in (2, 6):
            settle(zbuf_ref.at[0], bz_recv.at[k])
    for d in range(1, 4):
        cols = pl.ds(pl.multiple_of(((ctx ^ d) % 2) * half_cols, 128), half_cols)
        put(zbuf_ref.at[:, :, cols], cbuf_ref.at[ctx], bc_send.at[d], bc_recv.at[d], dp, ctx ^ d)
    lax.fori_loop(n_dp // 8, n_dp // 4, ship, 0)
    mine = pl.ds(pl.multiple_of(core * half_cols, 128), half_cols)
    cbuf_ref[pl.ds(ctx, 1)] = zbuf_ref[:, :, mine][None]
    pack(2)
    pack(3)
    for d in range(1, 4):
        settle(cbuf_ref.at[0], bc_recv.at[d])
    padded = cbuf_ref[...].astype(F32).reshape(pick_ref.shape[1], half_cols).astype(BF)
    own_start = pl.multiple_of((x * NY + yh) * block, 16)
    wfull_ref[core, pl.ds(own_start, block)] = dot(pick_ref[...], padded).astype(BF)
    for part in range(2):
        ref = piece(x, yh, part)
        put(ref, ref, by_send.at[part], by_recv.at[part], dp_of(x, other, z), ctx)
        if part == 0:
            own_to_x(0)
        to_sibling(0, x, yh, part)
    lax.fori_loop(per, n_dp - 1, ship, 0)
    own_to_x(1)
    got_ref[n_dp - 1] = send_ref[n_dp - 1]
    gmeta_ref[n_dp - 1] = meta_ref[n_dp - 1]

    segf = seg_ref[...].astype(F32)
    segc_ref[0:half] = jnp.full((half, tile), -1.0, F32)
    segc_ref[half + seq :] = jnp.full((half, tile), -1.0, F32)
    segc_ref[half : half + seq] = jnp.transpose(jnp.broadcast_to(segf, (tile, seq)))
    first = pl.multiple_of(ctx * rows, rows)
    segn_ref[...] = segc_ref[pl.ds(first, rows + 2 * half)]
    own_seg = segn_ref[half : half + rows]
    for tk in range(seq // tile):
        same = own_seg == segf[:, tk * tile : (tk + 1) * tile]
        for tq in range(rows // tile):
            off = (1 - tile_ref[tq, tk]).astype(F32) * MASKED
            bias_ref[tq * tile : (tq + 1) * tile, tk * tile : (tk + 1) * tile] = jnp.where(
                same[tq * tile : (tq + 1) * tile], off, MASKED
            )
    for k in range(taps):
        mask_ref[k] = jnp.where(segn_ref[k : k + rows] == own_seg, 1.0, 0.0)

    pair_to_x(0)
    pair_to_x(1)

    settle(gmeta_ref.at[pl.ds(0, n_dp - 1)], m_recv)
    spots = n_dp * cap
    spot = lax.broadcasted_iota(jnp.int32, (tile, spots), 1)
    spread = jnp.where(lax.broadcasted_iota(jnp.int32, (tile, spots), 0) == spot % cap, 1.0, 0.0).astype(BF)
    spread = dot(gmeta_ref[...].reshape(n_dp, tile).astype(BF), spread)
    spot = lax.broadcasted_iota(jnp.int32, (n_dp, spots), 1)
    from_peer = lax.broadcasted_iota(jnp.int32, (n_dp, spots), 0) == spot // cap
    slots = jnp.sum(jnp.where(from_peer, spread, 0.0), axis=0, keepdims=True)
    lane = lax.broadcasted_iota(jnp.int32, (rows, spots), 0).astype(F32) + 1.0
    place = jnp.where(lane == slots, 1.0, 0.0).astype(BF)
    settle(got_ref.at[pl.ds(0, n_dp - 1)], a_recv)
    got = got_ref[...].astype(F32).reshape(spots, width).astype(BF)
    placed = dot(place, got)
    placed_ref[...] = placed
    normed = layer_norm(placed, again_ref[...][None]).astype(BF)

    load_qkv.wait()
    base = pl.multiple_of(ctx * rows, rows)
    keys = dot(normed, wqkv_ref[:, head_cols : 2 * head_cols]).astype(BF)
    values = dot(normed, wqkv_ref[:, 2 * head_cols :]).astype(BF)
    for g in range(2):
        kv_ref[pl.ds(base, rows), 2 * g * group : (2 * g + 1) * group] = keys[:, g * group : (g + 1) * group]
        kv_ref[pl.ds(base, rows), (2 * g + 1) * group : (2 * g + 2) * group] = values[:, g * group : (g + 1) * group]

    def kv_part(c, i):
        return kv_ref.at[pl.ds(pl.multiple_of(c * rows, rows), rows), pl.ds(i * group, group)]

    for i in range(4):
        part = kv_part(ctx, i)
        put(part, part, kv_send.at[i, 0], kv_recv.at[i, 0], dp, ctx ^ 2)
        put(part, part, kv_send.at[i, 1], kv_recv.at[i, 1], dp, ctx ^ 1)
    scale = math.log2(math.e) / math.sqrt(head)
    q_ref[...] = (dot(normed, wqkv_ref[:, :head_cols]) * scale).astype(BF)

    def arrive(i):
        part = kv_part(ctx ^ 2, i)
        settle(part, kv_recv.at[i, 0])
        put(part, part, kv_send.at[i, 2], kv_recv.at[i, 2], dp, ctx ^ 1)
        settle(part, kv_recv.at[i, 1])
        settle(part, kv_recv.at[i, 2])

    def windows(h):
        lo, hi = h * head, (h + 1) * head
        c0, c1 = lo // tile * tile, (hi + tile - 1) // tile * tile
        lanes = lax.broadcasted_iota(jnp.int32, (rows, c1 - c0), 1) + c0
        return c0, c1, (lanes >= lo) & (lanes < hi)

    def score(g):
        totals = []
        for h in range(HEADS // 2):
            c0, c1, inside = windows(h)
            query = q_ref[:, g * group + c0 : g * group + c1].astype(F32)
            query = jnp.where(inside, query, 0.0).astype(BF)
            scores = dot_nt(query, kv_ref[:, 2 * g * group + c0 : 2 * g * group + c1]) + bias_ref[...]
            weights = jnp.exp2(scores - jnp.max(scores, axis=1, keepdims=True))
            totals.append(jnp.sum(weights, axis=1, keepdims=True))
            prob_ref[h] = weights.astype(BF)
        return totals

    def mix(g, totals):
        tiles = [None] * (group // tile)
        for h in range(HEADS // 2):
            c0, c1, inside = windows(h)
            mixed = dot(prob_ref[h], kv_ref[:, (2 * g + 1) * group + c0 : (2 * g + 1) * group + c1])
            mixed = jnp.where(inside, mixed / totals[h], 0.0)
            for t in range(c0 // tile, c1 // tile):
                term = mixed[:, t * tile - c0 : (t + 1) * tile - c0]
                tiles[t] = term if tiles[t] is None else tiles[t] + term
        for t, whole in enumerate(tiles):
            att_ref[:, g * group + t * tile : g * group + (t + 1) * tile] = whole.astype(BF)

    hand_right(0)
    arrive(0)
    totals = score(0)
    hand_left(0)
    arrive(1)
    mix(0, totals)
    arrive(2)
    totals = score(1)
    hand_right(1)
    arrive(3)
    mix(1, totals)

    load_out.wait()
    after = (placed_ref[...] + dot(att_ref[...], wout_ref[...])).astype(BF)
    after_ref[...] = after
    conv_normed = layer_norm(after.astype(F32), cgain_ref[...][None]).astype(BF)

    two_away(0)
    hand_left(1)
    from_sibling(0)

    gate = jax.nn.sigmoid(dot(conv_normed, wfull_ref[1, :, :channels]))
    gated = (dot(conv_normed, wfull_ref[0, :, :channels]) * gate).astype(BF)
    gat_ref[...] = gated
    gf_ref[half : half + rows] = gated.astype(F32)

    head_rows = gat_ref.at[0:half]
    tail_rows = gat_ref.at[rows - half : rows]

    @pl.when(ctx > 0)
    def _():
        put(head_rows, hbot_ref, halo_send.at[0], halo_recv.at[0], dp, ctx - 1)

    @pl.when(ctx < 3)
    def _():
        put(tail_rows, htop_ref, halo_send.at[1], halo_recv.at[1], dp, ctx + 1)

    @pl.when(ctx == 0)
    def _():
        htop_ref[...] = jnp.zeros_like(htop_ref)

    @pl.when(ctx == 3)
    def _():
        hbot_ref[...] = jnp.zeros_like(hbot_ref)

    span = 64

    def convolve(r0):
        def body(t, carry):
            lanes = pl.ds(pl.multiple_of(t * tile, tile), tile)
            near = gf_ref[r0 : r0 + span + 2 * half, lanes]
            total = jnp.zeros((span, tile), F32)
            for b in range(8):
                shifted = near if b == 0 else pltpu.roll(near, span + 2 * half - b, 0)
                for a in range(taps // 8):
                    k = 8 * a + b
                    term = shifted[8 * a : 8 * a + span] * mask_ref[k, r0 : r0 + span]
                    total = total + term * wdepth_ref[k : k + 1, lanes]
            moved = total * bns_ref[lanes][None] + bnb_ref[lanes][None]
            act_ref[r0 : r0 + span, lanes] = (moved * jax.nn.sigmoid(moved)).astype(BF)
            return carry

        lax.fori_loop(0, channels // tile, body, 0)

    for r0 in range(span, rows - span, span):
        convolve(r0)

    two_away(1)

    @pl.when(ctx > 0)
    def _():
        settle(htop_ref, halo_recv.at[1])

    @pl.when(ctx < 3)
    def _():
        settle(hbot_ref, halo_recv.at[0])

    gf_ref[0:half] = htop_ref[...].astype(F32)
    gf_ref[half + rows :] = hbot_ref[...].astype(F32)
    convolve(0)
    convolve(rows - span)

    from_sibling(1)
    quarter = channels // 2
    closing = dot_nt(act_ref[:, :quarter], wfull_ref[0, :, channels:])
    closing = closing + dot_nt(act_ref[:, quarter:], wfull_ref[1, :, channels:])
    out_ref[...] = (after_ref[...].astype(F32) + closing).astype(BF)

    settle(send_ref.at[pl.ds(0, n_dp - 1)], a_send)
    settle(meta_ref.at[pl.ds(0, n_dp - 1)], m_send)
    for k in range(1, nz):
        settle(zbuf_ref.at[0], bz_send.at[k])
    for d in range(1, 4):
        settle(cbuf_ref.at[0], bc_send.at[d])
    for part in range(2):
        settle(piece(x, yh, part), by_send.at[part])
        for i in range(6):
            settle(piece(x, yh, part), bx_send.at[part, i])
        for i in range(NX * NY):
            settle(piece(x, yh, part), sib_send.at[part, i])
    for i in range(4):
        for j in range(3):
            settle(kv_part(ctx, i), kv_send.at[i, j])

    @pl.when(ctx > 0)
    def _():
        settle(head_rows, halo_send.at[0])

    @pl.when(ctx < 3)
    def _():
        settle(tail_rows, halo_send.at[1])


def solution(mesh):
    n_dp = mesh.shape["dp"]
    n_ctx = mesh.shape["ctx"]
    nz = n_dp // (NX * NY)

    def per_device(
        frames,
        destinations,
        segments,
        tile_mask,
        attn_gain,
        w_qkv,
        w_out,
        conv_gain,
        w_pointin,
        w_pointout,
        w_depth,
        bn_scale,
        bn_shift,
    ):
        rows, width = frames.shape[1:]
        seq = segments.shape[1]
        channels = w_depth.shape[1]
        taps = w_depth.shape[0]
        head_cols = w_out.shape[0]
        cap = 2 * rows // n_dp
        shard_rows = w_pointin.shape[0]
        pad_rows = -(-shard_rows // 8) * 8
        half_cols = channels + channels // 2
        pick = np.zeros((nz * n_ctx * shard_rows, n_ctx * nz * pad_rows), np.float32)
        for a in range(nz):
            for b in range(n_ctx):
                for j in range(shard_rows):
                    pick[(a * n_ctx + b) * shard_rows + j, (b * nz + a) * pad_rows + j] = 1.0
        pick = jnp.asarray(pick, BF)
        vmem = pl.BlockSpec(memory_space=pltpu.VMEM)
        smem = pl.BlockSpec(memory_space=pltpu.SMEM)
        hbm = pl.BlockSpec(memory_space=pl.ANY)

        def body(*refs):
            layer_kernel(n_dp, shard_rows, *refs)

        dma = pltpu.SemaphoreType.DMA
        out = pl.pallas_call(
            body,
            name="conformer_layer",
            out_shape=jax.ShapeDtypeStruct((rows, width), BF),
            in_specs=[vmem, vmem, vmem, smem, vmem, hbm, hbm] + [vmem] * 7,
            out_specs=vmem,
            scratch_shapes=[
                pltpu.VMEM(w_qkv.shape, BF),
                pltpu.VMEM(w_out.shape, BF),
                pltpu.VMEM((n_dp, cap, width), BF),
                pltpu.VMEM((n_dp, cap, width), BF),
                pltpu.VMEM((n_dp, 1, 128), F32),
                pltpu.VMEM((n_dp, 1, 128), F32),
                pltpu.VMEM((HEADS // 2, rows, seq), BF),
                pltpu.VMEM((nz, pad_rows, 2 * half_cols), BF),
                pltpu.VMEM((n_ctx, nz, pad_rows, half_cols), BF),
                pltpu.VMEM((2, width, half_cols), BF),
                pltpu.VMEM((seq, 2 * head_cols), BF),
                pltpu.VMEM((rows, head_cols), BF),
                pltpu.VMEM((rows, head_cols), BF),
                pltpu.VMEM((rows, width), F32),
                pltpu.VMEM((rows, width), BF),
                pltpu.VMEM((rows, seq), F32),
                pltpu.VMEM((seq + taps, 128), F32),
                pltpu.VMEM((rows + taps, 128), F32),
                pltpu.VMEM((taps, rows, 128), F32),
                pltpu.VMEM((rows, channels), BF),
                pltpu.VMEM((taps // 2, channels), BF),
                pltpu.VMEM((taps // 2, channels), BF),
                pltpu.VMEM((rows + taps, channels), F32),
                pltpu.VMEM((rows, channels), BF),
                dma((2,)),
                dma,
                dma,
                dma,
                dma,
                dma((8,)),
                dma((8,)),
                dma((4,)),
                dma((4,)),
                dma((2,)),
                dma((2,)),
                dma((2, 6)),
                dma((2, 6)),
                dma((2, NX * NY)),
                dma((2, NX * NY)),
                dma((4, 3)),
                dma((4, 3)),
                dma((2,)),
                dma((2,)),
            ],
            compiler_params=pltpu.CompilerParams(
                collective_id=0, has_side_effects=True, vmem_limit_bytes=60 * 2**20
            ),
            cost_estimate=pl.CostEstimate(flops=6 * 10**9, bytes_accessed=20 * 10**6, transcendentals=3 * 10**6),
        )(
            destinations,
            frames[0],
            segments,
            tile_mask[0],
            attn_gain,
            w_qkv,
            w_out,
            conv_gain,
            w_pointin,
            w_pointout.T,
            pick,
            w_depth,
            bn_scale,
            bn_shift,
        )

        def hand_on(src_ref, dst_ref, sem):
            copies = []
            for i in range(4):
                part = pl.ds(i * (rows // 4), rows // 4)
                copies.append(pltpu.make_async_copy(src_ref.at[part], dst_ref.at[part], sem.at[i]))
                copies[i].start()
            for copy in copies:
                copy.wait()

        out = pl.pallas_call(
            hand_on,
            name="result",
            out_shape=jax.ShapeDtypeStruct((rows, width), BF),
            in_specs=[hbm],
            out_specs=hbm,
            scratch_shapes=[dma((4,))],
            compiler_params=pltpu.CompilerParams(vmem_limit_bytes=60 * 2**20),
        )(out)
        return out[None]

    return jax.shard_map(
        per_device,
        mesh=mesh,
        in_specs=(
            P("dp", "ctx", None),
            P("dp", "ctx"),
            P("dp", None),
            P("dp", "ctx", None),
            P(),
            P(),
            P(),
            P(),
            P(("dp", "ctx"), None),
            P(None, ("dp", "ctx")),
            P(),
            P(),
            P(),
        ),
        out_specs=P("dp", "ctx", None),
        check_vma=False,
    )
```

```python
import math

import numpy as np

import jax
import jax.numpy as jnp
from jax import lax
from jax.experimental import pallas as pl
from jax.experimental.pallas import tpu as pltpu
from jax.sharding import PartitionSpec as P

HEADS = 8
NX = 4
NY = 2
MESH = pl.DeviceIdType.MESH
BF = jnp.bfloat16
F32 = jnp.float32
MASKED = -2e38


def dot(a, b):
    return jnp.dot(a, b, preferred_element_type=F32)


def dot_nt(a, b):
    return lax.dot_general(a, b, (((1,), (1,)), ((), ())), preferred_element_type=F32)


def layer_norm(as_float, gain):
    row_mean = jnp.mean(as_float, axis=-1, keepdims=True)
    centred = as_float - row_mean
    row_var = jnp.mean(centred * centred, axis=-1, keepdims=True)
    return centred * lax.rsqrt(row_var + 1e-06) * gain


def layer_kernel(
    n_dp,
    shard_rows,
    dest_ref,
    frames_ref,
    seg_ref,
    tile_ref,
    again_ref,
    wqkv_hbm,
    wout_hbm,
    cgain_ref,
    pin_ref,
    pout_ref,
    pick_ref,
    wdepth_ref,
    bns_ref,
    bnb_ref,
    out_ref,
    wqkv_ref,
    wout_ref,
    send_ref,
    got_ref,
    meta_ref,
    gmeta_ref,
    prob_ref,
    zbuf_ref,
    cbuf_ref,
    wfull_ref,
    kv_ref,
    q_ref,
    att_ref,
    placed_ref,
    after_ref,
    bias_ref,
    segc_ref,
    segn_ref,
    mask_ref,
    gat_ref,
    htop_ref,
    hbot_ref,
    gf_ref,
    act_ref,
    load_sem,
    a_send,
    a_recv,
    m_send,
    m_recv,
    bz_send,
    bz_recv,
    by_send,
    by_recv,
    bx_send,
    bx_recv,
    sib_send,
    sib_recv,
    kv_send,
    kv_recv,
    halo_send,
    halo_recv,
):
    rows, width = frames_ref.shape
    seq = seg_ref.shape[1]
    nz = n_dp // (NX * NY)
    cap = send_ref.shape[1]
    head_cols = wout_ref.shape[0]
    head = head_cols // HEADS
    group = head_cols // 2
    half_cols = cbuf_ref.shape[4]
    block = wfull_ref.shape[1] // (NX * NY)
    channels = wdepth_ref.shape[1]
    taps = wdepth_ref.shape[0]
    half = taps // 2
    tile = 128

    dp = lax.axis_index("dp")
    ctx = lax.axis_index("ctx")
    x = dp // (NY * nz)
    yh = (dp // nz) % NY
    z = dp % nz
    core = ctx % 2

    def dp_of(px, py, pz):
        return (px * NY + py) * nz + pz

    def peer(i):
        zi, rest = i // (NX * NY), NX * NY - 1 - i % (NX * NY)
        kz = nz // 2 + ((zi + 1) // 2) * (1 - 2 * (zi % 2))
        return dp_of((x + rest // NY) % NX, (yh + rest % NY) % NY, (z + kz + nz) % nz)

    def put(src, dst, ssem, rsem, d, c):
        copy = pltpu.make_async_remote_copy(
            src_ref=src, dst_ref=dst, send_sem=ssem, recv_sem=rsem, device_id=(d, c), device_id_type=MESH
        )
        copy.start()

    def settle(ref, sem):
        pltpu.make_async_copy(ref, ref, sem).wait()

    barrier = pltpu.get_barrier_semaphore()

    def greet(k, carry):
        pl.semaphore_signal(barrier, inc=1, device_id=(peer(k), ctx), device_id_type=MESH)
        return carry

    lax.fori_loop(0, n_dp - 1, greet, 0)
    for d in range(1, 4):
        pl.semaphore_signal(barrier, inc=1, device_id=(dp, ctx ^ d), device_id_type=MESH)
        pl.semaphore_signal(barrier, inc=1, device_id=(dp_of(x, 1 - yh, z), ctx ^ d), device_id_type=MESH)

    load_qkv = pltpu.make_async_copy(wqkv_hbm, wqkv_ref, load_sem.at[0])
    load_qkv.start()
    load_out = pltpu.make_async_copy(wout_hbm, wout_ref, load_sem.at[1])
    load_out.start()

    dest = dest_ref[...]
    owner = dest // rows
    slot = dest % rows
    oz = owner % nz
    oy = (owner // nz) % NY
    ox = owner // (nz * NY)
    dz = (oz - z + nz) % nz - nz // 2
    zi = jnp.where(dz >= 0, 2 * dz, -2 * dz - 1)
    rel = (zi + 1) * (NX * NY) - 1 - (((ox - x + NX) % NX) * NY + (oy - yh + NY) % NY)
    rel_wide = jnp.broadcast_to(rel.astype(F32), (rows, rows))
    rel_tall = jnp.transpose(rel_wide)
    earlier = lax.broadcasted_iota(jnp.int32, (rows, rows), 0) < lax.broadcasted_iota(jnp.int32, (rows, rows), 1)
    rank = jnp.sum(jnp.where((rel_tall == rel_wide) & earlier, 1.0, 0.0), axis=0, keepdims=True)
    pos = rel * cap + rank.astype(jnp.int32)
    frames = frames_ref[...]
    per = n_dp // 4

    def pack(c):
        chunk = lax.broadcasted_iota(jnp.int32, (per * cap, rows), 0) + c * per * cap
        onehot = jnp.where(chunk == pos, 1.0, 0.0).astype(BF)
        send_ref[c * per : (c + 1) * per] = dot(onehot, frames).reshape(per, cap, width).astype(BF)

    def ship(i, carry):
        put(send_ref.at[i], got_ref.at[i], a_send, a_recv, peer(i), ctx)
        put(meta_ref.at[i], gmeta_ref.at[i], m_send, m_recv, peer(i), ctx)
        return carry

    def piece(px, py, part):
        start = pl.multiple_of((((px + NX) % NX) * NY + py) * block, 16)
        cols = pl.ds(0, channels) if part == 0 else pl.ds(channels, half_cols - channels)
        return wfull_ref.at[core, pl.ds(start, block), cols]

    right = dp_of((x + 1) % NX, yh, z)
    left = dp_of((x + NX - 1) % NX, yh, z)
    other = 1 - yh

    def to_sibling(i, px, py, part):
        ref = piece(px, py, part)
        put(ref, ref, sib_send.at[part, i], sib_recv.at[part, i], dp, ctx ^ 1)

    def to_x(i, px, py, part, d):
        ref = piece(px, py, part)
        put(ref, ref, bx_send.at[part, i], bx_recv.at[part, i], d, ctx)

    def own_to_x(part):
        to_x(0, x, yh, part, right)
        to_x(1, x, yh, part, left)

    def pair_to_x(part):
        to_x(2, x, other, part, right)
        to_x(3, x, other, part, left)

    def hand_right(part):
        settle(piece(x - 1, yh, part), bx_recv.at[part, 0])
        settle(piece(x + 1, yh, part), bx_recv.at[part, 1])
        to_x(4, x - 1, yh, part, right)
        to_sibling(2, x - 1, yh, part)
        to_sibling(3, x + 1, yh, part)

    def hand_left(part):
        settle(piece(x - 1, other, part), bx_recv.at[part, 2])
        settle(piece(x + 1, other, part), bx_recv.at[part, 3])
        to_x(5, x + 1, other, part, left)
        to_sibling(4, x - 1, other, part)
        to_sibling(5, x + 1, other, part)

    def two_away(part):
        settle(piece(x + 2, yh, part), bx_recv.at[part, 4])
        to_sibling(6, x + 2, yh, part)
        settle(piece(x + 2, other, part), bx_recv.at[part, 5])
        to_sibling(7, x + 2, other, part)

    def from_sibling(part):
        for i in range(NX * NY):
            settle(piece(x, yh, part), sib_recv.at[part, i])

    zbuf_ref[pl.ds(z, 1)] = jnp.zeros((1,) + zbuf_ref.shape[1:], BF)
    for c in range(2):
        left_col = c * half_cols
        zbuf_ref[pl.ds(z, 1), :shard_rows, left_col : left_col + channels] = pin_ref[
            :, c * channels : (c + 1) * channels
        ][None]
        zbuf_ref[pl.ds(z, 1), :shard_rows, left_col + channels : left_col + half_cols] = pout_ref[
            :, c * (channels // 2) : (c + 1) * (channels // 2)
        ][None]
    pack(0)
    rank_tall = jnp.transpose(jnp.broadcast_to(rank, (tile, rows)))
    slot_tall = jnp.transpose(jnp.broadcast_to(slot.astype(F32) + 1.0, (tile, rows)))
    lane = lax.broadcasted_iota(jnp.int32, (rows, tile), 1).astype(F32)
    at_rank = jnp.where(rank_tall == lane, slot_tall, 0.0).astype(BF)
    to_peer = jnp.where(lax.broadcasted_iota(jnp.int32, (n_dp, rows), 0) == rel, 1.0, 0.0).astype(BF)
    meta_ref[...] = dot(to_peer, at_rank).reshape(n_dp, 1, tile)
    pl.semaphore_wait(barrier, n_dp - 1 + 6)
    for k in range(1, nz):
        put(zbuf_ref.at[z], zbuf_ref.at[z], bz_send.at[k], bz_recv.at[k], dp_of(x, yh, (z + k) % nz), ctx)
    lax.fori_loop(0, per, ship, 0)
    pack(1)
    pack(2)
    for k in range(1, nz):
        settle(zbuf_ref.at[0], bz_recv.at[k])
    for i in range(1, 2 * 4):
        d, far = i // 2, i % 2
        cols = pl.ds(pl.multiple_of(((ctx ^ d) % 2) * half_cols, 128), half_cols)
        to_yh = other if far else yh
        put(zbuf_ref.at[:, :, cols], cbuf_ref.at[yh, ctx], by_send.at[i], by_recv.at[i], dp_of(x, to_yh, z), ctx ^ d)
    lax.fori_loop(per, 3 * per, ship, 0)
    mine = pl.ds(pl.multiple_of(core * half_cols, 128), half_cols)
    cbuf_ref[yh, pl.ds(ctx, 1)] = zbuf_ref[:, :, mine][None]
    pack(3)
    for i in range(1, 2 * 4):
        settle(cbuf_ref.at[0, 0], by_recv.at[i])
    for y in range(NY):
        padded = cbuf_ref[y].astype(F32).reshape(pick_ref.shape[1], half_cols).astype(BF)
        start = pl.multiple_of((x * NY + y) * block, 16)
        wfull_ref[core, pl.ds(start, block)] = dot(pick_ref[...], padded).astype(BF)
    own_to_x(0)
    pair_to_x(0)
    lax.fori_loop(3 * per, n_dp - 1, ship, 0)
    own_to_x(1)
    pair_to_x(1)
    for part in range(2):
        to_sibling(0, x, yh, part)
        to_sibling(1, x, other, part)
    got_ref[n_dp - 1] = send_ref[n_dp - 1]
    gmeta_ref[n_dp - 1] = meta_ref[n_dp - 1]

    segf = seg_ref[...].astype(F32)
    segc_ref[0:half] = jnp.full((half, tile), -1.0, F32)
    segc_ref[half + seq :] = jnp.full((half, tile), -1.0, F32)
    segc_ref[half : half + seq] = jnp.transpose(jnp.broadcast_to(segf, (tile, seq)))
    first = pl.multiple_of(ctx * rows, rows)
    segn_ref[...] = segc_ref[pl.ds(first, rows + 2 * half)]
    own_seg = segn_ref[half : half + rows]
    for tk in range(seq // tile):
        same = own_seg == segf[:, tk * tile : (tk + 1) * tile]
        for tq in range(rows // tile):
            off = (1 - tile_ref[tq, tk]).astype(F32) * MASKED
            bias_ref[tq * tile : (tq + 1) * tile, tk * tile : (tk + 1) * tile] = jnp.where(
                same[tq * tile : (tq + 1) * tile], off, MASKED
            )
    for k in range(taps):
        mask_ref[k] = jnp.where(segn_ref[k : k + rows] == own_seg, 1.0, 0.0)

    settle(gmeta_ref.at[pl.ds(0, n_dp - 1)], m_recv)
    spots = n_dp * cap
    spot = lax.broadcasted_iota(jnp.int32, (tile, spots), 1)
    spread = jnp.where(lax.broadcasted_iota(jnp.int32, (tile, spots), 0) == spot % cap, 1.0, 0.0).astype(BF)
    spread = dot(gmeta_ref[...].reshape(n_dp, tile).astype(BF), spread)
    spot = lax.broadcasted_iota(jnp.int32, (n_dp, spots), 1)
    from_peer = lax.broadcasted_iota(jnp.int32, (n_dp, spots), 0) == spot // cap
    slots = jnp.sum(jnp.where(from_peer, spread, 0.0), axis=0, keepdims=True)
    lane = lax.broadcasted_iota(jnp.int32, (rows, spots), 0).astype(F32) + 1.0
    place = jnp.where(lane == slots, 1.0, 0.0).astype(BF)
    settle(got_ref.at[pl.ds(0, n_dp - 1)], a_recv)
    got = got_ref[...].astype(F32).reshape(spots, width).astype(BF)
    placed = dot(place, got)
    placed_ref[...] = placed
    normed = layer_norm(placed, again_ref[...][None]).astype(BF)

    load_qkv.wait()
    base = pl.multiple_of(ctx * rows, rows)
    keys = dot(normed, wqkv_ref[:, head_cols : 2 * head_cols]).astype(BF)
    values = dot(normed, wqkv_ref[:, 2 * head_cols :]).astype(BF)
    for g in range(2):
        kv_ref[pl.ds(base, rows), 2 * g * group : (2 * g + 1) * group] = keys[:, g * group : (g + 1) * group]
        kv_ref[pl.ds(base, rows), (2 * g + 1) * group : (2 * g + 2) * group] = values[:, g * group : (g + 1) * group]

    def kv_part(c, i):
        return kv_ref.at[pl.ds(pl.multiple_of(c * rows, rows), rows), pl.ds(i * group, group)]

    for i in range(4):
        part = kv_part(ctx, i)
        put(part, part, kv_send.at[i, 0], kv_recv.at[i, 0], dp, ctx ^ 2)
        put(part, part, kv_send.at[i, 1], kv_recv.at[i, 1], dp, ctx ^ 1)
    scale = math.log2(math.e) / math.sqrt(head)
    q_ref[...] = (dot(normed, wqkv_ref[:, :head_cols]) * scale).astype(BF)

    def arrive(i):
        part = kv_part(ctx ^ 2, i)
        settle(part, kv_recv.at[i, 0])
        put(part, part, kv_send.at[i, 2], kv_recv.at[i, 2], dp, ctx ^ 1)
        settle(part, kv_recv.at[i, 1])
        settle(part, kv_recv.at[i, 2])

    def windows(h):
        lo, hi = h * head, (h + 1) * head
        c0, c1 = lo // tile * tile, (hi + tile - 1) // tile * tile
        lanes = lax.broadcasted_iota(jnp.int32, (rows, c1 - c0), 1) + c0
        return c0, c1, (lanes >= lo) & (lanes < hi)

    def score(g):
        totals = []
        for h in range(HEADS // 2):
            c0, c1, inside = windows(h)
            query = q_ref[:, g * group + c0 : g * group + c1].astype(F32)
            query = jnp.where(inside, query, 0.0).astype(BF)
            scores = dot_nt(query, kv_ref[:, 2 * g * group + c0 : 2 * g * group + c1]) + bias_ref[...]
            weights = jnp.exp2(scores - jnp.max(scores, axis=1, keepdims=True))
            totals.append(jnp.sum(weights, axis=1, keepdims=True))
            prob_ref[h] = weights.astype(BF)
        return totals

    def mix(g, totals):
        tiles = [None] * (group // tile)
        for h in range(HEADS // 2):
            c0, c1, inside = windows(h)
            mixed = dot(prob_ref[h], kv_ref[:, (2 * g + 1) * group + c0 : (2 * g + 1) * group + c1])
            mixed = jnp.where(inside, mixed / totals[h], 0.0)
            for t in range(c0 // tile, c1 // tile):
                term = mixed[:, t * tile - c0 : (t + 1) * tile - c0]
                tiles[t] = term if tiles[t] is None else tiles[t] + term
        for t, whole in enumerate(tiles):
            att_ref[:, g * group + t * tile : g * group + (t + 1) * tile] = whole.astype(BF)

    hand_right(0)
    arrive(0)
    totals = score(0)
    hand_left(0)
    arrive(1)
    mix(0, totals)
    arrive(2)
    totals = score(1)
    hand_right(1)
    arrive(3)
    mix(1, totals)

    load_out.wait()
    after = (placed_ref[...] + dot(att_ref[...], wout_ref[...])).astype(BF)
    after_ref[...] = after
    conv_normed = layer_norm(after.astype(F32), cgain_ref[...][None]).astype(BF)

    two_away(0)
    hand_left(1)
    from_sibling(0)

    gate = jax.nn.sigmoid(dot(conv_normed, wfull_ref[1, :, :channels]))
    gated = (dot(conv_normed, wfull_ref[0, :, :channels]) * gate).astype(BF)
    gat_ref[...] = gated
    gf_ref[half : half + rows] = gated.astype(F32)

    head_rows = gat_ref.at[0:half]
    tail_rows = gat_ref.at[rows - half : rows]

    @pl.when(ctx > 0)
    def _():
        put(head_rows, hbot_ref, halo_send.at[0], halo_recv.at[0], dp, ctx - 1)

    @pl.when(ctx < 3)
    def _():
        put(tail_rows, htop_ref, halo_send.at[1], halo_recv.at[1], dp, ctx + 1)

    @pl.when(ctx == 0)
    def _():
        htop_ref[...] = jnp.zeros_like(htop_ref)

    @pl.when(ctx == 3)
    def _():
        hbot_ref[...] = jnp.zeros_like(hbot_ref)

    span = 64

    def convolve(r0):
        def body(t, carry):
            lanes = pl.ds(pl.multiple_of(t * tile, tile), tile)
            near = gf_ref[r0 : r0 + span + 2 * half, lanes]
            total = jnp.zeros((span, tile), F32)
            for b in range(8):
                shifted = near if b == 0 else pltpu.roll(near, span + 2 * half - b, 0)
                for a in range(taps // 8):
                    k = 8 * a + b
                    term = shifted[8 * a : 8 * a + span] * mask_ref[k, r0 : r0 + span]
                    total = total + term * wdepth_ref[k : k + 1, lanes]
            moved = total * bns_ref[lanes][None] + bnb_ref[lanes][None]
            act_ref[r0 : r0 + span, lanes] = (moved * jax.nn.sigmoid(moved)).astype(BF)
            return carry

        lax.fori_loop(0, channels // tile, body, 0)

    for r0 in range(span, rows - span, span):
        convolve(r0)

    two_away(1)

    @pl.when(ctx > 0)
    def _():
        settle(htop_ref, halo_recv.at[1])

    @pl.when(ctx < 3)
    def _():
        settle(hbot_ref, halo_recv.at[0])

    gf_ref[0:half] = htop_ref[...].astype(F32)
    gf_ref[half + rows :] = hbot_ref[...].astype(F32)
    convolve(0)
    convolve(rows - span)

    from_sibling(1)
    quarter = channels // 2
    closing = dot_nt(act_ref[:, :quarter], wfull_ref[0, :, channels:])
    closing = closing + dot_nt(act_ref[:, quarter:], wfull_ref[1, :, channels:])
    out_ref[...] = (after_ref[...].astype(F32) + closing).astype(BF)

    settle(send_ref.at[pl.ds(0, n_dp - 1)], a_send)
    settle(meta_ref.at[pl.ds(0, n_dp - 1)], m_send)
    for k in range(1, nz):
        settle(zbuf_ref.at[0], bz_send.at[k])
    for i in range(1, 2 * 4):
        settle(cbuf_ref.at[0, 0], by_send.at[i])
    for part in range(2):
        for i in range(6):
            settle(piece(x, yh, part), bx_send.at[part, i])
        for i in range(NX * NY):
            settle(piece(x, yh, part), sib_send.at[part, i])
    for i in range(4):
        for j in range(3):
            settle(kv_part(ctx, i), kv_send.at[i, j])

    @pl.when(ctx > 0)
    def _():
        settle(head_rows, halo_send.at[0])

    @pl.when(ctx < 3)
    def _():
        settle(tail_rows, halo_send.at[1])


def solution(mesh):
    n_dp = mesh.shape["dp"]
    n_ctx = mesh.shape["ctx"]
    nz = n_dp // (NX * NY)

    def per_device(
        frames,
        destinations,
        segments,
        tile_mask,
        attn_gain,
        w_qkv,
        w_out,
        conv_gain,
        w_pointin,
        w_pointout,
        w_depth,
        bn_scale,
        bn_shift,
    ):
        rows, width = frames.shape[1:]
        seq = segments.shape[1]
        channels = w_depth.shape[1]
        taps = w_depth.shape[0]
        head_cols = w_out.shape[0]
        cap = 2 * rows // n_dp
        shard_rows = w_pointin.shape[0]
        pad_rows = -(-shard_rows // 8) * 8
        half_cols = channels + channels // 2
        pick = np.zeros((nz * n_ctx * shard_rows, n_ctx * nz * pad_rows), np.float32)
        for a in range(nz):
            for b in range(n_ctx):
                for j in range(shard_rows):
                    pick[(a * n_ctx + b) * shard_rows + j, (b * nz + a) * pad_rows + j] = 1.0
        pick = jnp.asarray(pick, BF)
        vmem = pl.BlockSpec(memory_space=pltpu.VMEM)
        smem = pl.BlockSpec(memory_space=pltpu.SMEM)
        hbm = pl.BlockSpec(memory_space=pl.ANY)

        def body(*refs):
            layer_kernel(n_dp, shard_rows, *refs)

        dma = pltpu.SemaphoreType.DMA
        out = pl.pallas_call(
            body,
            name="conformer_layer",
            out_shape=jax.ShapeDtypeStruct((rows, width), BF),
            in_specs=[vmem, vmem, vmem, smem, vmem, hbm, hbm] + [vmem] * 7,
            out_specs=vmem,
            scratch_shapes=[
                pltpu.VMEM(w_qkv.shape, BF),
                pltpu.VMEM(w_out.shape, BF),
                pltpu.VMEM((n_dp, cap, width), BF),
                pltpu.VMEM((n_dp, cap, width), BF),
                pltpu.VMEM((n_dp, 1, 128), F32),
                pltpu.VMEM((n_dp, 1, 128), F32),
                pltpu.VMEM((HEADS // 2, rows, seq), BF),
                pltpu.VMEM((nz, pad_rows, 2 * half_cols), BF),
                pltpu.VMEM((NY, n_ctx, nz, pad_rows, half_cols), BF),
                pltpu.VMEM((2, width, half_cols), BF),
                pltpu.VMEM((seq, 2 * head_cols), BF),
                pltpu.VMEM((rows, head_cols), BF),
                pltpu.VMEM((rows, head_cols), BF),
                pltpu.VMEM((rows, width), F32),
                pltpu.VMEM((rows, width), BF),
                pltpu.VMEM((rows, seq), F32),
                pltpu.VMEM((seq + taps, 128), F32),
                pltpu.VMEM((rows + taps, 128), F32),
                pltpu.VMEM((taps, rows, 128), F32),
                pltpu.VMEM((rows, channels), BF),
                pltpu.VMEM((taps // 2, channels), BF),
                pltpu.VMEM((taps // 2, channels), BF),
                pltpu.VMEM((rows + taps, channels), F32),
                pltpu.VMEM((rows, channels), BF),
                dma((2,)),
                dma,
                dma,
                dma,
                dma,
                dma((8,)),
                dma((8,)),
                dma((8,)),
                dma((8,)),
                dma((2, 6)),
                dma((2, 6)),
                dma((2, NX * NY)),
                dma((2, NX * NY)),
                dma((4, 3)),
                dma((4, 3)),
                dma((2,)),
                dma((2,)),
            ],
            compiler_params=pltpu.CompilerParams(
                collective_id=0, has_side_effects=True, vmem_limit_bytes=48 * 2**20
            ),
            cost_estimate=pl.CostEstimate(flops=6 * 10**9, bytes_accessed=20 * 10**6, transcendentals=3 * 10**6),
        )(
            destinations,
            frames[0],
            segments,
            tile_mask[0],
            attn_gain,
            w_qkv,
            w_out,
            conv_gain,
            w_pointin,
            w_pointout.T,
            pick,
            w_depth,
            bn_scale,
            bn_shift,
        )

        def hand_on(src_ref, dst_ref, sem):
            copies = []
            for i in range(4):
                part = pl.ds(i * (rows // 4), rows // 4)
                copies.append(pltpu.make_async_copy(src_ref.at[part], dst_ref.at[part], sem.at[i]))
                copies[i].start()
            for copy in copies:
                copy.wait()

        out = pl.pallas_call(
            hand_on,
            name="result",
            out_shape=jax.ShapeDtypeStruct((rows, width), BF),
            in_specs=[hbm],
            out_specs=hbm,
            scratch_shapes=[dma((4,))],
            compiler_params=pltpu.CompilerParams(vmem_limit_bytes=2**20),
        )(out)
        return out[None]

    return jax.shard_map(
        per_device,
        mesh=mesh,
        in_specs=(
            P("dp", "ctx", None),
            P("dp", "ctx"),
            P("dp", None),
            P("dp", "ctx", None),
            P(),
            P(),
            P(),
            P(),
            P(("dp", "ctx"), None),
            P(None, ("dp", "ctx")),
            P(),
            P(),
            P(),
        ),
        out_specs=P("dp", "ctx", None),
        check_vma=False,
    )
```

```python
import math

import numpy as np

import jax
import jax.numpy as jnp
from jax import lax
from jax.experimental import pallas as pl
from jax.experimental.pallas import tpu as pltpu
from jax.sharding import PartitionSpec as P

HEADS = 8
NX = 4
NY = 2
MESH = pl.DeviceIdType.MESH
BF = jnp.bfloat16
F32 = jnp.float32
MASKED = -2e38


def dot(a, b):
    return jnp.dot(a, b, preferred_element_type=F32)


def dot_nt(a, b):
    return lax.dot_general(a, b, (((1,), (1,)), ((), ())), preferred_element_type=F32)


def layer_norm(as_float, gain):
    row_mean = jnp.mean(as_float, axis=-1, keepdims=True)
    centred = as_float - row_mean
    row_var = jnp.mean(centred * centred, axis=-1, keepdims=True)
    return centred * lax.rsqrt(row_var + 1e-06) * gain


def layer_kernel(
    n_dp,
    shard_rows,
    fetches,
    dest_ref,
    frames_ref,
    seg_ref,
    tile_ref,
    again_ref,
    wqkv_hbm,
    wout_hbm,
    cgain_ref,
    pin_ref,
    pout_ref,
    pick_ref,
    wdepth_ref,
    bns_ref,
    bnb_ref,
    out_ref,
    wqkv_ref,
    wout_ref,
    send_ref,
    got_ref,
    meta_ref,
    gmeta_ref,
    prob_ref,
    zbuf_ref,
    cbuf_ref,
    wfull_ref,
    kv_ref,
    q_ref,
    att_ref,
    placed_ref,
    after_ref,
    bias_ref,
    segc_ref,
    segn_ref,
    mask_ref,
    gat_ref,
    htop_ref,
    hbot_ref,
    gf_ref,
    act_ref,
    load_sem,
    a_send,
    a_recv,
    m_send,
    m_recv,
    bz_send,
    bz_recv,
    by_send,
    by_recv,
    bx_send,
    bx_recv,
    sib_send,
    sib_recv,
    kv_send,
    kv_recv,
    halo_send,
    halo_recv,
):
    rows, width = frames_ref.shape
    seq = seg_ref.shape[1]
    nz = n_dp // (NX * NY)
    cap = send_ref.shape[1]
    head_cols = wout_ref.shape[0]
    head = head_cols // HEADS
    group = head_cols // 2
    half_cols = cbuf_ref.shape[4]
    block = wfull_ref.shape[1] // (NX * NY)
    channels = wdepth_ref.shape[1]
    taps = wdepth_ref.shape[0]
    half = taps // 2
    tile = 128

    dp = lax.axis_index("dp")
    ctx = lax.axis_index("ctx")
    x = dp // (NY * nz)
    yh = (dp // nz) % NY
    z = dp % nz
    core = ctx % 2

    def dp_of(px, py, pz):
        return (px * NY + py) * nz + pz

    def peer(i):
        zi, rest = i // (NX * NY), NX * NY - 1 - i % (NX * NY)
        kz = nz // 2 + ((zi + 1) // 2) * (1 - 2 * (zi % 2))
        return dp_of((x + rest // NY) % NX, (yh + rest % NY) % NY, (z + kz + nz) % nz)

    def put(src, dst, ssem, rsem, d, c):
        copy = pltpu.make_async_remote_copy(
            src_ref=src, dst_ref=dst, send_sem=ssem, recv_sem=rsem, device_id=(d, c), device_id_type=MESH
        )
        copy.start()

    def settle(ref, sem):
        pltpu.make_async_copy(ref, ref, sem).wait()

    barrier = pltpu.get_barrier_semaphore()

    def greet(k, carry):
        pl.semaphore_signal(barrier, inc=1, device_id=(peer(k), ctx), device_id_type=MESH)
        return carry

    lax.fori_loop(0, n_dp - 1, greet, 0)
    for d in range(1, 4):
        pl.semaphore_signal(barrier, inc=1, device_id=(dp, ctx ^ d), device_id_type=MESH)
        pl.semaphore_signal(barrier, inc=1, device_id=(dp_of(x, 1 - yh, z), ctx ^ d), device_id_type=MESH)

    load_qkv = pltpu.make_async_copy(wqkv_hbm, wqkv_ref, load_sem.at[0])
    load_qkv.start()
    load_out = pltpu.make_async_copy(wout_hbm, wout_ref, load_sem.at[1])
    load_out.start()

    for fetch in fetches:
        fetch.wait()

    dest = dest_ref[...]
    owner = dest // rows
    slot = dest % rows
    oz = owner % nz
    oy = (owner // nz) % NY
    ox = owner // (nz * NY)
    dz = (oz - z + nz) % nz - nz // 2
    zi = jnp.where(dz >= 0, 2 * dz, -2 * dz - 1)
    rel = (zi + 1) * (NX * NY) - 1 - (((ox - x + NX) % NX) * NY + (oy - yh + NY) % NY)
    rel_wide = jnp.broadcast_to(rel.astype(F32), (rows, rows))
    rel_tall = jnp.transpose(rel_wide)
    earlier = lax.broadcasted_iota(jnp.int32, (rows, rows), 0) < lax.broadcasted_iota(jnp.int32, (rows, rows), 1)
    rank = jnp.sum(jnp.where((rel_tall == rel_wide) & earlier, 1.0, 0.0), axis=0, keepdims=True)
    pos = rel * cap + rank.astype(jnp.int32)
    frames = frames_ref[...]
    per = n_dp // 4

    def pack(c):
        chunk = lax.broadcasted_iota(jnp.int32, (per * cap, rows), 0) + c * per * cap
        onehot = jnp.where(chunk == pos, 1.0, 0.0).astype(BF)
        send_ref[c * per : (c + 1) * per] = dot(onehot, frames).reshape(per, cap, width).astype(BF)

    def ship(i, carry):
        put(send_ref.at[i], got_ref.at[i], a_send, a_recv, peer(i), ctx)
        put(meta_ref.at[i], gmeta_ref.at[i], m_send, m_recv, peer(i), ctx)
        return carry

    def piece(px, py, part):
        start = pl.multiple_of((((px + NX) % NX) * NY + py) * block, 16)
        cols = pl.ds(0, channels) if part == 0 else pl.ds(channels, half_cols - channels)
        return wfull_ref.at[core, pl.ds(start, block), cols]

    right = dp_of((x + 1) % NX, yh, z)
    left = dp_of((x + NX - 1) % NX, yh, z)
    other = 1 - yh

    def to_sibling(i, px, py, part):
        ref = piece(px, py, part)
        put(ref, ref, sib_send.at[part, i], sib_recv.at[part, i], dp, ctx ^ 1)

    def to_x(i, px, py, part, d):
        ref = piece(px, py, part)
        put(ref, ref, bx_send.at[part, i], bx_recv.at[part, i], d, ctx)

    def own_to_x(part):
        to_x(0, x, yh, part, right)
        to_x(1, x, yh, part, left)

    def pair_to_x(part):
        to_x(2, x, other, part, right)
        to_x(3, x, other, part, left)

    def hand_right(part):
        settle(piece(x - 1, yh, part), bx_recv.at[part, 0])
        settle(piece(x + 1, yh, part), bx_recv.at[part, 1])
        to_x(4, x - 1, yh, part, right)
        to_sibling(2, x - 1, yh, part)
        to_sibling(3, x + 1, yh, part)

    def hand_left(part):
        settle(piece(x - 1, other, part), bx_recv.at[part, 2])
        settle(piece(x + 1, other, part), bx_recv.at[part, 3])
        to_x(5, x + 1, other, part, left)
        to_sibling(4, x - 1, other, part)
        to_sibling(5, x + 1, other, part)

    def two_away(part):
        settle(piece(x + 2, yh, part), bx_recv.at[part, 4])
        to_sibling(6, x + 2, yh, part)
        settle(piece(x + 2, other, part), bx_recv.at[part, 5])
        to_sibling(7, x + 2, other, part)

    def from_sibling(part):
        for i in range(NX * NY):
            settle(piece(x, yh, part), sib_recv.at[part, i])

    zbuf_ref[pl.ds(z, 1)] = jnp.zeros((1,) + zbuf_ref.shape[1:], BF)
    for c in range(2):
        left_col = c * half_cols
        zbuf_ref[pl.ds(z, 1), :shard_rows, left_col : left_col + channels] = pin_ref[
            :, c * channels : (c + 1) * channels
        ][None]
        zbuf_ref[pl.ds(z, 1), :shard_rows, left_col + channels : left_col + half_cols] = pout_ref[
            :, c * (channels // 2) : (c + 1) * (channels // 2)
        ][None]
    pack(0)
    rank_tall = jnp.transpose(jnp.broadcast_to(rank, (tile, rows)))
    slot_tall = jnp.transpose(jnp.broadcast_to(slot.astype(F32) + 1.0, (tile, rows)))
    lane = lax.broadcasted_iota(jnp.int32, (rows, tile), 1).astype(F32)
    at_rank = jnp.where(rank_tall == lane, slot_tall, 0.0).astype(BF)
    to_peer = jnp.where(lax.broadcasted_iota(jnp.int32, (n_dp, rows), 0) == rel, 1.0, 0.0).astype(BF)
    meta_ref[...] = dot(to_peer, at_rank).reshape(n_dp, 1, tile)
    pl.semaphore_wait(barrier, n_dp - 1 + 6)
    for k in range(1, nz):
        put(zbuf_ref.at[z], zbuf_ref.at[z], bz_send.at[k], bz_recv.at[k], dp_of(x, yh, (z + k) % nz), ctx)
    lax.fori_loop(0, per, ship, 0)
    pack(1)
    pack(2)
    for k in range(1, nz):
        settle(zbuf_ref.at[0], bz_recv.at[k])
    for i in range(1, 2 * 4):
        d, far = i // 2, i % 2
        cols = pl.ds(pl.multiple_of(((ctx ^ d) % 2) * half_cols, 128), half_cols)
        to_yh = other if far else yh
        put(zbuf_ref.at[:, :, cols], cbuf_ref.at[yh, ctx], by_send.at[i], by_recv.at[i], dp_of(x, to_yh, z), ctx ^ d)
    lax.fori_loop(per, 3 * per, ship, 0)
    mine = pl.ds(pl.multiple_of(core * half_cols, 128), half_cols)
    cbuf_ref[yh, pl.ds(ctx, 1)] = zbuf_ref[:, :, mine][None]
    pack(3)
    for i in range(1, 2 * 4):
        settle(cbuf_ref.at[0, 0], by_recv.at[i])
    for y in range(NY):
        padded = cbuf_ref[y].astype(F32).reshape(pick_ref.shape[1], half_cols).astype(BF)
        start = pl.multiple_of((x * NY + y) * block, 16)
        wfull_ref[core, pl.ds(start, block)] = dot(pick_ref[...], padded).astype(BF)
    own_to_x(0)
    pair_to_x(0)
    lax.fori_loop(3 * per, n_dp - 1, ship, 0)
    own_to_x(1)
    pair_to_x(1)
    for part in range(2):
        to_sibling(0, x, yh, part)
        to_sibling(1, x, other, part)
    got_ref[n_dp - 1] = send_ref[n_dp - 1]
    gmeta_ref[n_dp - 1] = meta_ref[n_dp - 1]

    segf = seg_ref[...].astype(F32)
    segc_ref[0:half] = jnp.full((half, tile), -1.0, F32)
    segc_ref[half + seq :] = jnp.full((half, tile), -1.0, F32)
    segc_ref[half : half + seq] = jnp.transpose(jnp.broadcast_to(segf, (tile, seq)))
    first = pl.multiple_of(ctx * rows, rows)
    segn_ref[...] = segc_ref[pl.ds(first, rows + 2 * half)]
    own_seg = segn_ref[half : half + rows]
    for tk in range(seq // tile):
        same = own_seg == segf[:, tk * tile : (tk + 1) * tile]
        for tq in range(rows // tile):
            off = (1 - tile_ref[tq, tk]).astype(F32) * MASKED
            bias_ref[tq * tile : (tq + 1) * tile, tk * tile : (tk + 1) * tile] = jnp.where(
                same[tq * tile : (tq + 1) * tile], off, MASKED
            )
    for k in range(taps):
        mask_ref[k] = jnp.where(segn_ref[k : k + rows] == own_seg, 1.0, 0.0)

    settle(gmeta_ref.at[pl.ds(0, n_dp - 1)], m_recv)
    spots = n_dp * cap
    spot = lax.broadcasted_iota(jnp.int32, (tile, spots), 1)
    spread = jnp.where(lax.broadcasted_iota(jnp.int32, (tile, spots), 0) == spot % cap, 1.0, 0.0).astype(BF)
    spread = dot(gmeta_ref[...].reshape(n_dp, tile).astype(BF), spread)
    spot = lax.broadcasted_iota(jnp.int32, (n_dp, spots), 1)
    from_peer = lax.broadcasted_iota(jnp.int32, (n_dp, spots), 0) == spot // cap
    slots = jnp.sum(jnp.where(from_peer, spread, 0.0), axis=0, keepdims=True)
    lane = lax.broadcasted_iota(jnp.int32, (rows, spots), 0).astype(F32) + 1.0
    place = jnp.where(lane == slots, 1.0, 0.0).astype(BF)
    settle(got_ref.at[pl.ds(0, n_dp - 1)], a_recv)
    got = got_ref[...].astype(F32).reshape(spots, width).astype(BF)
    placed = dot(place, got)
    placed_ref[...] = placed
    normed = layer_norm(placed, again_ref[...][None]).astype(BF)

    load_qkv.wait()
    base = pl.multiple_of(ctx * rows, rows)
    keys = dot(normed, wqkv_ref[:, head_cols : 2 * head_cols]).astype(BF)
    values = dot(normed, wqkv_ref[:, 2 * head_cols :]).astype(BF)
    for g in range(2):
        kv_ref[pl.ds(base, rows), 2 * g * group : (2 * g + 1) * group] = keys[:, g * group : (g + 1) * group]
        kv_ref[pl.ds(base, rows), (2 * g + 1) * group : (2 * g + 2) * group] = values[:, g * group : (g + 1) * group]

    def kv_part(c, i):
        return kv_ref.at[pl.ds(pl.multiple_of(c * rows, rows), rows), pl.ds(i * group, group)]

    for i in range(4):
        part = kv_part(ctx, i)
        put(part, part, kv_send.at[i, 0], kv_recv.at[i, 0], dp, ctx ^ 2)
        put(part, part, kv_send.at[i, 1], kv_recv.at[i, 1], dp, ctx ^ 1)
    scale = math.log2(math.e) / math.sqrt(head)
    q_ref[...] = (dot(normed, wqkv_ref[:, :head_cols]) * scale).astype(BF)

    def arrive(i):
        part = kv_part(ctx ^ 2, i)
        settle(part, kv_recv.at[i, 0])
        put(part, part, kv_send.at[i, 2], kv_recv.at[i, 2], dp, ctx ^ 1)
        settle(part, kv_recv.at[i, 1])
        settle(part, kv_recv.at[i, 2])

    def windows(h):
        lo, hi = h * head, (h + 1) * head
        c0, c1 = lo // tile * tile, (hi + tile - 1) // tile * tile
        lanes = lax.broadcasted_iota(jnp.int32, (rows, c1 - c0), 1) + c0
        return c0, c1, (lanes >= lo) & (lanes < hi)

    def score(g):
        totals = []
        for h in range(HEADS // 2):
            c0, c1, inside = windows(h)
            query = q_ref[:, g * group + c0 : g * group + c1].astype(F32)
            query = jnp.where(inside, query, 0.0).astype(BF)
            scores = dot_nt(query, kv_ref[:, 2 * g * group + c0 : 2 * g * group + c1]) + bias_ref[...]
            weights = jnp.exp2(scores - jnp.max(scores, axis=1, keepdims=True))
            totals.append(jnp.sum(weights, axis=1, keepdims=True))
            prob_ref[h] = weights.astype(BF)
        return totals

    def mix(g, totals):
        tiles = [None] * (group // tile)
        for h in range(HEADS // 2):
            c0, c1, inside = windows(h)
            mixed = dot(prob_ref[h], kv_ref[:, (2 * g + 1) * group + c0 : (2 * g + 1) * group + c1])
            mixed = jnp.where(inside, mixed / totals[h], 0.0)
            for t in range(c0 // tile, c1 // tile):
                term = mixed[:, t * tile - c0 : (t + 1) * tile - c0]
                tiles[t] = term if tiles[t] is None else tiles[t] + term
        for t, whole in enumerate(tiles):
            att_ref[:, g * group + t * tile : g * group + (t + 1) * tile] = whole.astype(BF)

    hand_right(0)
    arrive(0)
    totals = score(0)
    hand_left(0)
    arrive(1)
    mix(0, totals)
    arrive(2)
    totals = score(1)
    hand_right(1)
    arrive(3)
    mix(1, totals)

    load_out.wait()
    after = (placed_ref[...] + dot(att_ref[...], wout_ref[...])).astype(BF)
    after_ref[...] = after
    conv_normed = layer_norm(after.astype(F32), cgain_ref[...][None]).astype(BF)

    two_away(0)
    hand_left(1)
    from_sibling(0)

    gate = jax.nn.sigmoid(dot(conv_normed, wfull_ref[1, :, :channels]))
    gated = (dot(conv_normed, wfull_ref[0, :, :channels]) * gate).astype(BF)
    gat_ref[...] = gated
    gf_ref[half : half + rows] = gated.astype(F32)

    head_rows = gat_ref.at[0:half]
    tail_rows = gat_ref.at[rows - half : rows]

    @pl.when(ctx > 0)
    def _():
        put(head_rows, hbot_ref, halo_send.at[0], halo_recv.at[0], dp, ctx - 1)

    @pl.when(ctx < 3)
    def _():
        put(tail_rows, htop_ref, halo_send.at[1], halo_recv.at[1], dp, ctx + 1)

    @pl.when(ctx == 0)
    def _():
        htop_ref[...] = jnp.zeros_like(htop_ref)

    @pl.when(ctx == 3)
    def _():
        hbot_ref[...] = jnp.zeros_like(hbot_ref)

    span = 64

    def convolve(r0):
        def body(t, carry):
            lanes = pl.ds(pl.multiple_of(t * tile, tile), tile)
            near = gf_ref[r0 : r0 + span + 2 * half, lanes]
            total = jnp.zeros((span, tile), F32)
            for b in range(8):
                shifted = near if b == 0 else pltpu.roll(near, span + 2 * half - b, 0)
                for a in range(taps // 8):
                    k = 8 * a + b
                    term = shifted[8 * a : 8 * a + span] * mask_ref[k, r0 : r0 + span]
                    total = total + term * wdepth_ref[k : k + 1, lanes]
            moved = total * bns_ref[lanes][None] + bnb_ref[lanes][None]
            act_ref[r0 : r0 + span, lanes] = (moved * jax.nn.sigmoid(moved)).astype(BF)
            return carry

        lax.fori_loop(0, channels // tile, body, 0)

    for r0 in range(span, rows - span, span):
        convolve(r0)

    two_away(1)

    @pl.when(ctx > 0)
    def _():
        settle(htop_ref, halo_recv.at[1])

    @pl.when(ctx < 3)
    def _():
        settle(hbot_ref, halo_recv.at[0])

    gf_ref[0:half] = htop_ref[...].astype(F32)
    gf_ref[half + rows :] = hbot_ref[...].astype(F32)
    convolve(0)
    convolve(rows - span)

    from_sibling(1)
    quarter = channels // 2
    closing = dot_nt(act_ref[:, :quarter], wfull_ref[0, :, channels:])
    closing = closing + dot_nt(act_ref[:, quarter:], wfull_ref[1, :, channels:])
    out_ref[...] = (after_ref[...].astype(F32) + closing).astype(BF)

    settle(send_ref.at[pl.ds(0, n_dp - 1)], a_send)
    settle(meta_ref.at[pl.ds(0, n_dp - 1)], m_send)
    for k in range(1, nz):
        settle(zbuf_ref.at[0], bz_send.at[k])
    for i in range(1, 2 * 4):
        settle(cbuf_ref.at[0, 0], by_send.at[i])
    for part in range(2):
        for i in range(6):
            settle(piece(x, yh, part), bx_send.at[part, i])
        for i in range(NX * NY):
            settle(piece(x, yh, part), sib_send.at[part, i])
    for i in range(4):
        for j in range(3):
            settle(kv_part(ctx, i), kv_send.at[i, j])

    @pl.when(ctx > 0)
    def _():
        settle(head_rows, halo_send.at[0])

    @pl.when(ctx < 3)
    def _():
        settle(tail_rows, halo_send.at[1])


def solution(mesh):
    n_dp = mesh.shape["dp"]
    n_ctx = mesh.shape["ctx"]
    nz = n_dp // (NX * NY)

    def per_device(
        frames,
        destinations,
        segments,
        tile_mask,
        attn_gain,
        w_qkv,
        w_out,
        conv_gain,
        w_pointin,
        w_pointout,
        w_depth,
        bn_scale,
        bn_shift,
    ):
        rows, width = frames.shape[1:]
        seq = segments.shape[1]
        channels = w_depth.shape[1]
        taps = w_depth.shape[0]
        head_cols = w_out.shape[0]
        cap = 2 * rows // n_dp
        shard_rows = w_pointin.shape[0]
        pad_rows = -(-shard_rows // 8) * 8
        half_cols = channels + channels // 2
        pick = np.zeros((nz * n_ctx * shard_rows, n_ctx * nz * pad_rows), np.float32)
        for a in range(nz):
            for b in range(n_ctx):
                for j in range(shard_rows):
                    pick[(a * n_ctx + b) * shard_rows + j, (b * nz + a) * pad_rows + j] = 1.0
        pick = jnp.asarray(pick, BF)
        vmem = pl.BlockSpec(memory_space=pltpu.VMEM)
        hbm = pl.BlockSpec(memory_space=pltpu.HBM)
        operands = (
            destinations,
            frames[0],
            segments,
            tile_mask[0],
            attn_gain,
            w_qkv,
            w_out,
            conv_gain,
            w_pointin,
            w_pointout.T,
            pick,
            w_depth,
            bn_scale,
            bn_shift,
        )
        operands = tuple(pltpu.with_memory_space_constraint(a, pltpu.HBM) for a in operands)
        fetched = [i for i in range(len(operands)) if i not in (5, 6)]

        def body(*refs):
            given, out_ref, rest = list(refs[: len(operands)]), refs[len(operands)], refs[len(operands) + 1 :]
            local, sem, rest = rest[: len(fetched)], rest[len(fetched)], rest[len(fetched) + 1 :]
            fetches = []
            for j, i in enumerate(fetched):
                fetches.append(pltpu.make_async_copy(given[i], local[j], sem.at[j]))
                fetches[j].start()
                given[i] = local[j]
            layer_kernel(n_dp, shard_rows, fetches, *given, out_ref, *rest)

        dma = pltpu.SemaphoreType.DMA
        out = pl.pallas_call(
            body,
            name="conformer_layer",
            out_shape=jax.ShapeDtypeStruct((rows, width), BF),
            in_specs=[hbm] * len(operands),
            out_specs=vmem,
            scratch_shapes=[
                (pltpu.SMEM if i == 3 else pltpu.VMEM)(operands[i].shape, operands[i].dtype) for i in fetched
            ]
            + [
                pltpu.SemaphoreType.DMA((len(fetched),)),
                pltpu.VMEM(w_qkv.shape, BF),
                pltpu.VMEM(w_out.shape, BF),
                pltpu.VMEM((n_dp, cap, width), BF),
                pltpu.VMEM((n_dp, cap, width), BF),
                pltpu.VMEM((n_dp, 1, 128), F32),
                pltpu.VMEM((n_dp, 1, 128), F32),
                pltpu.VMEM((HEADS // 2, rows, seq), BF),
                pltpu.VMEM((nz, pad_rows, 2 * half_cols), BF),
                pltpu.VMEM((NY, n_ctx, nz, pad_rows, half_cols), BF),
                pltpu.VMEM((2, width, half_cols), BF),
                pltpu.VMEM((seq, 2 * head_cols), BF),
                pltpu.VMEM((rows, head_cols), BF),
                pltpu.VMEM((rows, head_cols), BF),
                pltpu.VMEM((rows, width), F32),
                pltpu.VMEM((rows, width), BF),
                pltpu.VMEM((rows, seq), F32),
                pltpu.VMEM((seq + taps, 128), F32),
                pltpu.VMEM((rows + taps, 128), F32),
                pltpu.VMEM((taps, rows, 128), F32),
                pltpu.VMEM((rows, channels), BF),
                pltpu.VMEM((taps // 2, channels), BF),
                pltpu.VMEM((taps // 2, channels), BF),
                pltpu.VMEM((rows + taps, channels), F32),
                pltpu.VMEM((rows, channels), BF),
                dma((2,)),
                dma,
                dma,
                dma,
                dma,
                dma((8,)),
                dma((8,)),
                dma((8,)),
                dma((8,)),
                dma((2, 6)),
                dma((2, 6)),
                dma((2, NX * NY)),
                dma((2, NX * NY)),
                dma((4, 3)),
                dma((4, 3)),
                dma((2,)),
                dma((2,)),
            ],
            compiler_params=pltpu.CompilerParams(
                collective_id=0, has_side_effects=True, vmem_limit_bytes=48 * 2**20
            ),
            cost_estimate=pl.CostEstimate(flops=6 * 10**9, bytes_accessed=20 * 10**6, transcendentals=3 * 10**6),
        )(*operands)

        def hand_on(src_ref, dst_ref, sem):
            copies = []
            for i in range(4):
                part = pl.ds(i * (rows // 4), rows // 4)
                copies.append(pltpu.make_async_copy(src_ref.at[part], dst_ref.at[part], sem.at[i]))
                copies[i].start()
            for copy in copies:
                copy.wait()

        out = pl.pallas_call(
            hand_on,
            name="result",
            out_shape=jax.ShapeDtypeStruct((rows, width), BF),
            in_specs=[pl.BlockSpec(memory_space=pl.ANY)],
            out_specs=pl.BlockSpec(memory_space=pl.ANY),
            scratch_shapes=[dma((4,))],
            compiler_params=pltpu.CompilerParams(vmem_limit_bytes=2**20),
        )(out)
        return out[None]

    return jax.shard_map(
        per_device,
        mesh=mesh,
        in_specs=(
            P("dp", "ctx", None),
            P("dp", "ctx"),
            P("dp", None),
            P("dp", "ctx", None),
            P(),
            P(),
            P(),
            P(),
            P(("dp", "ctx"), None),
            P(None, ("dp", "ctx")),
            P(),
            P(),
            P(),
        ),
        out_specs=P("dp", "ctx", None),
        check_vma=False,
    )
```

```python
import math

import numpy as np

import jax
import jax.numpy as jnp
from jax import lax
from jax.experimental import pallas as pl
from jax.experimental.pallas import tpu as pltpu
from jax.sharding import PartitionSpec as P

HEADS = 8
NX = 4
NY = 2
MESH = pl.DeviceIdType.MESH
BF = jnp.bfloat16
F32 = jnp.float32
MASKED = -2e38


def dot(a, b):
    return jnp.dot(a, b, preferred_element_type=F32)


def dot_nt(a, b):
    return lax.dot_general(a, b, (((1,), (1,)), ((), ())), preferred_element_type=F32)


def layer_norm(as_float, gain):
    row_mean = jnp.mean(as_float, axis=-1, keepdims=True)
    centred = as_float - row_mean
    row_var = jnp.mean(centred * centred, axis=-1, keepdims=True)
    return centred * lax.rsqrt(row_var + 1e-06) * gain


def layer_kernel(
    n_dp,
    shard_rows,
    fetches,
    dest_ref,
    frames_ref,
    seg_ref,
    tile_ref,
    again_ref,
    wqkv_hbm,
    wout_hbm,
    cgain_ref,
    pin_ref,
    pout_ref,
    pick_ref,
    wdepth_ref,
    bns_ref,
    bnb_ref,
    out_ref,
    wqkv_ref,
    wout_ref,
    send_ref,
    got_ref,
    meta_ref,
    gmeta_ref,
    prob_ref,
    zbuf_ref,
    cbuf_ref,
    wfull_ref,
    kv_ref,
    q_ref,
    att_ref,
    placed_ref,
    after_ref,
    bias_ref,
    segc_ref,
    segn_ref,
    mask_ref,
    gat_ref,
    htop_ref,
    hbot_ref,
    gf_ref,
    act_ref,
    load_sem,
    a_send,
    a_recv,
    m_send,
    m_recv,
    bz_send,
    bz_recv,
    by_send,
    by_recv,
    bx_send,
    bx_recv,
    sib_send,
    sib_recv,
    kv_send,
    kv_recv,
    halo_send,
    halo_recv,
):
    rows, width = frames_ref.shape
    seq = seg_ref.shape[1]
    nz = n_dp // (NX * NY)
    cap = send_ref.shape[1]
    head_cols = wout_ref.shape[0]
    head = head_cols // HEADS
    group = head_cols // 2
    half_cols = cbuf_ref.shape[4]
    block = wfull_ref.shape[1] // (NX * NY)
    channels = wdepth_ref.shape[1]
    taps = wdepth_ref.shape[0]
    half = taps // 2
    tile = 128

    dp = lax.axis_index("dp")
    ctx = lax.axis_index("ctx")
    x = dp // (NY * nz)
    yh = (dp // nz) % NY
    z = dp % nz
    core = ctx % 2

    def dp_of(px, py, pz):
        return (px * NY + py) * nz + pz

    def peer(i):
        zi, rest = i // (NX * NY), NX * NY - 1 - i % (NX * NY)
        kz = nz // 2 + ((zi + 1) // 2) * (1 - 2 * (zi % 2))
        return dp_of((x + rest // NY) % NX, (yh + rest % NY) % NY, (z + kz + nz) % nz)

    def put(src, dst, ssem, rsem, d, c):
        copy = pltpu.make_async_remote_copy(
            src_ref=src, dst_ref=dst, send_sem=ssem, recv_sem=rsem, device_id=(d, c), device_id_type=MESH
        )
        copy.start()

    def settle(ref, sem):
        pltpu.make_async_copy(ref, ref, sem).wait()

    barrier = pltpu.get_barrier_semaphore()

    def greet(k, carry):
        pl.semaphore_signal(barrier, inc=1, device_id=(peer(k), ctx), device_id_type=MESH)
        return carry

    lax.fori_loop(0, n_dp - 1, greet, 0)
    for d in range(1, 4):
        pl.semaphore_signal(barrier, inc=1, device_id=(dp, ctx ^ d), device_id_type=MESH)
        pl.semaphore_signal(barrier, inc=1, device_id=(dp_of(x, 1 - yh, z), ctx ^ d), device_id_type=MESH)

    load_qkv = pltpu.make_async_copy(wqkv_hbm, wqkv_ref, load_sem.at[0])
    load_qkv.start()
    load_out = pltpu.make_async_copy(wout_hbm, wout_ref, load_sem.at[1])
    load_out.start()

    for fetch in fetches:
        fetch.wait()

    zbuf_ref[pl.ds(z, 1)] = jnp.zeros((1,) + zbuf_ref.shape[1:], BF)
    for c in range(2):
        left_col = c * half_cols
        zbuf_ref[pl.ds(z, 1), :shard_rows, left_col : left_col + channels] = pin_ref[
            :, c * channels : (c + 1) * channels
        ][None]
        zbuf_ref[pl.ds(z, 1), :shard_rows, left_col + channels : left_col + half_cols] = pout_ref[
            :, c * (channels // 2) : (c + 1) * (channels // 2)
        ][None]
    pl.semaphore_wait(barrier, n_dp - 1 + 6)
    for k in range(1, nz):
        put(zbuf_ref.at[z], zbuf_ref.at[z], bz_send.at[k], bz_recv.at[k], dp_of(x, yh, (z + k) % nz), ctx)

    dest = dest_ref[...]
    owner = dest // rows
    slot = dest % rows
    oz = owner % nz
    oy = (owner // nz) % NY
    ox = owner // (nz * NY)
    dz = (oz - z + nz) % nz - nz // 2
    zi = jnp.where(dz >= 0, 2 * dz, -2 * dz - 1)
    rel = (zi + 1) * (NX * NY) - 1 - (((ox - x + NX) % NX) * NY + (oy - yh + NY) % NY)
    rel_wide = jnp.broadcast_to(rel.astype(F32), (rows, rows))
    rel_tall = jnp.transpose(rel_wide)
    earlier = lax.broadcasted_iota(jnp.int32, (rows, rows), 0) < lax.broadcasted_iota(jnp.int32, (rows, rows), 1)
    rank = jnp.sum(jnp.where((rel_tall == rel_wide) & earlier, 1.0, 0.0), axis=0, keepdims=True)
    pos = rel * cap + rank.astype(jnp.int32)
    frames = frames_ref[...]
    per = n_dp // 4

    def pack(c):
        chunk = lax.broadcasted_iota(jnp.int32, (per * cap, rows), 0) + c * per * cap
        onehot = jnp.where(chunk == pos, 1.0, 0.0).astype(BF)
        send_ref[c * per : (c + 1) * per] = dot(onehot, frames).reshape(per, cap, width).astype(BF)

    def ship(i, carry):
        put(send_ref.at[i], got_ref.at[i], a_send, a_recv, peer(i), ctx)
        put(meta_ref.at[i], gmeta_ref.at[i], m_send, m_recv, peer(i), ctx)
        return carry

    def piece(px, py, part):
        start = pl.multiple_of((((px + NX) % NX) * NY + py) * block, 16)
        cols = pl.ds(0, channels) if part == 0 else pl.ds(channels, half_cols - channels)
        return wfull_ref.at[core, pl.ds(start, block), cols]

    right = dp_of((x + 1) % NX, yh, z)
    left = dp_of((x + NX - 1) % NX, yh, z)
    other = 1 - yh

    def to_sibling(i, px, py, part):
        ref = piece(px, py, part)
        put(ref, ref, sib_send.at[part, i], sib_recv.at[part, i], dp, ctx ^ 1)

    def to_x(i, px, py, part, d):
        ref = piece(px, py, part)
        put(ref, ref, bx_send.at[part, i], bx_recv.at[part, i], d, ctx)

    def own_to_x(part):
        to_x(0, x, yh, part, right)
        to_x(1, x, yh, part, left)

    def pair_to_x(part):
        to_x(2, x, other, part, right)
        to_x(3, x, other, part, left)

    def hand_right(part):
        settle(piece(x - 1, yh, part), bx_recv.at[part, 0])
        settle(piece(x + 1, yh, part), bx_recv.at[part, 1])
        to_x(4, x - 1, yh, part, right)
        to_sibling(2, x - 1, yh, part)
        to_sibling(3, x + 1, yh, part)

    def hand_left(part):
        settle(piece(x - 1, other, part), bx_recv.at[part, 2])
        settle(piece(x + 1, other, part), bx_recv.at[part, 3])
        to_x(5, x + 1, other, part, left)
        to_sibling(4, x - 1, other, part)
        to_sibling(5, x + 1, other, part)

    def two_away(part):
        settle(piece(x + 2, yh, part), bx_recv.at[part, 4])
        to_sibling(6, x + 2, yh, part)
        settle(piece(x + 2, other, part), bx_recv.at[part, 5])
        to_sibling(7, x + 2, other, part)

    def from_sibling(part):
        for i in range(NX * NY):
            settle(piece(x, yh, part), sib_recv.at[part, i])

    pack(0)
    rank_tall = jnp.transpose(jnp.broadcast_to(rank, (tile, rows)))
    slot_tall = jnp.transpose(jnp.broadcast_to(slot.astype(F32) + 1.0, (tile, rows)))
    lane = lax.broadcasted_iota(jnp.int32, (rows, tile), 1).astype(F32)
    at_rank = jnp.where(rank_tall == lane, slot_tall, 0.0).astype(BF)
    to_peer = jnp.where(lax.broadcasted_iota(jnp.int32, (n_dp, rows), 0) == rel, 1.0, 0.0).astype(BF)
    meta_ref[...] = dot(to_peer, at_rank).reshape(n_dp, 1, tile)
    lax.fori_loop(0, per, ship, 0)
    pack(1)
    pack(2)
    for k in range(1, nz):
        settle(zbuf_ref.at[0], bz_recv.at[k])
    for i in range(1, 2 * 4):
        d, far = i // 2, i % 2
        cols = pl.ds(pl.multiple_of(((ctx ^ d) % 2) * half_cols, 128), half_cols)
        to_yh = other if far else yh
        put(zbuf_ref.at[:, :, cols], cbuf_ref.at[yh, ctx], by_send.at[i], by_recv.at[i], dp_of(x, to_yh, z), ctx ^ d)
    lax.fori_loop(per, 3 * per, ship, 0)
    mine = pl.ds(pl.multiple_of(core * half_cols, 128), half_cols)
    cbuf_ref[yh, pl.ds(ctx, 1)] = zbuf_ref[:, :, mine][None]
    pack(3)
    for i in range(1, 2 * 4):
        settle(cbuf_ref.at[0, 0], by_recv.at[i])
    for y in range(NY):
        padded = cbuf_ref[y].astype(F32).reshape(pick_ref.shape[1], half_cols).astype(BF)
        start = pl.multiple_of((x * NY + y) * block, 16)
        wfull_ref[core, pl.ds(start, block)] = dot(pick_ref[...], padded).astype(BF)
    own_to_x(0)
    pair_to_x(0)
    lax.fori_loop(3 * per, n_dp - 1, ship, 0)
    for part in range(2):
        to_sibling(0, x, yh, part)
        to_sibling(1, x, other, part)
    got_ref[n_dp - 1] = send_ref[n_dp - 1]
    gmeta_ref[n_dp - 1] = meta_ref[n_dp - 1]

    segf = seg_ref[...].astype(F32)
    segc_ref[0:half] = jnp.full((half, tile), -1.0, F32)
    segc_ref[half + seq :] = jnp.full((half, tile), -1.0, F32)
    segc_ref[half : half + seq] = jnp.transpose(jnp.broadcast_to(segf, (tile, seq)))
    first = pl.multiple_of(ctx * rows, rows)
    segn_ref[...] = segc_ref[pl.ds(first, rows + 2 * half)]
    own_seg = segn_ref[half : half + rows]
    for tk in range(seq // tile):
        same = own_seg == segf[:, tk * tile : (tk + 1) * tile]
        for tq in range(rows // tile):
            off = (1 - tile_ref[tq, tk]).astype(F32) * MASKED
            bias_ref[tq * tile : (tq + 1) * tile, tk * tile : (tk + 1) * tile] = jnp.where(
                same[tq * tile : (tq + 1) * tile], off, MASKED
            )
    for k in range(taps):
        mask_ref[k] = jnp.where(segn_ref[k : k + rows] == own_seg, 1.0, 0.0)

    settle(gmeta_ref.at[pl.ds(0, n_dp - 1)], m_recv)
    spots = n_dp * cap
    spot = lax.broadcasted_iota(jnp.int32, (tile, spots), 1)
    spread = jnp.where(lax.broadcasted_iota(jnp.int32, (tile, spots), 0) == spot % cap, 1.0, 0.0).astype(BF)
    spread = dot(gmeta_ref[...].reshape(n_dp, tile).astype(BF), spread)
    spot = lax.broadcasted_iota(jnp.int32, (n_dp, spots), 1)
    from_peer = lax.broadcasted_iota(jnp.int32, (n_dp, spots), 0) == spot // cap
    slots = jnp.sum(jnp.where(from_peer, spread, 0.0), axis=0, keepdims=True)
    lane = lax.broadcasted_iota(jnp.int32, (rows, spots), 0).astype(F32) + 1.0
    place = jnp.where(lane == slots, 1.0, 0.0).astype(BF)
    settle(got_ref.at[pl.ds(0, n_dp - 1)], a_recv)
    got = got_ref[...].astype(F32).reshape(spots, width).astype(BF)
    placed = dot(place, got)
    placed_ref[...] = placed
    normed = layer_norm(placed, again_ref[...][None]).astype(BF)

    load_qkv.wait()
    base = pl.multiple_of(ctx * rows, rows)
    keys = dot(normed, wqkv_ref[:, head_cols : 2 * head_cols]).astype(BF)
    values = dot(normed, wqkv_ref[:, 2 * head_cols :]).astype(BF)
    for g in range(2):
        kv_ref[pl.ds(base, rows), 2 * g * group : (2 * g + 1) * group] = keys[:, g * group : (g + 1) * group]
        kv_ref[pl.ds(base, rows), (2 * g + 1) * group : (2 * g + 2) * group] = values[:, g * group : (g + 1) * group]

    def kv_part(c, i):
        return kv_ref.at[pl.ds(pl.multiple_of(c * rows, rows), rows), pl.ds(i * group, group)]

    for i in range(4):
        part = kv_part(ctx, i)
        put(part, part, kv_send.at[i, 0], kv_recv.at[i, 0], dp, ctx ^ 2)
        put(part, part, kv_send.at[i, 1], kv_recv.at[i, 1], dp, ctx ^ 1)
    scale = math.log2(math.e) / math.sqrt(head)
    q_ref[...] = (dot(normed, wqkv_ref[:, :head_cols]) * scale).astype(BF)

    def arrive(i):
        part = kv_part(ctx ^ 2, i)
        settle(part, kv_recv.at[i, 0])
        put(part, part, kv_send.at[i, 2], kv_recv.at[i, 2], dp, ctx ^ 1)
        settle(part, kv_recv.at[i, 1])
        settle(part, kv_recv.at[i, 2])

    def windows(h):
        lo, hi = h * head, (h + 1) * head
        c0, c1 = lo // tile * tile, (hi + tile - 1) // tile * tile
        lanes = lax.broadcasted_iota(jnp.int32, (rows, c1 - c0), 1) + c0
        return c0, c1, (lanes >= lo) & (lanes < hi)

    def score(g):
        totals = []
        for h in range(HEADS // 2):
            c0, c1, inside = windows(h)
            query = q_ref[:, g * group + c0 : g * group + c1].astype(F32)
            query = jnp.where(inside, query, 0.0).astype(BF)
            scores = dot_nt(query, kv_ref[:, 2 * g * group + c0 : 2 * g * group + c1]) + bias_ref[...]
            weights = jnp.exp2(scores - jnp.max(scores, axis=1, keepdims=True))
            totals.append(jnp.sum(weights, axis=1, keepdims=True))
            prob_ref[h] = weights.astype(BF)
        return totals

    def mix(g, totals):
        tiles = [None] * (group // tile)
        for h in range(HEADS // 2):
            c0, c1, inside = windows(h)
            mixed = dot(prob_ref[h], kv_ref[:, (2 * g + 1) * group + c0 : (2 * g + 1) * group + c1])
            mixed = jnp.where(inside, mixed / totals[h], 0.0)
            for t in range(c0 // tile, c1 // tile):
                term = mixed[:, t * tile - c0 : (t + 1) * tile - c0]
                tiles[t] = term if tiles[t] is None else tiles[t] + term
        for t, whole in enumerate(tiles):
            att_ref[:, g * group + t * tile : g * group + (t + 1) * tile] = whole.astype(BF)

    hand_right(0)
    hand_left(0)
    own_to_x(1)
    pair_to_x(1)
    arrive(0)
    totals = score(0)
    arrive(1)
    mix(0, totals)
    arrive(2)
    totals = score(1)
    arrive(3)
    mix(1, totals)

    load_out.wait()
    after = (placed_ref[...] + dot(att_ref[...], wout_ref[...])).astype(BF)
    after_ref[...] = after
    conv_normed = layer_norm(after.astype(F32), cgain_ref[...][None]).astype(BF)

    two_away(0)
    from_sibling(0)

    gate = jax.nn.sigmoid(dot(conv_normed, wfull_ref[1, :, :channels]))
    gated = (dot(conv_normed, wfull_ref[0, :, :channels]) * gate).astype(BF)
    gat_ref[...] = gated
    gf_ref[half : half + rows] = gated.astype(F32)

    head_rows = gat_ref.at[0:half]
    tail_rows = gat_ref.at[rows - half : rows]

    @pl.when(ctx > 0)
    def _():
        put(head_rows, hbot_ref, halo_send.at[0], halo_recv.at[0], dp, ctx - 1)

    @pl.when(ctx < 3)
    def _():
        put(tail_rows, htop_ref, halo_send.at[1], halo_recv.at[1], dp, ctx + 1)

    @pl.when(ctx == 0)
    def _():
        htop_ref[...] = jnp.zeros_like(htop_ref)

    @pl.when(ctx == 3)
    def _():
        hbot_ref[...] = jnp.zeros_like(hbot_ref)

    span = 64

    def convolve(r0):
        def body(t, carry):
            lanes = pl.ds(pl.multiple_of(t * tile, tile), tile)
            near = gf_ref[r0 : r0 + span + 2 * half, lanes]
            total = jnp.zeros((span, tile), F32)
            for b in range(8):
                shifted = near if b == 0 else pltpu.roll(near, span + 2 * half - b, 0)
                for a in range(taps // 8):
                    k = 8 * a + b
                    term = shifted[8 * a : 8 * a + span] * mask_ref[k, r0 : r0 + span]
                    total = total + term * wdepth_ref[k : k + 1, lanes]
            moved = total * bns_ref[lanes][None] + bnb_ref[lanes][None]
            act_ref[r0 : r0 + span, lanes] = (moved * jax.nn.sigmoid(moved)).astype(BF)
            return carry

        lax.fori_loop(0, channels // tile, body, 0)

    hand_right(1)
    hand_left(1)
    for r0 in range(span, rows - span, span):
        convolve(r0)

    two_away(1)

    @pl.when(ctx > 0)
    def _():
        settle(htop_ref, halo_recv.at[1])

    @pl.when(ctx < 3)
    def _():
        settle(hbot_ref, halo_recv.at[0])

    gf_ref[0:half] = htop_ref[...].astype(F32)
    gf_ref[half + rows :] = hbot_ref[...].astype(F32)
    convolve(0)
    convolve(rows - span)

    from_sibling(1)
    quarter = channels // 2
    closing = dot_nt(act_ref[:, :quarter], wfull_ref[0, :, channels:])
    closing = closing + dot_nt(act_ref[:, quarter:], wfull_ref[1, :, channels:])
    out_ref[...] = (after_ref[...].astype(F32) + closing).astype(BF)

    settle(send_ref.at[pl.ds(0, n_dp - 1)], a_send)
    settle(meta_ref.at[pl.ds(0, n_dp - 1)], m_send)
    for k in range(1, nz):
        settle(zbuf_ref.at[0], bz_send.at[k])
    for i in range(1, 2 * 4):
        settle(cbuf_ref.at[0, 0], by_send.at[i])
    for part in range(2):
        for i in range(6):
            settle(piece(x, yh, part), bx_send.at[part, i])
        for i in range(NX * NY):
            settle(piece(x, yh, part), sib_send.at[part, i])
    for i in range(4):
        for j in range(3):
            settle(kv_part(ctx, i), kv_send.at[i, j])

    @pl.when(ctx > 0)
    def _():
        settle(head_rows, halo_send.at[0])

    @pl.when(ctx < 3)
    def _():
        settle(tail_rows, halo_send.at[1])


def solution(mesh):
    n_dp = mesh.shape["dp"]
    n_ctx = mesh.shape["ctx"]
    nz = n_dp // (NX * NY)

    def per_device(
        frames,
        destinations,
        segments,
        tile_mask,
        attn_gain,
        w_qkv,
        w_out,
        conv_gain,
        w_pointin,
        w_pointout,
        w_depth,
        bn_scale,
        bn_shift,
    ):
        rows, width = frames.shape[1:]
        seq = segments.shape[1]
        channels = w_depth.shape[1]
        taps = w_depth.shape[0]
        head_cols = w_out.shape[0]
        cap = 2 * rows // n_dp
        shard_rows = w_pointin.shape[0]
        pad_rows = -(-shard_rows // 8) * 8
        half_cols = channels + channels // 2
        pick = np.zeros((nz * n_ctx * shard_rows, n_ctx * nz * pad_rows), np.float32)
        for a in range(nz):
            for b in range(n_ctx):
                for j in range(shard_rows):
                    pick[(a * n_ctx + b) * shard_rows + j, (b * nz + a) * pad_rows + j] = 1.0
        pick = jnp.asarray(pick, BF)
        vmem = pl.BlockSpec(memory_space=pltpu.VMEM)
        hbm = pl.BlockSpec(memory_space=pltpu.HBM)
        operands = (
            destinations,
            frames[0],
            segments,
            tile_mask[0],
            attn_gain,
            w_qkv,
            w_out,
            conv_gain,
            w_pointin,
            w_pointout.T,
            pick,
            w_depth,
            bn_scale,
            bn_shift,
        )
        operands = tuple(pltpu.with_memory_space_constraint(a, pltpu.HBM) for a in operands)
        fetched = [i for i in range(len(operands)) if i not in (5, 6)]

        def body(*refs):
            given, out_ref, rest = list(refs[: len(operands)]), refs[len(operands)], refs[len(operands) + 1 :]
            local, sem, rest = rest[: len(fetched)], rest[len(fetched)], rest[len(fetched) + 1 :]
            fetches = []
            for j, i in enumerate(fetched):
                fetches.append(pltpu.make_async_copy(given[i], local[j], sem.at[j]))
                fetches[j].start()
                given[i] = local[j]
            layer_kernel(n_dp, shard_rows, fetches, *given, out_ref, *rest)

        dma = pltpu.SemaphoreType.DMA
        out = pl.pallas_call(
            body,
            name="conformer_layer",
            out_shape=jax.ShapeDtypeStruct((rows, width), BF),
            in_specs=[hbm] * len(operands),
            out_specs=vmem,
            scratch_shapes=[
                (pltpu.SMEM if i == 3 else pltpu.VMEM)(operands[i].shape, operands[i].dtype) for i in fetched
            ]
            + [
                pltpu.SemaphoreType.DMA((len(fetched),)),
                pltpu.VMEM(w_qkv.shape, BF),
                pltpu.VMEM(w_out.shape, BF),
                pltpu.VMEM((n_dp, cap, width), BF),
                pltpu.VMEM((n_dp, cap, width), BF),
                pltpu.VMEM((n_dp, 1, 128), F32),
                pltpu.VMEM((n_dp, 1, 128), F32),
                pltpu.VMEM((HEADS // 2, rows, seq), BF),
                pltpu.VMEM((nz, pad_rows, 2 * half_cols), BF),
                pltpu.VMEM((NY, n_ctx, nz, pad_rows, half_cols), BF),
                pltpu.VMEM((2, width, half_cols), BF),
                pltpu.VMEM((seq, 2 * head_cols), BF),
                pltpu.VMEM((rows, head_cols), BF),
                pltpu.VMEM((rows, head_cols), BF),
                pltpu.VMEM((rows, width), F32),
                pltpu.VMEM((rows, width), BF),
                pltpu.VMEM((rows, seq), F32),
                pltpu.VMEM((seq + taps, 128), F32),
                pltpu.VMEM((rows + taps, 128), F32),
                pltpu.VMEM((taps, rows, 128), F32),
                pltpu.VMEM((rows, channels), BF),
                pltpu.VMEM((taps // 2, channels), BF),
                pltpu.VMEM((taps // 2, channels), BF),
                pltpu.VMEM((rows + taps, channels), F32),
                pltpu.VMEM((rows, channels), BF),
                dma((2,)),
                dma,
                dma,
                dma,
                dma,
                dma((8,)),
                dma((8,)),
                dma((8,)),
                dma((8,)),
                dma((2, 6)),
                dma((2, 6)),
                dma((2, NX * NY)),
                dma((2, NX * NY)),
                dma((4, 3)),
                dma((4, 3)),
                dma((2,)),
                dma((2,)),
            ],
            compiler_params=pltpu.CompilerParams(
                collective_id=0, has_side_effects=True, vmem_limit_bytes=48 * 2**20
            ),
            cost_estimate=pl.CostEstimate(flops=6 * 10**9, bytes_accessed=20 * 10**6, transcendentals=3 * 10**6),
        )(*operands)

        def hand_on(src_ref, dst_ref, sem):
            copies = []
            for i in range(4):
                part = pl.ds(i * (rows // 4), rows // 4)
                copies.append(pltpu.make_async_copy(src_ref.at[part], dst_ref.at[part], sem.at[i]))
                copies[i].start()
            for copy in copies:
                copy.wait()

        out = pl.pallas_call(
            hand_on,
            name="result",
            out_shape=jax.ShapeDtypeStruct((rows, width), BF),
            in_specs=[pl.BlockSpec(memory_space=pl.ANY)],
            out_specs=pl.BlockSpec(memory_space=pl.ANY),
            scratch_shapes=[dma((4,))],
            compiler_params=pltpu.CompilerParams(vmem_limit_bytes=2**20),
        )(out)
        return out[None]

    return jax.shard_map(
        per_device,
        mesh=mesh,
        in_specs=(
            P("dp", "ctx", None),
            P("dp", "ctx"),
            P("dp", None),
            P("dp", "ctx", None),
            P(),
            P(),
            P(),
            P(),
            P(("dp", "ctx"), None),
            P(None, ("dp", "ctx")),
            P(),
            P(),
            P(),
        ),
        out_specs=P("dp", "ctx", None),
        check_vma=False,
    )
```

```python
import math

import numpy as np

import jax
import jax.numpy as jnp
from jax import lax
from jax.experimental import pallas as pl
from jax.experimental.pallas import tpu as pltpu
from jax.sharding import PartitionSpec as P

HEADS = 8
NX = 4
NY = 2
MESH = pl.DeviceIdType.MESH
BF = jnp.bfloat16
F32 = jnp.float32
MASKED = -2e38


def dot(a, b):
    return jnp.dot(a, b, preferred_element_type=F32)


def dot_nt(a, b):
    return lax.dot_general(a, b, (((1,), (1,)), ((), ())), preferred_element_type=F32)


def layer_norm(as_float, gain):
    row_mean = jnp.mean(as_float, axis=-1, keepdims=True)
    centred = as_float - row_mean
    row_var = jnp.mean(centred * centred, axis=-1, keepdims=True)
    return centred * lax.rsqrt(row_var + 1e-06) * gain


def layer_kernel(
    n_dp,
    shard_rows,
    fetches,
    dest_ref,
    frames_ref,
    seg_ref,
    tile_ref,
    again_ref,
    wqkv_hbm,
    wout_hbm,
    cgain_ref,
    pin_ref,
    pout_ref,
    pick_ref,
    wdepth_ref,
    bns_ref,
    bnb_ref,
    out_ref,
    wqkv_ref,
    wout_ref,
    send_ref,
    got_ref,
    meta_ref,
    gmeta_ref,
    prob_ref,
    zbuf_ref,
    cbuf_ref,
    wfull_ref,
    kv_ref,
    q_ref,
    att_ref,
    placed_ref,
    after_ref,
    bias_ref,
    segc_ref,
    segn_ref,
    mask_ref,
    gat_ref,
    htop_ref,
    hbot_ref,
    gf_ref,
    act_ref,
    load_sem,
    a_send,
    a_recv,
    m_send,
    m_recv,
    bz_send,
    bz_recv,
    by_send,
    by_recv,
    bx_send,
    bx_recv,
    sib_send,
    sib_recv,
    kv_send,
    kv_recv,
    halo_send,
    halo_recv,
):
    rows, width = frames_ref.shape
    seq = seg_ref.shape[1]
    nz = n_dp // (NX * NY)
    cap = send_ref.shape[1]
    head_cols = wout_ref.shape[0]
    head = head_cols // HEADS
    group = head_cols // 2
    half_cols = cbuf_ref.shape[4]
    block = wfull_ref.shape[1] // (NX * NY)
    channels = wdepth_ref.shape[1]
    taps = wdepth_ref.shape[0]
    half = taps // 2
    tile = 128

    dp = lax.axis_index("dp")
    ctx = lax.axis_index("ctx")
    x = dp // (NY * nz)
    yh = (dp // nz) % NY
    z = dp % nz
    core = ctx % 2

    def dp_of(px, py, pz):
        return (px * NY + py) * nz + pz

    def peer(i):
        zi, rest = i // (NX * NY), NX * NY - 1 - i % (NX * NY)
        kz = nz // 2 + ((zi + 1) // 2) * (1 - 2 * (zi % 2))
        return dp_of((x + rest // NY) % NX, (yh + rest % NY) % NY, (z + kz + nz) % nz)

    def put(src, dst, ssem, rsem, d, c):
        copy = pltpu.make_async_remote_copy(
            src_ref=src, dst_ref=dst, send_sem=ssem, recv_sem=rsem, device_id=(d, c), device_id_type=MESH
        )
        copy.start()

    def settle(ref, sem):
        pltpu.make_async_copy(ref, ref, sem).wait()

    barrier = pltpu.get_barrier_semaphore()

    def greet(k, carry):
        pl.semaphore_signal(barrier, inc=1, device_id=(peer(k), ctx), device_id_type=MESH)
        return carry

    lax.fori_loop(0, n_dp - 1, greet, 0)
    for d in range(1, 4):
        pl.semaphore_signal(barrier, inc=1, device_id=(dp, ctx ^ d), device_id_type=MESH)
        pl.semaphore_signal(barrier, inc=1, device_id=(dp_of(x, 1 - yh, z), ctx ^ d), device_id_type=MESH)

    load_qkv = pltpu.make_async_copy(wqkv_hbm, wqkv_ref, load_sem.at[0])
    load_qkv.start()
    load_out = pltpu.make_async_copy(wout_hbm, wout_ref, load_sem.at[1])
    load_out.start()

    for fetch in fetches:
        fetch.wait()

    zbuf_ref[pl.ds(z, 1)] = jnp.zeros((1,) + zbuf_ref.shape[1:], BF)
    for c in range(2):
        left_col = c * half_cols
        zbuf_ref[pl.ds(z, 1), :shard_rows, left_col : left_col + channels] = pin_ref[
            :, c * channels : (c + 1) * channels
        ][None]
        zbuf_ref[pl.ds(z, 1), :shard_rows, left_col + channels : left_col + half_cols] = pout_ref[
            :, c * (channels // 2) : (c + 1) * (channels // 2)
        ][None]
    pl.semaphore_wait(barrier, n_dp - 1 + 6)
    for k in range(1, nz):
        put(zbuf_ref.at[z], zbuf_ref.at[z], bz_send.at[k], bz_recv.at[k], dp_of(x, yh, (z + k) % nz), ctx)

    dest = dest_ref[...]
    owner = dest // rows
    slot = dest % rows
    oz = owner % nz
    oy = (owner // nz) % NY
    ox = owner // (nz * NY)
    dz = (oz - z + nz) % nz - nz // 2
    zi = jnp.where(dz >= 0, 2 * dz, -2 * dz - 1)
    rel = (zi + 1) * (NX * NY) - 1 - (((ox - x + NX) % NX) * NY + (oy - yh + NY) % NY)
    rel_wide = jnp.broadcast_to(rel.astype(F32), (rows, rows))
    rel_tall = jnp.transpose(rel_wide)
    earlier = lax.broadcasted_iota(jnp.int32, (rows, rows), 0) < lax.broadcasted_iota(jnp.int32, (rows, rows), 1)
    rank = jnp.sum(jnp.where((rel_tall == rel_wide) & earlier, 1.0, 0.0), axis=0, keepdims=True)
    pos = rel * cap + rank.astype(jnp.int32)
    frames = frames_ref[...]
    per = n_dp // 4

    def pack(c):
        chunk = lax.broadcasted_iota(jnp.int32, (per * cap, rows), 0) + c * per * cap
        onehot = jnp.where(chunk == pos, 1.0, 0.0).astype(BF)
        send_ref[c * per : (c + 1) * per] = dot(onehot, frames).reshape(per, cap, width).astype(BF)

    def ship(i, carry):
        put(send_ref.at[i], got_ref.at[i], a_send, a_recv, peer(i), ctx)
        put(meta_ref.at[i], gmeta_ref.at[i], m_send, m_recv, peer(i), ctx)
        return carry

    def piece(px, py, part):
        start = pl.multiple_of((((px + NX) % NX) * NY + py) * block, 16)
        cols = pl.ds(0, channels) if part == 0 else pl.ds(channels, half_cols - channels)
        return wfull_ref.at[core, pl.ds(start, block), cols]

    right = dp_of((x + 1) % NX, yh, z)
    left = dp_of((x + NX - 1) % NX, yh, z)
    other = 1 - yh

    def to_sibling(i, px, py, part):
        ref = piece(px, py, part)
        put(ref, ref, sib_send.at[part, i], sib_recv.at[part, i], dp, ctx ^ 1)

    def to_x(i, px, py, part, d):
        ref = piece(px, py, part)
        put(ref, ref, bx_send.at[part, i], bx_recv.at[part, i], d, ctx)

    def own_to_x(part):
        to_x(0, x, yh, part, right)
        to_x(1, x, yh, part, left)

    def pair_to_x(part):
        to_x(2, x, other, part, right)
        to_x(3, x, other, part, left)

    def hand_right(part):
        settle(piece(x - 1, yh, part), bx_recv.at[part, 0])
        settle(piece(x + 1, yh, part), bx_recv.at[part, 1])
        to_x(4, x - 1, yh, part, right)
        to_sibling(2, x - 1, yh, part)
        to_sibling(3, x + 1, yh, part)

    def hand_left(part):
        settle(piece(x - 1, other, part), bx_recv.at[part, 2])
        settle(piece(x + 1, other, part), bx_recv.at[part, 3])
        to_x(5, x + 1, other, part, left)
        to_sibling(4, x - 1, other, part)
        to_sibling(5, x + 1, other, part)

    def two_away(part):
        settle(piece(x + 2, yh, part), bx_recv.at[part, 4])
        to_sibling(6, x + 2, yh, part)
        settle(piece(x + 2, other, part), bx_recv.at[part, 5])
        to_sibling(7, x + 2, other, part)

    def from_sibling(part):
        for i in range(NX * NY):
            settle(piece(x, yh, part), sib_recv.at[part, i])

    pack(3)
    rank_tall = jnp.transpose(jnp.broadcast_to(rank, (tile, rows)))
    slot_tall = jnp.transpose(jnp.broadcast_to(slot.astype(F32) + 1.0, (tile, rows)))
    lane = lax.broadcasted_iota(jnp.int32, (rows, tile), 1).astype(F32)
    at_rank = jnp.where(rank_tall == lane, slot_tall, 0.0).astype(BF)
    to_peer = jnp.where(lax.broadcasted_iota(jnp.int32, (n_dp, rows), 0) == rel, 1.0, 0.0).astype(BF)
    meta_ref[...] = dot(to_peer, at_rank).reshape(n_dp, 1, tile)
    lax.fori_loop(3 * per, n_dp - 1, ship, 0)
    pack(0)
    pack(1)
    for k in range(1, nz):
        settle(zbuf_ref.at[0], bz_recv.at[k])
    for i in range(1, 2 * 4):
        d, far = i // 2, i % 2
        cols = pl.ds(pl.multiple_of(((ctx ^ d) % 2) * half_cols, 128), half_cols)
        to_yh = other if far else yh
        put(zbuf_ref.at[:, :, cols], cbuf_ref.at[yh, ctx], by_send.at[i], by_recv.at[i], dp_of(x, to_yh, z), ctx ^ d)
    lax.fori_loop(0, 3 * n_dp // 8, ship, 0)
    mine = pl.ds(pl.multiple_of(core * half_cols, 128), half_cols)
    cbuf_ref[yh, pl.ds(ctx, 1)] = zbuf_ref[:, :, mine][None]
    pack(2)
    lax.fori_loop(3 * n_dp // 8, 3 * per, ship, 0)
    for i in range(1, 2 * 4):
        settle(cbuf_ref.at[0, 0], by_recv.at[i])
    for y in range(NY):
        padded = cbuf_ref[y].astype(F32).reshape(pick_ref.shape[1], half_cols).astype(BF)
        start = pl.multiple_of((x * NY + y) * block, 16)
        wfull_ref[core, pl.ds(start, block)] = dot(pick_ref[...], padded).astype(BF)
    own_to_x(0)
    pair_to_x(0)
    own_to_x(1)
    pair_to_x(1)
    for part in range(2):
        to_sibling(0, x, yh, part)
        to_sibling(1, x, other, part)
    got_ref[n_dp - 1] = send_ref[n_dp - 1]
    gmeta_ref[n_dp - 1] = meta_ref[n_dp - 1]

    segf = seg_ref[...].astype(F32)
    segc_ref[0:half] = jnp.full((half, tile), -1.0, F32)
    segc_ref[half + seq :] = jnp.full((half, tile), -1.0, F32)
    segc_ref[half : half + seq] = jnp.transpose(jnp.broadcast_to(segf, (tile, seq)))
    first = pl.multiple_of(ctx * rows, rows)
    segn_ref[...] = segc_ref[pl.ds(first, rows + 2 * half)]
    own_seg = segn_ref[half : half + rows]
    for tk in range(seq // tile):
        same = own_seg == segf[:, tk * tile : (tk + 1) * tile]
        for tq in range(rows // tile):
            off = (1 - tile_ref[tq, tk]).astype(F32) * MASKED
            bias_ref[tq * tile : (tq + 1) * tile, tk * tile : (tk + 1) * tile] = jnp.where(
                same[tq * tile : (tq + 1) * tile], off, MASKED
            )
    for k in range(taps):
        mask_ref[k] = jnp.where(segn_ref[k : k + rows] == own_seg, 1.0, 0.0)

    settle(gmeta_ref.at[pl.ds(0, n_dp - 1)], m_recv)
    spots = n_dp * cap
    spot = lax.broadcasted_iota(jnp.int32, (tile, spots), 1)
    spread = jnp.where(lax.broadcasted_iota(jnp.int32, (tile, spots), 0) == spot % cap, 1.0, 0.0).astype(BF)
    spread = dot(gmeta_ref[...].reshape(n_dp, tile).astype(BF), spread)
    spot = lax.broadcasted_iota(jnp.int32, (n_dp, spots), 1)
    from_peer = lax.broadcasted_iota(jnp.int32, (n_dp, spots), 0) == spot // cap
    slots = jnp.sum(jnp.where(from_peer, spread, 0.0), axis=0, keepdims=True)
    lane = lax.broadcasted_iota(jnp.int32, (rows, spots), 0).astype(F32) + 1.0
    place = jnp.where(lane == slots, 1.0, 0.0).astype(BF)
    settle(got_ref.at[pl.ds(0, n_dp - 1)], a_recv)
    got = got_ref[...].astype(F32).reshape(spots, width).astype(BF)
    placed = dot(place, got)
    placed_ref[...] = placed
    normed = layer_norm(placed, again_ref[...][None]).astype(BF)

    load_qkv.wait()
    base = pl.multiple_of(ctx * rows, rows)
    keys = dot(normed, wqkv_ref[:, head_cols : 2 * head_cols]).astype(BF)
    values = dot(normed, wqkv_ref[:, 2 * head_cols :]).astype(BF)
    for g in range(2):
        kv_ref[pl.ds(base, rows), 2 * g * group : (2 * g + 1) * group] = keys[:, g * group : (g + 1) * group]
        kv_ref[pl.ds(base, rows), (2 * g + 1) * group : (2 * g + 2) * group] = values[:, g * group : (g + 1) * group]

    def kv_part(c, i):
        return kv_ref.at[pl.ds(pl.multiple_of(c * rows, rows), rows), pl.ds(i * group, group)]

    for i in range(4):
        part = kv_part(ctx, i)
        put(part, part, kv_send.at[i, 0], kv_recv.at[i, 0], dp, ctx ^ 2)
        put(part, part, kv_send.at[i, 1], kv_recv.at[i, 1], dp, ctx ^ 1)
    scale = math.log2(math.e) / math.sqrt(head)
    q_ref[...] = (dot(normed, wqkv_ref[:, :head_cols]) * scale).astype(BF)

    def arrive(i):
        part = kv_part(ctx ^ 2, i)
        settle(part, kv_recv.at[i, 0])
        put(part, part, kv_send.at[i, 2], kv_recv.at[i, 2], dp, ctx ^ 1)
        settle(part, kv_recv.at[i, 1])
        settle(part, kv_recv.at[i, 2])

    def windows(h):
        lo, hi = h * head, (h + 1) * head
        c0, c1 = lo // tile * tile, (hi + tile - 1) // tile * tile
        lanes = lax.broadcasted_iota(jnp.int32, (rows, c1 - c0), 1) + c0
        return c0, c1, (lanes >= lo) & (lanes < hi)

    def score(g):
        totals = []
        for h in range(HEADS // 2):
            c0, c1, inside = windows(h)
            query = q_ref[:, g * group + c0 : g * group + c1].astype(F32)
            query = jnp.where(inside, query, 0.0).astype(BF)
            scores = dot_nt(query, kv_ref[:, 2 * g * group + c0 : 2 * g * group + c1]) + bias_ref[...]
            weights = jnp.exp2(scores - jnp.max(scores, axis=1, keepdims=True))
            totals.append(jnp.sum(weights, axis=1, keepdims=True))
            prob_ref[h] = weights.astype(BF)
        return totals

    def mix(g, totals):
        tiles = [None] * (group // tile)
        for h in range(HEADS // 2):
            c0, c1, inside = windows(h)
            mixed = dot(prob_ref[h], kv_ref[:, (2 * g + 1) * group + c0 : (2 * g + 1) * group + c1])
            mixed = jnp.where(inside, mixed / totals[h], 0.0)
            for t in range(c0 // tile, c1 // tile):
                term = mixed[:, t * tile - c0 : (t + 1) * tile - c0]
                tiles[t] = term if tiles[t] is None else tiles[t] + term
        for t, whole in enumerate(tiles):
            att_ref[:, g * group + t * tile : g * group + (t + 1) * tile] = whole.astype(BF)

    hand_right(0)
    hand_left(0)
    arrive(0)
    totals = score(0)
    arrive(1)
    mix(0, totals)
    hand_right(1)
    hand_left(1)
    arrive(2)
    totals = score(1)
    arrive(3)
    mix(1, totals)

    load_out.wait()
    after = (placed_ref[...] + dot(att_ref[...], wout_ref[...])).astype(BF)
    after_ref[...] = after
    conv_normed = layer_norm(after.astype(F32), cgain_ref[...][None]).astype(BF)

    two_away(0)
    from_sibling(0)

    gate = jax.nn.sigmoid(dot(conv_normed, wfull_ref[1, :, :channels]))
    gated = (dot(conv_normed, wfull_ref[0, :, :channels]) * gate).astype(BF)
    gat_ref[...] = gated
    gf_ref[half : half + rows] = gated.astype(F32)

    head_rows = gat_ref.at[0:half]
    tail_rows = gat_ref.at[rows - half : rows]

    @pl.when(ctx > 0)
    def _():
        put(head_rows, hbot_ref, halo_send.at[0], halo_recv.at[0], dp, ctx - 1)

    @pl.when(ctx < 3)
    def _():
        put(tail_rows, htop_ref, halo_send.at[1], halo_recv.at[1], dp, ctx + 1)

    @pl.when(ctx == 0)
    def _():
        htop_ref[...] = jnp.zeros_like(htop_ref)

    @pl.when(ctx == 3)
    def _():
        hbot_ref[...] = jnp.zeros_like(hbot_ref)

    span = 64

    def convolve(r0):
        def body(t, carry):
            lanes = pl.ds(pl.multiple_of(t * tile, tile), tile)
            near = gf_ref[r0 : r0 + span + 2 * half, lanes]
            total = jnp.zeros((span, tile), F32)
            for b in range(8):
                shifted = near if b == 0 else pltpu.roll(near, span + 2 * half - b, 0)
                for a in range(taps // 8):
                    k = 8 * a + b
                    term = shifted[8 * a : 8 * a + span] * mask_ref[k, r0 : r0 + span]
                    total = total + term * wdepth_ref[k : k + 1, lanes]
            moved = total * bns_ref[lanes][None] + bnb_ref[lanes][None]
            act_ref[r0 : r0 + span, lanes] = (moved * jax.nn.sigmoid(moved)).astype(BF)
            return carry

        lax.fori_loop(0, channels // tile, body, 0)

    for r0 in range(span, rows - span, span):
        convolve(r0)

    two_away(1)

    @pl.when(ctx > 0)
    def _():
        settle(htop_ref, halo_recv.at[1])

    @pl.when(ctx < 3)
    def _():
        settle(hbot_ref, halo_recv.at[0])

    gf_ref[0:half] = htop_ref[...].astype(F32)
    gf_ref[half + rows :] = hbot_ref[...].astype(F32)
    convolve(0)
    convolve(rows - span)

    from_sibling(1)
    quarter = channels // 2
    closing = dot_nt(act_ref[:, :quarter], wfull_ref[0, :, channels:])
    closing = closing + dot_nt(act_ref[:, quarter:], wfull_ref[1, :, channels:])
    out_ref[...] = (after_ref[...].astype(F32) + closing).astype(BF)

    settle(send_ref.at[pl.ds(0, n_dp - 1)], a_send)
    settle(meta_ref.at[pl.ds(0, n_dp - 1)], m_send)
    for k in range(1, nz):
        settle(zbuf_ref.at[0], bz_send.at[k])
    for i in range(1, 2 * 4):
        settle(cbuf_ref.at[0, 0], by_send.at[i])
    for part in range(2):
        for i in range(6):
            settle(piece(x, yh, part), bx_send.at[part, i])
        for i in range(NX * NY):
            settle(piece(x, yh, part), sib_send.at[part, i])
    for i in range(4):
        for j in range(3):
            settle(kv_part(ctx, i), kv_send.at[i, j])

    @pl.when(ctx > 0)
    def _():
        settle(head_rows, halo_send.at[0])

    @pl.when(ctx < 3)
    def _():
        settle(tail_rows, halo_send.at[1])


def solution(mesh):
    n_dp = mesh.shape["dp"]
    n_ctx = mesh.shape["ctx"]
    nz = n_dp // (NX * NY)

    def per_device(
        frames,
        destinations,
        segments,
        tile_mask,
        attn_gain,
        w_qkv,
        w_out,
        conv_gain,
        w_pointin,
        w_pointout,
        w_depth,
        bn_scale,
        bn_shift,
    ):
        rows, width = frames.shape[1:]
        seq = segments.shape[1]
        channels = w_depth.shape[1]
        taps = w_depth.shape[0]
        head_cols = w_out.shape[0]
        cap = 2 * rows // n_dp
        shard_rows = w_pointin.shape[0]
        pad_rows = -(-shard_rows // 8) * 8
        half_cols = channels + channels // 2
        pick = np.zeros((nz * n_ctx * shard_rows, n_ctx * nz * pad_rows), np.float32)
        for a in range(nz):
            for b in range(n_ctx):
                for j in range(shard_rows):
                    pick[(a * n_ctx + b) * shard_rows + j, (b * nz + a) * pad_rows + j] = 1.0
        pick = jnp.asarray(pick, BF)
        vmem = pl.BlockSpec(memory_space=pltpu.VMEM)
        hbm = pl.BlockSpec(memory_space=pltpu.HBM)
        operands = (
            destinations,
            frames[0],
            segments,
            tile_mask[0],
            attn_gain,
            w_qkv,
            w_out,
            conv_gain,
            w_pointin,
            w_pointout.T,
            pick,
            w_depth,
            bn_scale,
            bn_shift,
        )
        operands = tuple(pltpu.with_memory_space_constraint(a, pltpu.HBM) for a in operands)
        fetched = [i for i in range(len(operands)) if i not in (5, 6)]

        def body(*refs):
            given, out_ref, rest = list(refs[: len(operands)]), refs[len(operands)], refs[len(operands) + 1 :]
            local, sem, rest = rest[: len(fetched)], rest[len(fetched)], rest[len(fetched) + 1 :]
            fetches = []
            for j, i in enumerate(fetched):
                fetches.append(pltpu.make_async_copy(given[i], local[j], sem.at[j]))
                fetches[j].start()
                given[i] = local[j]
            layer_kernel(n_dp, shard_rows, fetches, *given, out_ref, *rest)

        dma = pltpu.SemaphoreType.DMA
        out = pl.pallas_call(
            body,
            name="conformer_layer",
            out_shape=jax.ShapeDtypeStruct((rows, width), BF),
            in_specs=[hbm] * len(operands),
            out_specs=vmem,
            scratch_shapes=[
                (pltpu.SMEM if i == 3 else pltpu.VMEM)(operands[i].shape, operands[i].dtype) for i in fetched
            ]
            + [
                pltpu.SemaphoreType.DMA((len(fetched),)),
                pltpu.VMEM(w_qkv.shape, BF),
                pltpu.VMEM(w_out.shape, BF),
                pltpu.VMEM((n_dp, cap, width), BF),
                pltpu.VMEM((n_dp, cap, width), BF),
                pltpu.VMEM((n_dp, 1, 128), F32),
                pltpu.VMEM((n_dp, 1, 128), F32),
                pltpu.VMEM((HEADS // 2, rows, seq), BF),
                pltpu.VMEM((nz, pad_rows, 2 * half_cols), BF),
                pltpu.VMEM((NY, n_ctx, nz, pad_rows, half_cols), BF),
                pltpu.VMEM((2, width, half_cols), BF),
                pltpu.VMEM((seq, 2 * head_cols), BF),
                pltpu.VMEM((rows, head_cols), BF),
                pltpu.VMEM((rows, head_cols), BF),
                pltpu.VMEM((rows, width), F32),
                pltpu.VMEM((rows, width), BF),
                pltpu.VMEM((rows, seq), F32),
                pltpu.VMEM((seq + taps, 128), F32),
                pltpu.VMEM((rows + taps, 128), F32),
                pltpu.VMEM((taps, rows, 128), F32),
                pltpu.VMEM((rows, channels), BF),
                pltpu.VMEM((taps // 2, channels), BF),
                pltpu.VMEM((taps // 2, channels), BF),
                pltpu.VMEM((rows + taps, channels), F32),
                pltpu.VMEM((rows, channels), BF),
                dma((2,)),
                dma,
                dma,
                dma,
                dma,
                dma((8,)),
                dma((8,)),
                dma((8,)),
                dma((8,)),
                dma((2, 6)),
                dma((2, 6)),
                dma((2, NX * NY)),
                dma((2, NX * NY)),
                dma((4, 3)),
                dma((4, 3)),
                dma((2,)),
                dma((2,)),
            ],
            compiler_params=pltpu.CompilerParams(
                collective_id=0, has_side_effects=True, vmem_limit_bytes=48 * 2**20
            ),
            cost_estimate=pl.CostEstimate(flops=6 * 10**9, bytes_accessed=20 * 10**6, transcendentals=3 * 10**6),
        )(*operands)

        def hand_on(src_ref, dst_ref, sem):
            copies = []
            for i in range(4):
                part = pl.ds(i * (rows // 4), rows // 4)
                copies.append(pltpu.make_async_copy(src_ref.at[part], dst_ref.at[part], sem.at[i]))
                copies[i].start()
            for copy in copies:
                copy.wait()

        out = pl.pallas_call(
            hand_on,
            name="result",
            out_shape=jax.ShapeDtypeStruct((rows, width), BF),
            in_specs=[pl.BlockSpec(memory_space=pl.ANY)],
            out_specs=pl.BlockSpec(memory_space=pl.ANY),
            scratch_shapes=[dma((4,))],
            compiler_params=pltpu.CompilerParams(vmem_limit_bytes=2**20),
        )(out)
        return out[None]

    return jax.shard_map(
        per_device,
        mesh=mesh,
        in_specs=(
            P("dp", "ctx", None),
            P("dp", "ctx"),
            P("dp", None),
            P("dp", "ctx", None),
            P(),
            P(),
            P(),
            P(),
            P(("dp", "ctx"), None),
            P(None, ("dp", "ctx")),
            P(),
            P(),
            P(),
        ),
        out_specs=P("dp", "ctx", None),
        check_vma=False,
    )
```

```python
import math

import numpy as np

import jax
import jax.numpy as jnp
from jax import lax
from jax.experimental import pallas as pl
from jax.experimental.pallas import tpu as pltpu
from jax.sharding import PartitionSpec as P

HEADS = 8
NX = 4
NY = 2
MESH = pl.DeviceIdType.MESH
BF = jnp.bfloat16
F32 = jnp.float32
MASKED = -2e38


def dot(a, b):
    return jnp.dot(a, b, preferred_element_type=F32)


def dot_nt(a, b):
    return lax.dot_general(a, b, (((1,), (1,)), ((), ())), preferred_element_type=F32)


def layer_norm(as_float, gain):
    row_mean = jnp.mean(as_float, axis=-1, keepdims=True)
    centred = as_float - row_mean
    row_var = jnp.mean(centred * centred, axis=-1, keepdims=True)
    return centred * lax.rsqrt(row_var + 1e-06) * gain


def layer_kernel(
    n_dp,
    shard_rows,
    fetches,
    dest_ref,
    frames_ref,
    seg_ref,
    tile_ref,
    again_ref,
    wqkv_hbm,
    wout_hbm,
    cgain_ref,
    pin_ref,
    pout_ref,
    pick_ref,
    wdepth_ref,
    bns_ref,
    bnb_ref,
    out_ref,
    wqkv_ref,
    wout_ref,
    send_ref,
    got_ref,
    meta_ref,
    gmeta_ref,
    prob_ref,
    zbuf_ref,
    cbuf_ref,
    wfull_ref,
    kv_ref,
    q_ref,
    att_ref,
    placed_ref,
    after_ref,
    bias_ref,
    segc_ref,
    segn_ref,
    mask_ref,
    gat_ref,
    htop_ref,
    hbot_ref,
    gf_ref,
    act_ref,
    load_sem,
    a_send,
    a_recv,
    m_send,
    m_recv,
    bz_send,
    bz_recv,
    by_send,
    by_recv,
    bx_send,
    bx_recv,
    sib_send,
    sib_recv,
    kv_send,
    kv_recv,
    halo_send,
    halo_recv,
):
    rows, width = frames_ref.shape
    seq = seg_ref.shape[1]
    nz = n_dp // (NX * NY)
    cap = send_ref.shape[1]
    head_cols = wout_ref.shape[0]
    head = head_cols // HEADS
    group = head_cols // 2
    half_cols = cbuf_ref.shape[4]
    block = wfull_ref.shape[1] // (NX * NY)
    channels = wdepth_ref.shape[1]
    taps = wdepth_ref.shape[0]
    half = taps // 2
    tile = 128

    dp = lax.axis_index("dp")
    ctx = lax.axis_index("ctx")
    x = dp // (NY * nz)
    yh = (dp // nz) % NY
    z = dp % nz
    core = ctx % 2

    def dp_of(px, py, pz):
        return (px * NY + py) * nz + pz

    def peer(i):
        zi, rest = i // (NX * NY), NX * NY - 1 - i % (NX * NY)
        kz = nz // 2 + ((zi + 1) // 2) * (1 - 2 * (zi % 2))
        return dp_of((x + rest // NY) % NX, (yh + rest % NY) % NY, (z + kz + nz) % nz)

    def put(src, dst, ssem, rsem, d, c):
        copy = pltpu.make_async_remote_copy(
            src_ref=src, dst_ref=dst, send_sem=ssem, recv_sem=rsem, device_id=(d, c), device_id_type=MESH
        )
        copy.start()

    def settle(ref, sem):
        pltpu.make_async_copy(ref, ref, sem).wait()

    barrier = pltpu.get_barrier_semaphore()

    def greet(k, carry):
        pl.semaphore_signal(barrier, inc=1, device_id=(peer(k), ctx), device_id_type=MESH)
        return carry

    lax.fori_loop(0, n_dp - 1, greet, 0)
    for d in range(1, 4):
        pl.semaphore_signal(barrier, inc=1, device_id=(dp, ctx ^ d), device_id_type=MESH)
        pl.semaphore_signal(barrier, inc=1, device_id=(dp_of(x, 1 - yh, z), ctx ^ d), device_id_type=MESH)

    load_qkv = pltpu.make_async_copy(wqkv_hbm, wqkv_ref, load_sem.at[0])
    load_qkv.start()
    load_out = pltpu.make_async_copy(wout_hbm, wout_ref, load_sem.at[1])
    load_out.start()

    for fetch in fetches:
        fetch.wait()

    zbuf_ref[pl.ds(z, 1)] = jnp.zeros((1,) + zbuf_ref.shape[1:], BF)
    for c in range(2):
        left_col = c * half_cols
        zbuf_ref[pl.ds(z, 1), :shard_rows, left_col : left_col + channels] = pin_ref[
            :, c * channels : (c + 1) * channels
        ][None]
        zbuf_ref[pl.ds(z, 1), :shard_rows, left_col + channels : left_col + half_cols] = pout_ref[
            :, c * (channels // 2) : (c + 1) * (channels // 2)
        ][None]
    pl.semaphore_wait(barrier, n_dp - 1 + 6)
    for k in range(1, nz):
        put(zbuf_ref.at[z], zbuf_ref.at[z], bz_send.at[k], bz_recv.at[k], dp_of(x, yh, (z + k) % nz), ctx)

    dest = dest_ref[...]
    owner = dest // rows
    slot = dest % rows
    oz = owner % nz
    oy = (owner // nz) % NY
    ox = owner // (nz * NY)
    dz = (oz - z + nz) % nz - nz // 2
    zi = jnp.where(dz >= 0, 2 * dz, -2 * dz - 1)
    rel = (zi + 1) * (NX * NY) - 1 - (((ox - x + NX) % NX) * NY + (oy - yh + NY) % NY)
    rel_wide = jnp.broadcast_to(rel.astype(F32), (rows, rows))
    rel_tall = jnp.transpose(rel_wide)
    earlier = lax.broadcasted_iota(jnp.int32, (rows, rows), 0) < lax.broadcasted_iota(jnp.int32, (rows, rows), 1)
    rank = jnp.sum(jnp.where((rel_tall == rel_wide) & earlier, 1.0, 0.0), axis=0, keepdims=True)
    pos = rel * cap + rank.astype(jnp.int32)
    frames = frames_ref[...]
    per = n_dp // 4

    def pack(c):
        chunk = lax.broadcasted_iota(jnp.int32, (per * cap, rows), 0) + c * per * cap
        onehot = jnp.where(chunk == pos, 1.0, 0.0).astype(BF)
        send_ref[c * per : (c + 1) * per] = dot(onehot, frames).reshape(per, cap, width).astype(BF)

    def ship(i, carry):
        put(send_ref.at[i], got_ref.at[i], a_send, a_recv, peer(i), ctx)
        put(meta_ref.at[i], gmeta_ref.at[i], m_send, m_recv, peer(i), ctx)
        return carry

    def piece(px, py, part):
        start = pl.multiple_of((((px + NX) % NX) * NY + py) * block, 16)
        cols = pl.ds(0, channels) if part == 0 else pl.ds(channels, half_cols - channels)
        return wfull_ref.at[core, pl.ds(start, block), cols]

    right = dp_of((x + 1) % NX, yh, z)
    left = dp_of((x + NX - 1) % NX, yh, z)
    other = 1 - yh

    def to_sibling(i, px, py, part):
        ref = piece(px, py, part)
        put(ref, ref, sib_send.at[part, i], sib_recv.at[part, i], dp, ctx ^ 1)

    def to_x(i, px, py, part, d):
        ref = piece(px, py, part)
        put(ref, ref, bx_send.at[part, i], bx_recv.at[part, i], d, ctx)

    def own_to_x(part):
        to_x(0, x, yh, part, right)
        to_x(1, x, yh, part, left)

    def pair_to_x(part):
        to_x(2, x, other, part, right)
        to_x(3, x, other, part, left)

    def hand_right(part):
        settle(piece(x - 1, yh, part), bx_recv.at[part, 0])
        settle(piece(x + 1, yh, part), bx_recv.at[part, 1])
        to_x(4, x - 1, yh, part, right)
        to_sibling(2, x - 1, yh, part)
        to_sibling(3, x + 1, yh, part)

    def hand_left(part):
        settle(piece(x - 1, other, part), bx_recv.at[part, 2])
        settle(piece(x + 1, other, part), bx_recv.at[part, 3])
        to_x(5, x + 1, other, part, left)
        to_sibling(4, x - 1, other, part)
        to_sibling(5, x + 1, other, part)

    def two_away(part):
        settle(piece(x + 2, yh, part), bx_recv.at[part, 4])
        to_sibling(6, x + 2, yh, part)
        settle(piece(x + 2, other, part), bx_recv.at[part, 5])
        to_sibling(7, x + 2, other, part)

    def from_sibling(part):
        for i in range(NX * NY):
            settle(piece(x, yh, part), sib_recv.at[part, i])

    pack(3)
    rank_tall = jnp.transpose(jnp.broadcast_to(rank, (tile, rows)))
    slot_tall = jnp.transpose(jnp.broadcast_to(slot.astype(F32) + 1.0, (tile, rows)))
    lane = lax.broadcasted_iota(jnp.int32, (rows, tile), 1).astype(F32)
    at_rank = jnp.where(rank_tall == lane, slot_tall, 0.0).astype(BF)
    to_peer = jnp.where(lax.broadcasted_iota(jnp.int32, (n_dp, rows), 0) == rel, 1.0, 0.0).astype(BF)
    meta_ref[...] = dot(to_peer, at_rank).reshape(n_dp, 1, tile)
    lax.fori_loop(3 * per, n_dp - 1, ship, 0)
    pack(0)
    pack(1)
    for k in range(1, nz):
        settle(zbuf_ref.at[0], bz_recv.at[k])
    for i in range(1, 2 * 4):
        d, far = i // 2, i % 2
        cols = pl.ds(pl.multiple_of(((ctx ^ d) % 2) * half_cols, 128), half_cols)
        to_yh = other if far else yh
        put(zbuf_ref.at[:, :, cols], cbuf_ref.at[yh, ctx], by_send.at[i], by_recv.at[i], dp_of(x, to_yh, z), ctx ^ d)
    lax.fori_loop(0, 3 * n_dp // 8, ship, 0)
    mine = pl.ds(pl.multiple_of(core * half_cols, 128), half_cols)
    cbuf_ref[yh, pl.ds(ctx, 1)] = zbuf_ref[:, :, mine][None]
    pack(2)
    lax.fori_loop(3 * n_dp // 8, 3 * per, ship, 0)
    for i in range(1, 2 * 4):
        settle(cbuf_ref.at[0, 0], by_recv.at[i])
    for y in range(NY):
        padded = cbuf_ref[y].astype(F32).reshape(pick_ref.shape[1], half_cols).astype(BF)
        start = pl.multiple_of((x * NY + y) * block, 16)
        wfull_ref[core, pl.ds(start, block)] = dot(pick_ref[...], padded).astype(BF)
    own_to_x(0)
    pair_to_x(0)
    own_to_x(1)
    pair_to_x(1)
    for part in range(2):
        to_sibling(0, x, yh, part)
        to_sibling(1, x, other, part)
    got_ref[n_dp - 1] = send_ref[n_dp - 1]
    gmeta_ref[n_dp - 1] = meta_ref[n_dp - 1]

    segf = seg_ref[...].astype(F32)
    segc_ref[0:half] = jnp.full((half, tile), -1.0, F32)
    segc_ref[half + seq :] = jnp.full((half, tile), -1.0, F32)
    segc_ref[half : half + seq] = jnp.transpose(jnp.broadcast_to(segf, (tile, seq)))
    first = pl.multiple_of(ctx * rows, rows)
    segn_ref[...] = segc_ref[pl.ds(first, rows + 2 * half)]
    own_seg = segn_ref[half : half + rows]
    for tk in range(seq // tile):
        same = own_seg == segf[:, tk * tile : (tk + 1) * tile]
        for tq in range(rows // tile):
            off = (1 - tile_ref[tq, tk]).astype(F32) * MASKED
            bias_ref[tq * tile : (tq + 1) * tile, tk * tile : (tk + 1) * tile] = jnp.where(
                same[tq * tile : (tq + 1) * tile], off, MASKED
            )
    for k in range(taps):
        mask_ref[k] = jnp.where(segn_ref[k : k + rows] == own_seg, 1.0, 0.0)

    settle(gmeta_ref.at[pl.ds(0, n_dp - 1)], m_recv)
    spots = n_dp * cap
    spot = lax.broadcasted_iota(jnp.int32, (tile, spots), 1)
    spread = jnp.where(lax.broadcasted_iota(jnp.int32, (tile, spots), 0) == spot % cap, 1.0, 0.0).astype(BF)
    spread = dot(gmeta_ref[...].reshape(n_dp, tile).astype(BF), spread)
    spot = lax.broadcasted_iota(jnp.int32, (n_dp, spots), 1)
    from_peer = lax.broadcasted_iota(jnp.int32, (n_dp, spots), 0) == spot // cap
    slots = jnp.sum(jnp.where(from_peer, spread, 0.0), axis=0, keepdims=True)
    lane = lax.broadcasted_iota(jnp.int32, (rows, spots), 0).astype(F32) + 1.0
    place = jnp.where(lane == slots, 1.0, 0.0).astype(BF)
    settle(got_ref.at[pl.ds(0, n_dp - 1)], a_recv)
    got = got_ref[...].astype(F32).reshape(spots, width).astype(BF)
    placed = dot(place, got)
    placed_ref[...] = placed
    normed = layer_norm(placed, again_ref[...][None]).astype(BF)

    load_qkv.wait()
    base = pl.multiple_of(ctx * rows, rows)
    keys = dot(normed, wqkv_ref[:, head_cols : 2 * head_cols]).astype(BF)
    values = dot(normed, wqkv_ref[:, 2 * head_cols :]).astype(BF)
    for g in range(2):
        kv_ref[pl.ds(base, rows), 2 * g * group : (2 * g + 1) * group] = keys[:, g * group : (g + 1) * group]
        kv_ref[pl.ds(base, rows), (2 * g + 1) * group : (2 * g + 2) * group] = values[:, g * group : (g + 1) * group]

    def kv_part(c, i):
        return kv_ref.at[pl.ds(pl.multiple_of(c * rows, rows), rows), pl.ds(i * group, group)]

    for i in range(4):
        part = kv_part(ctx, i)
        put(part, part, kv_send.at[i, 0], kv_recv.at[i, 0], dp, ctx ^ 2)
        put(part, part, kv_send.at[i, 1], kv_recv.at[i, 1], dp, ctx ^ 1)
    scale = math.log2(math.e) / math.sqrt(head)
    q_ref[...] = (dot(normed, wqkv_ref[:, :head_cols]) * scale).astype(BF)

    def arrive(i):
        part = kv_part(ctx ^ 2, i)
        settle(part, kv_recv.at[i, 0])
        put(part, part, kv_send.at[i, 2], kv_recv.at[i, 2], dp, ctx ^ 1)
        settle(part, kv_recv.at[i, 1])
        settle(part, kv_recv.at[i, 2])

    def windows(h):
        lo, hi = h * head, (h + 1) * head
        c0, c1 = lo // tile * tile, (hi + tile - 1) // tile * tile
        lanes = lax.broadcasted_iota(jnp.int32, (rows, c1 - c0), 1) + c0
        return c0, c1, (lanes >= lo) & (lanes < hi)

    def score(g):
        totals = []
        for h in range(HEADS // 2):
            c0, c1, inside = windows(h)
            query = q_ref[:, g * group + c0 : g * group + c1].astype(F32)
            query = jnp.where(inside, query, 0.0).astype(BF)
            scores = dot_nt(query, kv_ref[:, 2 * g * group + c0 : 2 * g * group + c1]) + bias_ref[...]
            weights = jnp.exp2(scores - jnp.max(scores, axis=1, keepdims=True))
            totals.append(jnp.sum(weights, axis=1, keepdims=True))
            prob_ref[h] = weights.astype(BF)
        return totals

    def mix(g, totals):
        tiles = [None] * (group // tile)
        for h in range(HEADS // 2):
            c0, c1, inside = windows(h)
            mixed = dot(prob_ref[h], kv_ref[:, (2 * g + 1) * group + c0 : (2 * g + 1) * group + c1])
            mixed = jnp.where(inside, mixed / totals[h], 0.0)
            for t in range(c0 // tile, c1 // tile):
                term = mixed[:, t * tile - c0 : (t + 1) * tile - c0]
                tiles[t] = term if tiles[t] is None else tiles[t] + term
        for t, whole in enumerate(tiles):
            att_ref[:, g * group + t * tile : g * group + (t + 1) * tile] = whole.astype(BF)

    arrive(0)
    totals = score(0)
    hand_right(0)
    hand_left(0)
    arrive(1)
    mix(0, totals)
    hand_right(1)
    hand_left(1)
    arrive(2)
    totals = score(1)
    arrive(3)
    mix(1, totals)

    load_out.wait()
    after = (placed_ref[...] + dot(att_ref[...], wout_ref[...])).astype(BF)
    after_ref[...] = after
    conv_normed = layer_norm(after.astype(F32), cgain_ref[...][None]).astype(BF)

    two_away(0)
    near = dot(conv_normed, wfull_ref[core, :, :channels])
    from_sibling(0)
    far = dot(conv_normed, wfull_ref[1 - core, :, :channels])
    gated = (jnp.where(core == 0, near, far) * jax.nn.sigmoid(jnp.where(core == 0, far, near))).astype(BF)
    gat_ref[...] = gated
    gf_ref[half : half + rows] = gated.astype(F32)

    head_rows = gat_ref.at[0:half]
    tail_rows = gat_ref.at[rows - half : rows]

    @pl.when(ctx > 0)
    def _():
        put(head_rows, hbot_ref, halo_send.at[0], halo_recv.at[0], dp, ctx - 1)

    @pl.when(ctx < 3)
    def _():
        put(tail_rows, htop_ref, halo_send.at[1], halo_recv.at[1], dp, ctx + 1)

    @pl.when(ctx == 0)
    def _():
        htop_ref[...] = jnp.zeros_like(htop_ref)

    @pl.when(ctx == 3)
    def _():
        hbot_ref[...] = jnp.zeros_like(hbot_ref)

    span = 64

    def convolve(r0):
        def body(t, carry):
            lanes = pl.ds(pl.multiple_of(t * tile, tile), tile)
            near = gf_ref[r0 : r0 + span + 2 * half, lanes]
            total = jnp.zeros((span, tile), F32)
            for b in range(8):
                shifted = near if b == 0 else pltpu.roll(near, span + 2 * half - b, 0)
                for a in range(taps // 8):
                    k = 8 * a + b
                    term = shifted[8 * a : 8 * a + span] * mask_ref[k, r0 : r0 + span]
                    total = total + term * wdepth_ref[k : k + 1, lanes]
            moved = total * bns_ref[lanes][None] + bnb_ref[lanes][None]
            act_ref[r0 : r0 + span, lanes] = (moved * jax.nn.sigmoid(moved)).astype(BF)
            return carry

        lax.fori_loop(0, channels // tile, body, 0)

    for r0 in range(span, rows - span, span):
        convolve(r0)

    two_away(1)

    @pl.when(ctx > 0)
    def _():
        settle(htop_ref, halo_recv.at[1])

    @pl.when(ctx < 3)
    def _():
        settle(hbot_ref, halo_recv.at[0])

    gf_ref[0:half] = htop_ref[...].astype(F32)
    gf_ref[half + rows :] = hbot_ref[...].astype(F32)
    convolve(0)
    convolve(rows - span)

    quarter = channels // 2

    def close(c):
        lanes = pl.ds(pl.multiple_of(c * quarter, 128), quarter)
        return dot_nt(act_ref[:, lanes], wfull_ref[c, :, channels:])

    closing = close(core)
    from_sibling(1)
    closing = closing + close(1 - core)
    out_ref[...] = (after_ref[...].astype(F32) + closing).astype(BF)

    settle(send_ref.at[pl.ds(0, n_dp - 1)], a_send)
    settle(meta_ref.at[pl.ds(0, n_dp - 1)], m_send)
    for k in range(1, nz):
        settle(zbuf_ref.at[0], bz_send.at[k])
    for i in range(1, 2 * 4):
        settle(cbuf_ref.at[0, 0], by_send.at[i])
    for part in range(2):
        for i in range(6):
            settle(piece(x, yh, part), bx_send.at[part, i])
        for i in range(NX * NY):
            settle(piece(x, yh, part), sib_send.at[part, i])
    for i in range(4):
        for j in range(3):
            settle(kv_part(ctx, i), kv_send.at[i, j])

    @pl.when(ctx > 0)
    def _():
        settle(head_rows, halo_send.at[0])

    @pl.when(ctx < 3)
    def _():
        settle(tail_rows, halo_send.at[1])


def solution(mesh):
    n_dp = mesh.shape["dp"]
    n_ctx = mesh.shape["ctx"]
    nz = n_dp // (NX * NY)

    def per_device(
        frames,
        destinations,
        segments,
        tile_mask,
        attn_gain,
        w_qkv,
        w_out,
        conv_gain,
        w_pointin,
        w_pointout,
        w_depth,
        bn_scale,
        bn_shift,
    ):
        rows, width = frames.shape[1:]
        seq = segments.shape[1]
        channels = w_depth.shape[1]
        taps = w_depth.shape[0]
        head_cols = w_out.shape[0]
        cap = 2 * rows // n_dp
        shard_rows = w_pointin.shape[0]
        pad_rows = -(-shard_rows // 8) * 8
        half_cols = channels + channels // 2
        pick = np.zeros((nz * n_ctx * shard_rows, n_ctx * nz * pad_rows), np.float32)
        for a in range(nz):
            for b in range(n_ctx):
                for j in range(shard_rows):
                    pick[(a * n_ctx + b) * shard_rows + j, (b * nz + a) * pad_rows + j] = 1.0
        pick = jnp.asarray(pick, BF)
        vmem = pl.BlockSpec(memory_space=pltpu.VMEM)
        hbm = pl.BlockSpec(memory_space=pltpu.HBM)
        operands = (
            destinations,
            frames[0],
            segments,
            tile_mask[0],
            attn_gain,
            w_qkv,
            w_out,
            conv_gain,
            w_pointin,
            w_pointout.T,
            pick,
            w_depth,
            bn_scale,
            bn_shift,
        )
        operands = tuple(pltpu.with_memory_space_constraint(a, pltpu.HBM) for a in operands)
        fetched = [i for i in range(len(operands)) if i not in (5, 6)]

        def body(*refs):
            given, out_ref, rest = list(refs[: len(operands)]), refs[len(operands)], refs[len(operands) + 1 :]
            local, sem, rest = rest[: len(fetched)], rest[len(fetched)], rest[len(fetched) + 1 :]
            fetches = []
            for j, i in enumerate(fetched):
                fetches.append(pltpu.make_async_copy(given[i], local[j], sem.at[j]))
                fetches[j].start()
                given[i] = local[j]
            layer_kernel(n_dp, shard_rows, fetches, *given, out_ref, *rest)

        dma = pltpu.SemaphoreType.DMA
        out = pl.pallas_call(
            body,
            name="conformer_layer",
            out_shape=jax.ShapeDtypeStruct((rows, width), BF),
            in_specs=[hbm] * len(operands),
            out_specs=vmem,
            scratch_shapes=[
                (pltpu.SMEM if i == 3 else pltpu.VMEM)(operands[i].shape, operands[i].dtype) for i in fetched
            ]
            + [
                pltpu.SemaphoreType.DMA((len(fetched),)),
                pltpu.VMEM(w_qkv.shape, BF),
                pltpu.VMEM(w_out.shape, BF),
                pltpu.VMEM((n_dp, cap, width), BF),
                pltpu.VMEM((n_dp, cap, width), BF),
                pltpu.VMEM((n_dp, 1, 128), F32),
                pltpu.VMEM((n_dp, 1, 128), F32),
                pltpu.VMEM((HEADS // 2, rows, seq), BF),
                pltpu.VMEM((nz, pad_rows, 2 * half_cols), BF),
                pltpu.VMEM((NY, n_ctx, nz, pad_rows, half_cols), BF),
                pltpu.VMEM((2, width, half_cols), BF),
                pltpu.VMEM((seq, 2 * head_cols), BF),
                pltpu.VMEM((rows, head_cols), BF),
                pltpu.VMEM((rows, head_cols), BF),
                pltpu.VMEM((rows, width), F32),
                pltpu.VMEM((rows, width), BF),
                pltpu.VMEM((rows, seq), F32),
                pltpu.VMEM((seq + taps, 128), F32),
                pltpu.VMEM((rows + taps, 128), F32),
                pltpu.VMEM((taps, rows, 128), F32),
                pltpu.VMEM((rows, channels), BF),
                pltpu.VMEM((taps // 2, channels), BF),
                pltpu.VMEM((taps // 2, channels), BF),
                pltpu.VMEM((rows + taps, channels), F32),
                pltpu.VMEM((rows, channels), BF),
                dma((2,)),
                dma,
                dma,
                dma,
                dma,
                dma((8,)),
                dma((8,)),
                dma((8,)),
                dma((8,)),
                dma((2, 6)),
                dma((2, 6)),
                dma((2, NX * NY)),
                dma((2, NX * NY)),
                dma((4, 3)),
                dma((4, 3)),
                dma((2,)),
                dma((2,)),
            ],
            compiler_params=pltpu.CompilerParams(
                collective_id=0, has_side_effects=True, vmem_limit_bytes=48 * 2**20
            ),
            cost_estimate=pl.CostEstimate(flops=6 * 10**9, bytes_accessed=20 * 10**6, transcendentals=3 * 10**6),
        )(*operands)

        def hand_on(src_ref, dst_ref, sem):
            copies = []
            for i in range(4):
                part = pl.ds(i * (rows // 4), rows // 4)
                copies.append(pltpu.make_async_copy(src_ref.at[part], dst_ref.at[part], sem.at[i]))
                copies[i].start()
            for copy in copies:
                copy.wait()

        out = pl.pallas_call(
            hand_on,
            name="result",
            out_shape=jax.ShapeDtypeStruct((rows, width), BF),
            in_specs=[pl.BlockSpec(memory_space=pl.ANY)],
            out_specs=pl.BlockSpec(memory_space=pl.ANY),
            scratch_shapes=[dma((4,))],
            compiler_params=pltpu.CompilerParams(vmem_limit_bytes=2**20),
        )(out)
        return out[None]

    return jax.shard_map(
        per_device,
        mesh=mesh,
        in_specs=(
            P("dp", "ctx", None),
            P("dp", "ctx"),
            P("dp", None),
            P("dp", "ctx", None),
            P(),
            P(),
            P(),
            P(),
            P(("dp", "ctx"), None),
            P(None, ("dp", "ctx")),
            P(),
            P(),
            P(),
        ),
        out_specs=P("dp", "ctx", None),
        check_vma=False,
    )
```

```python
import math

import numpy as np

import jax
import jax.numpy as jnp
from jax import lax
from jax.experimental import pallas as pl
from jax.experimental.pallas import tpu as pltpu
from jax.sharding import PartitionSpec as P

HEADS = 8
NX = 4
NY = 2
MESH = pl.DeviceIdType.MESH
BF = jnp.bfloat16
F32 = jnp.float32
MASKED = -2e38


def dot(a, b):
    return jnp.dot(a, b, preferred_element_type=F32)


def dot_nt(a, b):
    return lax.dot_general(a, b, (((1,), (1,)), ((), ())), preferred_element_type=F32)


def layer_norm(as_float, gain):
    row_mean = jnp.mean(as_float, axis=-1, keepdims=True)
    centred = as_float - row_mean
    row_var = jnp.mean(centred * centred, axis=-1, keepdims=True)
    return centred * lax.rsqrt(row_var + 1e-06) * gain


def layer_kernel(
    n_dp,
    shard_rows,
    fetches,
    dest_ref,
    frames_ref,
    seg_ref,
    tile_ref,
    again_ref,
    wqkv_hbm,
    wout_hbm,
    cgain_ref,
    pin_ref,
    pout_ref,
    pick_ref,
    wdepth_ref,
    bns_ref,
    bnb_ref,
    out_ref,
    wqkv_ref,
    wout_ref,
    send_ref,
    got_ref,
    meta_ref,
    gmeta_ref,
    prob_ref,
    zbuf_ref,
    cbuf_ref,
    wfull_ref,
    kv_ref,
    q_ref,
    att_ref,
    placed_ref,
    after_ref,
    bias_ref,
    segc_ref,
    segn_ref,
    mask_ref,
    gat_ref,
    htop_ref,
    hbot_ref,
    gf_ref,
    act_ref,
    load_sem,
    a_send,
    a_recv,
    m_send,
    m_recv,
    bz_send,
    bz_recv,
    by_send,
    by_recv,
    bx_send,
    bx_recv,
    sib_send,
    sib_recv,
    kv_send,
    kv_recv,
    halo_send,
    halo_recv,
):
    rows, width = frames_ref.shape
    seq = seg_ref.shape[1]
    nz = n_dp // (NX * NY)
    cap = send_ref.shape[1]
    head_cols = wout_ref.shape[0]
    head = head_cols // HEADS
    group = head_cols // 2
    half_cols = cbuf_ref.shape[4]
    block = wfull_ref.shape[1] // (NX * NY)
    channels = wdepth_ref.shape[1]
    taps = wdepth_ref.shape[0]
    half = taps // 2
    tile = 128

    dp = lax.axis_index("dp")
    ctx = lax.axis_index("ctx")
    x = dp // (NY * nz)
    yh = (dp // nz) % NY
    z = dp % nz
    core = ctx % 2

    def dp_of(px, py, pz):
        return (px * NY + py) * nz + pz

    def peer(i):
        zi, rest = i // (NX * NY), NX * NY - 1 - i % (NX * NY)
        kz = nz // 2 + ((zi + 1) // 2) * (1 - 2 * (zi % 2))
        return dp_of((x + rest // NY) % NX, (yh + rest % NY) % NY, (z + kz + nz) % nz)

    def put(src, dst, ssem, rsem, d, c):
        copy = pltpu.make_async_remote_copy(
            src_ref=src, dst_ref=dst, send_sem=ssem, recv_sem=rsem, device_id=(d, c), device_id_type=MESH
        )
        copy.start()

    def settle(ref, sem):
        pltpu.make_async_copy(ref, ref, sem).wait()

    barrier = pltpu.get_barrier_semaphore()

    def greet(k, carry):
        pl.semaphore_signal(barrier, inc=1, device_id=(peer(k), ctx), device_id_type=MESH)
        return carry

    lax.fori_loop(0, n_dp - 1, greet, 0)
    for d in range(1, 4):
        pl.semaphore_signal(barrier, inc=1, device_id=(dp, ctx ^ d), device_id_type=MESH)
        pl.semaphore_signal(barrier, inc=1, device_id=(dp_of(x, 1 - yh, z), ctx ^ d), device_id_type=MESH)

    load_qkv = pltpu.make_async_copy(wqkv_hbm, wqkv_ref, load_sem.at[0])
    load_qkv.start()
    load_out = pltpu.make_async_copy(wout_hbm, wout_ref, load_sem.at[1])
    load_out.start()

    for fetch in fetches:
        fetch.wait()

    zbuf_ref[pl.ds(z, 1)] = jnp.zeros((1,) + zbuf_ref.shape[1:], BF)
    for c in range(2):
        left_col = c * half_cols
        zbuf_ref[pl.ds(z, 1), :shard_rows, left_col : left_col + channels] = pin_ref[
            :, c * channels : (c + 1) * channels
        ][None]
        zbuf_ref[pl.ds(z, 1), :shard_rows, left_col + channels : left_col + half_cols] = pout_ref[
            :, c * (channels // 2) : (c + 1) * (channels // 2)
        ][None]
    pl.semaphore_wait(barrier, n_dp - 1 + 6)
    for k in range(1, nz):
        put(zbuf_ref.at[z], zbuf_ref.at[z], bz_send.at[k], bz_recv.at[k], dp_of(x, yh, (z + k) % nz), ctx)

    dest = dest_ref[...]
    owner = dest // rows
    slot = dest % rows
    oz = owner % nz
    oy = (owner // nz) % NY
    ox = owner // (nz * NY)
    dz = (oz - z + nz) % nz - nz // 2
    zi = jnp.where(dz >= 0, 2 * dz, -2 * dz - 1)
    rel = (zi + 1) * (NX * NY) - 1 - (((ox - x + NX) % NX) * NY + (oy - yh + NY) % NY)
    rel_wide = jnp.broadcast_to(rel.astype(F32), (rows, rows))
    rel_tall = jnp.transpose(rel_wide)
    earlier = lax.broadcasted_iota(jnp.int32, (rows, rows), 0) < lax.broadcasted_iota(jnp.int32, (rows, rows), 1)
    rank = jnp.sum(jnp.where((rel_tall == rel_wide) & earlier, 1.0, 0.0), axis=0, keepdims=True)
    pos = rel * cap + rank.astype(jnp.int32)
    frames = frames_ref[...]
    per = n_dp // 4

    def pack(c):
        chunk = lax.broadcasted_iota(jnp.int32, (per * cap, rows), 0) + c * per * cap
        onehot = jnp.where(chunk == pos, 1.0, 0.0).astype(BF)
        send_ref[c * per : (c + 1) * per] = dot(onehot, frames).reshape(per, cap, width).astype(BF)

    def ship(i, carry):
        put(send_ref.at[i], got_ref.at[i], a_send, a_recv, peer(i), ctx)
        put(meta_ref.at[i], gmeta_ref.at[i], m_send, m_recv, peer(i), ctx)
        return carry

    def piece(px, py, part):
        start = pl.multiple_of((((px + NX) % NX) * NY + py) * block, 16)
        cols = pl.ds(0, channels) if part == 0 else pl.ds(channels, half_cols - channels)
        return wfull_ref.at[core, pl.ds(start, block), cols]

    right = dp_of((x + 1) % NX, yh, z)
    left = dp_of((x + NX - 1) % NX, yh, z)
    other = 1 - yh

    def to_sibling(i, px, py, part):
        ref = piece(px, py, part)
        put(ref, ref, sib_send.at[part, i], sib_recv.at[part, i], dp, ctx ^ 1)

    def to_x(i, px, py, part, d):
        ref = piece(px, py, part)
        put(ref, ref, bx_send.at[part, i], bx_recv.at[part, i], d, ctx)

    def own_to_x(part):
        to_x(0, x, yh, part, right)
        to_x(1, x, yh, part, left)

    def pair_to_x(part):
        to_x(2, x, other, part, right)
        to_x(3, x, other, part, left)

    def hand_right(part):
        settle(piece(x - 1, yh, part), bx_recv.at[part, 0])
        settle(piece(x + 1, yh, part), bx_recv.at[part, 1])
        to_x(4, x - 1, yh, part, right)
        to_sibling(2, x - 1, yh, part)
        to_sibling(3, x + 1, yh, part)

    def hand_left(part):
        settle(piece(x - 1, other, part), bx_recv.at[part, 2])
        settle(piece(x + 1, other, part), bx_recv.at[part, 3])
        to_x(5, x + 1, other, part, left)
        to_sibling(4, x - 1, other, part)
        to_sibling(5, x + 1, other, part)

    def two_away(part):
        settle(piece(x + 2, yh, part), bx_recv.at[part, 4])
        to_sibling(6, x + 2, yh, part)
        settle(piece(x + 2, other, part), bx_recv.at[part, 5])
        to_sibling(7, x + 2, other, part)

    def from_sibling(part):
        for i in range(NX * NY):
            settle(piece(x, yh, part), sib_recv.at[part, i])

    pack(3)
    rank_tall = jnp.transpose(jnp.broadcast_to(rank, (tile, rows)))
    slot_tall = jnp.transpose(jnp.broadcast_to(slot.astype(F32) + 1.0, (tile, rows)))
    lane = lax.broadcasted_iota(jnp.int32, (rows, tile), 1).astype(F32)
    at_rank = jnp.where(rank_tall == lane, slot_tall, 0.0).astype(BF)
    to_peer = jnp.where(lax.broadcasted_iota(jnp.int32, (n_dp, rows), 0) == rel, 1.0, 0.0).astype(BF)
    meta_ref[...] = dot(to_peer, at_rank).reshape(n_dp, 1, tile)
    lax.fori_loop(3 * per, n_dp - 1, ship, 0)
    pack(0)
    pack(1)
    for k in range(1, nz):
        settle(zbuf_ref.at[0], bz_recv.at[k])
    for i in range(1, 2 * 4):
        d, far = i // 2, i % 2
        cols = pl.ds(pl.multiple_of(((ctx ^ d) % 2) * half_cols, 128), half_cols)
        to_yh = other if far else yh
        put(zbuf_ref.at[:, :, cols], cbuf_ref.at[yh, ctx], by_send.at[i], by_recv.at[i], dp_of(x, to_yh, z), ctx ^ d)
    lax.fori_loop(0, 3 * n_dp // 8, ship, 0)
    mine = pl.ds(pl.multiple_of(core * half_cols, 128), half_cols)
    cbuf_ref[yh, pl.ds(ctx, 1)] = zbuf_ref[:, :, mine][None]
    pack(2)
    lax.fori_loop(3 * n_dp // 8, 3 * per, ship, 0)
    for i in range(1, 2 * 4):
        settle(cbuf_ref.at[0, 0], by_recv.at[i])
    for y in range(NY):
        padded = cbuf_ref[y].astype(F32).reshape(pick_ref.shape[1], half_cols).astype(BF)
        start = pl.multiple_of((x * NY + y) * block, 16)
        wfull_ref[core, pl.ds(start, block)] = dot(pick_ref[...], padded).astype(BF)
    own_to_x(0)
    pair_to_x(0)
    own_to_x(1)
    pair_to_x(1)
    for part in range(2):
        to_sibling(0, x, yh, part)
        to_sibling(1, x, other, part)
    got_ref[n_dp - 1] = send_ref[n_dp - 1]
    gmeta_ref[n_dp - 1] = meta_ref[n_dp - 1]

    segf = seg_ref[...].astype(F32)
    segc_ref[0:half] = jnp.full((half, tile), -1.0, F32)
    segc_ref[half + seq :] = jnp.full((half, tile), -1.0, F32)
    segc_ref[half : half + seq] = jnp.transpose(jnp.broadcast_to(segf, (tile, seq)))
    first = pl.multiple_of(ctx * rows, rows)
    segn_ref[...] = segc_ref[pl.ds(first, rows + 2 * half)]
    own_seg = segn_ref[half : half + rows]
    for tk in range(seq // tile):
        same = own_seg == segf[:, tk * tile : (tk + 1) * tile]
        for tq in range(rows // tile):
            off = (1 - tile_ref[tq, tk]).astype(F32) * MASKED
            bias_ref[tq * tile : (tq + 1) * tile, tk * tile : (tk + 1) * tile] = jnp.where(
                same[tq * tile : (tq + 1) * tile], off, MASKED
            )
    for k in range(taps):
        mask_ref[k] = jnp.where(segn_ref[k : k + rows] == own_seg, 1.0, 0.0)

    settle(gmeta_ref.at[pl.ds(0, n_dp - 1)], m_recv)
    spots = n_dp * cap
    spot = lax.broadcasted_iota(jnp.int32, (tile, spots), 1)
    spread = jnp.where(lax.broadcasted_iota(jnp.int32, (tile, spots), 0) == spot % cap, 1.0, 0.0).astype(BF)
    spread = dot(gmeta_ref[...].reshape(n_dp, tile).astype(BF), spread)
    spot = lax.broadcasted_iota(jnp.int32, (n_dp, spots), 1)
    from_peer = lax.broadcasted_iota(jnp.int32, (n_dp, spots), 0) == spot // cap
    slots = jnp.sum(jnp.where(from_peer, spread, 0.0), axis=0, keepdims=True)
    lane = lax.broadcasted_iota(jnp.int32, (rows, spots), 0).astype(F32) + 1.0
    place = jnp.where(lane == slots, 1.0, 0.0).astype(BF)
    settle(got_ref.at[pl.ds(0, n_dp - 1)], a_recv)
    got = got_ref[...].astype(F32).reshape(spots, width).astype(BF)
    placed = dot(place, got)
    placed_ref[...] = placed
    normed = layer_norm(placed, again_ref[...][None]).astype(BF)

    load_qkv.wait()
    base = pl.multiple_of(ctx * rows, rows)
    keys = dot(normed, wqkv_ref[:, head_cols : 2 * head_cols]).astype(BF)
    values = dot(normed, wqkv_ref[:, 2 * head_cols :]).astype(BF)
    for g in range(2):
        kv_ref[pl.ds(base, rows), 2 * g * group : (2 * g + 1) * group] = keys[:, g * group : (g + 1) * group]
        kv_ref[pl.ds(base, rows), (2 * g + 1) * group : (2 * g + 2) * group] = values[:, g * group : (g + 1) * group]

    def kv_part(c, i):
        return kv_ref.at[pl.ds(pl.multiple_of(c * rows, rows), rows), pl.ds(i * group, group)]

    for i in range(4):
        part = kv_part(ctx, i)
        put(part, part, kv_send.at[i, 0], kv_recv.at[i, 0], dp, ctx ^ 2)
        put(part, part, kv_send.at[i, 1], kv_recv.at[i, 1], dp, ctx ^ 1)
    scale = math.log2(math.e) / math.sqrt(head)
    q_ref[...] = (dot(normed, wqkv_ref[:, :head_cols]) * scale).astype(BF)

    def arrive(i):
        part = kv_part(ctx ^ 2, i)
        settle(part, kv_recv.at[i, 0])
        put(part, part, kv_send.at[i, 2], kv_recv.at[i, 2], dp, ctx ^ 1)
        settle(part, kv_recv.at[i, 1])
        settle(part, kv_recv.at[i, 2])

    def windows(h):
        lo, hi = h * head, (h + 1) * head
        c0, c1 = lo // tile * tile, (hi + tile - 1) // tile * tile
        lanes = lax.broadcasted_iota(jnp.int32, (rows, c1 - c0), 1) + c0
        return c0, c1, (lanes >= lo) & (lanes < hi)

    def score(g):
        totals = []
        for h in range(HEADS // 2):
            c0, c1, inside = windows(h)
            query = q_ref[:, g * group + c0 : g * group + c1].astype(F32)
            query = jnp.where(inside, query, 0.0).astype(BF)
            scores = dot_nt(query, kv_ref[:, 2 * g * group + c0 : 2 * g * group + c1]) + bias_ref[...]
            weights = jnp.exp2(scores - jnp.max(scores, axis=1, keepdims=True))
            totals.append(jnp.sum(weights, axis=1, keepdims=True))
            prob_ref[h] = weights.astype(BF)
        return totals

    def mix(g, totals):
        tiles = [None] * (group // tile)
        for h in range(HEADS // 2):
            c0, c1, inside = windows(h)
            mixed = dot(prob_ref[h], kv_ref[:, (2 * g + 1) * group + c0 : (2 * g + 1) * group + c1])
            mixed = jnp.where(inside, mixed / totals[h], 0.0)
            for t in range(c0 // tile, c1 // tile):
                term = mixed[:, t * tile - c0 : (t + 1) * tile - c0]
                tiles[t] = term if tiles[t] is None else tiles[t] + term
        for t, whole in enumerate(tiles):
            att_ref[:, g * group + t * tile : g * group + (t + 1) * tile] = whole.astype(BF)

    arrive(0)
    totals = score(0)
    hand_right(0)
    hand_left(0)
    arrive(1)
    mix(0, totals)
    arrive(2)
    totals = score(1)
    hand_right(1)
    hand_left(1)
    arrive(3)
    mix(1, totals)

    load_out.wait()
    after = (placed_ref[...] + dot(att_ref[...], wout_ref[...])).astype(BF)
    after_ref[...] = after
    conv_normed = layer_norm(after.astype(F32), cgain_ref[...][None]).astype(BF)

    two_away(0)
    near = dot(conv_normed, wfull_ref[core, :, :channels])
    from_sibling(0)
    far = dot(conv_normed, wfull_ref[1 - core, :, :channels])
    gated = (jnp.where(core == 0, near, far) * jax.nn.sigmoid(jnp.where(core == 0, far, near))).astype(BF)
    gat_ref[...] = gated
    gf_ref[half : half + rows] = gated.astype(F32)

    head_rows = gat_ref.at[0:half]
    tail_rows = gat_ref.at[rows - half : rows]

    @pl.when(ctx > 0)
    def _():
        put(head_rows, hbot_ref, halo_send.at[0], halo_recv.at[0], dp, ctx - 1)

    @pl.when(ctx < 3)
    def _():
        put(tail_rows, htop_ref, halo_send.at[1], halo_recv.at[1], dp, ctx + 1)

    @pl.when(ctx == 0)
    def _():
        htop_ref[...] = jnp.zeros_like(htop_ref)

    @pl.when(ctx == 3)
    def _():
        hbot_ref[...] = jnp.zeros_like(hbot_ref)

    span = 64

    def convolve(r0):
        def body(t, carry):
            lanes = pl.ds(pl.multiple_of(t * tile, tile), tile)
            near = gf_ref[r0 : r0 + span + 2 * half, lanes]
            total = jnp.zeros((span, tile), F32)
            for b in range(8):
                shifted = near if b == 0 else pltpu.roll(near, span + 2 * half - b, 0)
                for a in range(taps // 8):
                    k = 8 * a + b
                    term = shifted[8 * a : 8 * a + span] * mask_ref[k, r0 : r0 + span]
                    total = total + term * wdepth_ref[k : k + 1, lanes]
            moved = total * bns_ref[lanes][None] + bnb_ref[lanes][None]
            act_ref[r0 : r0 + span, lanes] = (moved * jax.nn.sigmoid(moved)).astype(BF)
            return carry

        lax.fori_loop(0, channels // tile, body, 0)

    for r0 in range(span, rows - span, span):
        convolve(r0)

    two_away(1)

    @pl.when(ctx > 0)
    def _():
        settle(htop_ref, halo_recv.at[1])

    @pl.when(ctx < 3)
    def _():
        settle(hbot_ref, halo_recv.at[0])

    gf_ref[0:half] = htop_ref[...].astype(F32)
    gf_ref[half + rows :] = hbot_ref[...].astype(F32)
    convolve(0)
    convolve(rows - span)

    quarter = channels // 2

    def close(c):
        lanes = pl.ds(pl.multiple_of(c * quarter, 128), quarter)
        return dot_nt(act_ref[:, lanes], wfull_ref[c, :, channels:])

    closing = close(core)
    from_sibling(1)
    closing = closing + close(1 - core)
    out_ref[...] = (after_ref[...].astype(F32) + closing).astype(BF)

    settle(send_ref.at[pl.ds(0, n_dp - 1)], a_send)
    settle(meta_ref.at[pl.ds(0, n_dp - 1)], m_send)
    for k in range(1, nz):
        settle(zbuf_ref.at[0], bz_send.at[k])
    for i in range(1, 2 * 4):
        settle(cbuf_ref.at[0, 0], by_send.at[i])
    for part in range(2):
        for i in range(6):
            settle(piece(x, yh, part), bx_send.at[part, i])
        for i in range(NX * NY):
            settle(piece(x, yh, part), sib_send.at[part, i])
    for i in range(4):
        for j in range(3):
            settle(kv_part(ctx, i), kv_send.at[i, j])

    @pl.when(ctx > 0)
    def _():
        settle(head_rows, halo_send.at[0])

    @pl.when(ctx < 3)
    def _():
        settle(tail_rows, halo_send.at[1])


def solution(mesh):
    n_dp = mesh.shape["dp"]
    n_ctx = mesh.shape["ctx"]
    nz = n_dp // (NX * NY)

    def per_device(
        frames,
        destinations,
        segments,
        tile_mask,
        attn_gain,
        w_qkv,
        w_out,
        conv_gain,
        w_pointin,
        w_pointout,
        w_depth,
        bn_scale,
        bn_shift,
    ):
        rows, width = frames.shape[1:]
        seq = segments.shape[1]
        channels = w_depth.shape[1]
        taps = w_depth.shape[0]
        head_cols = w_out.shape[0]
        cap = 2 * rows // n_dp
        shard_rows = w_pointin.shape[0]
        pad_rows = -(-shard_rows // 8) * 8
        half_cols = channels + channels // 2
        pick = np.zeros((nz * n_ctx * shard_rows, n_ctx * nz * pad_rows), np.float32)
        for a in range(nz):
            for b in range(n_ctx):
                for j in range(shard_rows):
                    pick[(a * n_ctx + b) * shard_rows + j, (b * nz + a) * pad_rows + j] = 1.0
        pick = jnp.asarray(pick, BF)
        vmem = pl.BlockSpec(memory_space=pltpu.VMEM)
        hbm = pl.BlockSpec(memory_space=pltpu.HBM)
        operands = (
            destinations,
            frames[0],
            segments,
            tile_mask[0],
            attn_gain,
            w_qkv,
            w_out,
            conv_gain,
            w_pointin,
            w_pointout.T,
            pick,
            w_depth,
            bn_scale,
            bn_shift,
        )
        operands = tuple(pltpu.with_memory_space_constraint(a, pltpu.HBM) for a in operands)
        fetched = [i for i in range(len(operands)) if i not in (5, 6)]

        def body(*refs):
            given, out_ref, rest = list(refs[: len(operands)]), refs[len(operands)], refs[len(operands) + 1 :]
            local, sem, rest = rest[: len(fetched)], rest[len(fetched)], rest[len(fetched) + 1 :]
            fetches = []
            for j, i in enumerate(fetched):
                fetches.append(pltpu.make_async_copy(given[i], local[j], sem.at[j]))
                fetches[j].start()
                given[i] = local[j]
            layer_kernel(n_dp, shard_rows, fetches, *given, out_ref, *rest)

        dma = pltpu.SemaphoreType.DMA
        out = pl.pallas_call(
            body,
            name="conformer_layer",
            out_shape=jax.ShapeDtypeStruct((rows, width), BF),
            in_specs=[hbm] * len(operands),
            out_specs=vmem,
            scratch_shapes=[
                (pltpu.SMEM if i == 3 else pltpu.VMEM)(operands[i].shape, operands[i].dtype) for i in fetched
            ]
            + [
                pltpu.SemaphoreType.DMA((len(fetched),)),
                pltpu.VMEM(w_qkv.shape, BF),
                pltpu.VMEM(w_out.shape, BF),
                pltpu.VMEM((n_dp, cap, width), BF),
                pltpu.VMEM((n_dp, cap, width), BF),
                pltpu.VMEM((n_dp, 1, 128), F32),
                pltpu.VMEM((n_dp, 1, 128), F32),
                pltpu.VMEM((HEADS // 2, rows, seq), BF),
                pltpu.VMEM((nz, pad_rows, 2 * half_cols), BF),
                pltpu.VMEM((NY, n_ctx, nz, pad_rows, half_cols), BF),
                pltpu.VMEM((2, width, half_cols), BF),
                pltpu.VMEM((seq, 2 * head_cols), BF),
                pltpu.VMEM((rows, head_cols), BF),
                pltpu.VMEM((rows, head_cols), BF),
                pltpu.VMEM((rows, width), F32),
                pltpu.VMEM((rows, width), BF),
                pltpu.VMEM((rows, seq), F32),
                pltpu.VMEM((seq + taps, 128), F32),
                pltpu.VMEM((rows + taps, 128), F32),
                pltpu.VMEM((taps, rows, 128), F32),
                pltpu.VMEM((rows, channels), BF),
                pltpu.VMEM((taps // 2, channels), BF),
                pltpu.VMEM((taps // 2, channels), BF),
                pltpu.VMEM((rows + taps, channels), F32),
                pltpu.VMEM((rows, channels), BF),
                dma((2,)),
                dma,
                dma,
                dma,
                dma,
                dma((8,)),
                dma((8,)),
                dma((8,)),
                dma((8,)),
                dma((2, 6)),
                dma((2, 6)),
                dma((2, NX * NY)),
                dma((2, NX * NY)),
                dma((4, 3)),
                dma((4, 3)),
                dma((2,)),
                dma((2,)),
            ],
            compiler_params=pltpu.CompilerParams(
                collective_id=0, has_side_effects=True, vmem_limit_bytes=48 * 2**20
            ),
            cost_estimate=pl.CostEstimate(flops=6 * 10**9, bytes_accessed=20 * 10**6, transcendentals=3 * 10**6),
        )(*operands)

        def hand_on(src_ref, dst_ref, sem):
            copies = []
            for i in range(4):
                part = pl.ds(i * (rows // 4), rows // 4)
                copies.append(pltpu.make_async_copy(src_ref.at[part], dst_ref.at[part], sem.at[i]))
                copies[i].start()
            for copy in copies:
                copy.wait()

        out = pl.pallas_call(
            hand_on,
            name="result",
            out_shape=jax.ShapeDtypeStruct((rows, width), BF),
            in_specs=[pl.BlockSpec(memory_space=pl.ANY)],
            out_specs=pl.BlockSpec(memory_space=pl.ANY),
            scratch_shapes=[dma((4,))],
            compiler_params=pltpu.CompilerParams(vmem_limit_bytes=2**20),
        )(out)
        return out[None]

    return jax.shard_map(
        per_device,
        mesh=mesh,
        in_specs=(
            P("dp", "ctx", None),
            P("dp", "ctx"),
            P("dp", None),
            P("dp", "ctx", None),
            P(),
            P(),
            P(),
            P(),
            P(("dp", "ctx"), None),
            P(None, ("dp", "ctx")),
            P(),
            P(),
            P(),
        ),
        out_specs=P("dp", "ctx", None),
        check_vma=False,
    )
```
